32 devices in a mesh: grp: 4 (over y, x), seq: 8 (over z, core).
Axes of the slice: x: 2, y: 2, z: 4, core: 2. Of those that a mesh axis runs over, the one named last changes fastest.
Arguments:
- hidden: bfloat16 [4, 1024, 2048], P('grp', 'seq'), may hold values from -6 to 6
- modality: int32 [4, 1024], P('grp', 'seq'), may hold values from 0 to 2, as said below
- starts: int32 [4], P('grp'), may hold values from 32 to 992, as said below
- norm_gain: bfloat16 [2048], P(('grp', 'seq')), may hold values from 0.099609375 to 1.8984375
- in_weight: bfloat16 [2048, 3, 8192], P(('grp', 'seq')), may hold values from -0.125 to 0.125
- conv_weight: bfloat16 [4096, 4], P(('grp', 'seq')), may hold values from -3 to 3
- conv_bias: bfloat16 [4096], P(('grp', 'seq')), may hold values from -3 to 3
- xproj_weight: bfloat16 [4096, 3, 160], P(('grp', 'seq')), may hold values from -0.09375 to 0.09375
- dtproj_weight: bfloat16 [128, 3, 4096], P(('grp', 'seq')), may hold values from -0.5 to 0.5
- step_bias: bfloat16 [4096, 3], P(('grp', 'seq')), may hold values from -11 to -2
- decay_log: bfloat16 [4096, 16], P(('grp', 'seq')), may hold values from 0 to 2.765625
- skip_weight: bfloat16 [4096], P(('grp', 'seq')), may hold values from -4 to 4
- out_weight: bfloat16 [4096, 3, 2048], P(('grp', 'seq')), may hold values from -0.1875 to 0.1875
- cotangent: bfloat16 [4, 1024, 2048], P('grp', 'seq'), may hold values from -6 to 6
Outputs:
- output: bfloat16 [4, 1024, 2048], P('grp', 'seq')
- grad_hidden: float32 [4, 1024, 2048], P('grp', 'seq')
- grad_norm_gain: float32 [2048], P(('grp', 'seq'))
- grad_in_weight: float32 [2048, 3, 8192], P(('grp', 'seq'))
- grad_conv_weight: float32 [4096, 4], P(('grp', 'seq'))
- grad_conv_bias: float32 [4096], P(('grp', 'seq'))
- grad_xproj_weight: float32 [4096, 3, 160], P(('grp', 'seq'))
- grad_dtproj_weight: float32 [128, 3, 4096], P(('grp', 'seq'))
- grad_step_bias: float32 [4096, 3], P(('grp', 'seq'))
- grad_decay_log: float32 [4096, 16], P(('grp', 'seq'))
- grad_skip_weight: float32 [4096], P(('grp', 'seq'))
- grad_out_weight: float32 [4096, 3, 2048], P(('grp', 'seq'))
The draws below stay inside these ranges and needn't reach their ends.
Inputs may be any that keep to these rules, and one draw needn't show every extreme that they name: Token modality ids; within a group they change only at multiples of 16 positions; every draw has a group that mixes modalities, and some groups may hold modality 0 only. `starts`: A group's first sequence begins at 0 and its second at this position; one of the two has 32 to 64 tokens.
All inputs are finite; a program needn't handle non-finite values.
Results may differ from the reference program's by a relative error of at most 0.011.
Values may be sent and summed in bfloat16 or wider, within the bound.
No kernel may reach another device: no remote copies, remote signals or barrier semaphores. Data moves between devices by JAX's collectives and lax.ppermute only.
A program may use at most 1.1875 GiB of HBM per device.

```python
import math
import jax
import jax.numpy as jnp
from jax import lax

D = 2048
INNER = 4096
STATE = 16
CONV = 4
RANK = 128
MODES = 3
TOK_DEV = 128
GROUP_TOK = 1024
GROUPS = 4


def draw_modality(key, part):
    key = jax.random.fold_in(key, 11)
    run_key, pure_key, pick_key = jax.random.split(key, 3)
    run_table = jax.random.randint(run_key, (GROUPS, GROUP_TOK), 0, 3)
    where_run = jnp.arange(GROUP_TOK) // 16 * 16
    run_values = run_table[:, where_run]
    pure_flag = jax.random.randint(pure_key, (GROUPS,), 0, 2)
    mixed_group = jax.random.randint(pick_key, (), 0, GROUPS)
    pure_flag = pure_flag * (jnp.arange(GROUPS) != mixed_group).astype(jnp.int32)
    return (run_values * (1 - pure_flag[:, None])).astype(jnp.int32)


def draw_starts(key, part):
    key = jax.random.fold_in(key, 23)
    length_key, side_key = jax.random.split(key)
    short_len = jax.random.randint(length_key, (GROUPS,), TOK_DEV // 4, TOK_DEV // 2 + 1)
    short_last = jax.random.randint(side_key, (GROUPS,), 0, 2)
    return jnp.where(short_last == 1, GROUP_TOK - short_len, short_len).astype(jnp.int32)


def steps_of(stream_key, shape, shards, low, top_value):
    level = 1.0
    for dim, shards_of in shards:
        heights = jax.random.uniform(jax.random.fold_in(jax.random.fold_in(stream_key, 6), dim), (shards_of,), jnp.float32, low / len(shards), top_value / len(shards))
        level = level * jnp.repeat(jnp.exp(heights), shape[dim] // shards_of).reshape((-1,) + (1,) * (len(shape) - 1 - dim))
    return level


def gaussian(rng, shape, deviation, most, cuts=(), kind=jnp.bfloat16):
    values = deviation * jax.random.normal(rng, shape, jnp.float32)
    if cuts:
        values = values * steps_of(rng, shape, cuts, -0.22, 0.18)
    return jnp.clip(values, -most, most).astype(kind)


def setup_inputs(seed: int = 0) -> dict:
    keys = jax.random.split(jax.random.key(seed), 15)
    return {
        "hidden": gaussian(keys[0], (GROUPS, GROUP_TOK, D), 1.0, 6.0, ((0, 4), (1, 8))),
        "modality": draw_modality(jax.random.fold_in(keys[14], 71), 0),
        "starts": draw_starts(jax.random.fold_in(keys[14], 71), 0),
        "norm_gain": jnp.clip(1.0 + 0.18 * jax.random.normal(keys[3], (D,), jnp.float32), 0.099609375, 1.8984375).astype(jnp.bfloat16),
        "in_weight": gaussian(keys[4], (D, MODES, 2 * INNER), D ** -0.5, 0.125, ((0, 32),)),
        "conv_weight": gaussian(keys[5], (INNER, CONV), 0.5, 3.0, ((0, 32),)),
        "conv_bias": gaussian(keys[6], (INNER,), 0.5, 3.0, ((0, 32),)),
        "xproj_weight": gaussian(keys[7], (INNER, MODES, RANK + 2 * STATE), INNER ** -0.5, 0.09375, ((0, 32),)),
        "dtproj_weight": gaussian(keys[8], (RANK, MODES, INNER), RANK ** -0.5, 0.5, ((0, 32),)),
        "step_bias": jnp.clip(-11.0 + 9.0 * jax.random.uniform(keys[9], (INNER, MODES), jnp.float32) ** steps_of(keys[9], (INNER, MODES), ((0, 32),), -0.2, 0.2), -11.0, -2.0).astype(jnp.bfloat16),
        "decay_log": jnp.clip(2.765625 * jax.random.uniform(keys[10], (INNER, STATE), jnp.float32) ** steps_of(keys[10], (INNER, STATE), ((0, 32),), -0.2, 0.2), 0.0, 2.765625).astype(jnp.bfloat16),
        "skip_weight": gaussian(keys[11], (INNER,), 1.0, 4.0, ((0, 32),)),
        "out_weight": gaussian(keys[12], (INNER, MODES, D), (INNER // 4) ** -0.5, 0.1875, ((0, 32),)),
        "cotangent": gaussian(keys[13], (GROUPS, GROUP_TOK, D), 1.0, 6.0, ((0, 4), (1, 8))),
    }


EPS = 1e-05

@jax.custom_vjp
def low(v):
    return lax.optimization_barrier(v.astype(jnp.bfloat16)).astype(jnp.float32)

@jax.custom_vjp
def low_back(v):
    return v

def low_keep(v):
    return (low(v), None)

def low_pass(kept, grad):
    return (grad,)

def back_keep(v):
    return (v, None)

def back_low(kept, grad):
    return (low(grad),)
low.defvjp(low_keep, low_pass)
low_back.defvjp(back_keep, back_low)

def mix_rows(values, weight, mode_masks):
    running = jnp.zeros((values.shape[0], weight.shape[2]), jnp.float32)
    for mode_index in range(weight.shape[1]):
        running = running + mode_masks[:, mode_index:mode_index + 1] * jnp.dot(values, weight[:, mode_index, :], precision=lax.Precision.HIGHEST)
    return running

def run_group(params, tokens, mode_ids, second_start):
    norm_gain, in_weight, conv_weight, conv_bias, xproj_weight, dtproj_weight, step_bias, decay_log, skip_weight, out_weight = params
    group_len = tokens.shape[0]
    inner_width = conv_weight.shape[0]
    rank_width = dtproj_weight.shape[0]
    states = decay_log.shape[1]
    mode_count = in_weight.shape[1]
    block_len = math.gcd(group_len, 512)
    position = jnp.arange(group_len, dtype=jnp.int32)
    seq_begin = jnp.where(position >= second_start, second_start, 0).astype(jnp.int32)
    keep_mask = 1.0 - ((position == 0) | (position == second_start)).astype(jnp.float32)
    mode_masks = (mode_ids[:, None] == jnp.arange(mode_count, dtype=jnp.int32)[None, :]).astype(jnp.float32)
    decay_rate = -jnp.exp(decay_log)

    def one_block(block_carry, block_items):
        left_rim, carry_state = block_carry
        block_tokens, block_masks, block_pos, block_begin, block_keep = block_items
        norm_scale = lax.rsqrt(lax.optimization_barrier(jnp.mean(block_tokens * block_tokens, axis=1, keepdims=True)) + EPS)
        normed = low(block_tokens * norm_scale * norm_gain)
        projected = low_back(mix_rows(normed, in_weight, block_masks))
        conv_in = projected[:, :inner_width]
        gate_in = projected[:, inner_width:]
        extended = jnp.concatenate([left_rim, conv_in], axis=0)
        pre_act = jnp.zeros_like(conv_in) + conv_bias
        for tap_index in range(4):
            tap_valid = (block_pos - 3 + tap_index >= block_begin).astype(jnp.float32)[:, None]
            pre_act = pre_act + conv_weight[:, tap_index] * extended[tap_index:tap_index + block_len] * tap_valid
        activated = jax.nn.silu(pre_act)
        xproj_out = low_back(mix_rows(low(activated), xproj_weight, block_masks))
        rank_part = low(xproj_out[:, :rank_width])
        in_select = xproj_out[:, rank_width:rank_width + states]
        out_select = xproj_out[:, rank_width + states:]
        step_pre = low_back(mix_rows(rank_part, dtproj_weight, block_masks)) + jnp.dot(block_masks, step_bias.T, precision=lax.Precision.HIGHEST)
        step_size = jax.nn.softplus(step_pre)

        def one_token(token_state, token_items):
            step_row, select_row, read_row, act_row, keep_row = token_items
            token_state = keep_row * jnp.exp(step_row[:, None] * decay_rate) * token_state + (step_row * act_row)[:, None] * select_row[None, :]
            return (token_state, lax.optimization_barrier(jnp.sum(token_state * read_row[None, :], axis=1)))
        carry_state, readout_value = lax.scan(one_token, carry_state, (step_size, in_select, out_select, activated, block_keep))
        readout_value = readout_value + skip_weight * activated
        gated_low = low(readout_value * jax.nn.silu(gate_in))
        block_out = block_tokens + low_back(mix_rows(gated_low, out_weight, block_masks))
        return ((extended[-3:], carry_state), block_out)

    def shape_blocks(values):
        return values.reshape((group_len // block_len, block_len) + values.shape[1:])
    initial = (jnp.zeros((3, inner_width), jnp.float32), jnp.zeros((inner_width, states), jnp.float32))
    _, block_outs = lax.scan(jax.checkpoint(one_block), initial, tuple((shape_blocks(values) for values in (tokens, mode_masks, position, seq_begin, keep_mask))))
    return block_outs.reshape(group_len, -1)

def reference(hidden, modality, starts, norm_gain, in_weight, conv_weight, conv_bias, xproj_weight, dtproj_weight, step_bias, decay_log, skip_weight, out_weight, cotangent):
    params = tuple((weight.astype(jnp.float32) for weight in (norm_gain, in_weight, conv_weight, conv_bias, xproj_weight, dtproj_weight, step_bias, decay_log, skip_weight, out_weight)))

    def whole(tokens, weights):

        def per_group(group_items):
            return run_group(weights, group_items[0], group_items[1], group_items[2])
        return lax.map(per_group, (tokens, modality, starts))
    output, pullback = jax.vjp(whole, hidden.astype(jnp.float32), params)
    grad_hidden, grads = pullback(cotangent.astype(jnp.float32))
    return (output.astype(jnp.bfloat16), grad_hidden, grads[0], grads[1], grads[2], grads[3], grads[4], grads[5], grads[6], grads[7], grads[8], grads[9])
```

```python
import functools
import math

import jax
import jax.numpy as jnp
import numpy as np
from jax import lax
from jax.experimental import pallas as pl
from jax.experimental.pallas import tpu as pltpu
from jax.sharding import PartitionSpec as P

EPS = 1e-05
BF = jnp.bfloat16
F32 = jnp.float32
LOG2E = math.log2(math.e)
RESET = 1e4
VMEM = 48 * 1024 * 1024


def dot(a, b, dims=((1,), (0,))):
    return lax.dot_general(a, b, (dims, ((), ())), preferred_element_type=F32)


def silu_slope(v):
    s = jax.nn.sigmoid(v)
    return s * (1.0 + v * (1.0 - s))


def pick(values, masks):
    count = masks.shape[1]
    width = values.shape[1] // count
    return sum(values[:, m * width : (m + 1) * width] * masks[:, m : m + 1] for m in range(count))


def spread(values, masks):
    return jnp.concatenate(
        [values * masks[:, m : m + 1].astype(values.dtype) for m in range(masks.shape[1])], axis=1
    )


def to_time_major(ref, values, row, count):
    ref[pl.ds(row, count, stride=8), :] = values


def scan_kernel(groups, length, starts, step, act, sel, rate, y, prior, end, sf, du, bc, ys, state):
    copies, count = 8 // groups, rate.shape[0] // 8
    i = pl.program_id(0)

    @pl.when(i == 0)
    def _():
        state[...] = jnp.zeros_like(state)

    position = i * length + lax.broadcasted_iota(jnp.int32, (length, 1), 0)
    for g in range(groups):
        begin = (position == 0) | (position == starts[g])
        fade_step = jnp.where(begin, RESET, step[g])
        drive = step[g] * act[g]
        for j in range(copies):
            to_time_major(sf, fade_step, j * groups + g, length)
            to_time_major(du, drive, j * groups + g, length)
            to_time_major(bc, sel[j, g], j * groups + g, length)
    rates = [rate[s * 8 : s * 8 + 8, :] for s in range(count)]

    def one(p, h):
        row = pl.ds(pl.multiple_of(p * 8, 8), 8)
        step_p, drive_p, sel_p = sf[row, :], du[row, :], bc[row, :]
        read = None
        out = []
        for s in range(count):
            prior[pl.ds(pl.multiple_of((p * count + s) * 8, 8), 8), :] = h[s]
            now = jnp.exp2(step_p * rates[s]) * h[s] + drive_p * sel_p[:, s : s + 1]
            term = now * sel_p[:, count + s : count + s + 1]
            read = term if read is None else read + term
            out.append(now)
        ys[row, :] = read
        return tuple(out)

    first = tuple(state[s * 8 : s * 8 + 8, :] for s in range(count))
    last = lax.fori_loop(0, length, one, first, unroll=4)
    for s in range(count):
        state[s * 8 : s * 8 + 8, :] = last[s]
    end[...] = state[...]
    for g in range(groups):
        y[g] = sum(ys[pl.ds(j * groups + g, length, stride=8), :] for j in range(copies))


def back_kernel(
    groups, length, blocks, starts, step, act, sel, rate, read_grad, prior, end, pick_b, pick_c,
    weighted, faded, sel_grad, rate_grad, sf, du, gy, bc, wt, ft, pb, pc, res, carry, held,
):
    copies, count = 8 // groups, rate.shape[0] // 8
    lanes = step.shape[2]
    i = pl.program_id(0)

    @pl.when(i == 0)
    def _():
        carry[...] = jnp.zeros_like(carry)
        held[...] = end[...]
        rate_grad[...] = jnp.zeros_like(rate_grad)

    position = (blocks - 1 - i) * length + lax.broadcasted_iota(jnp.int32, (length, 1), 0)
    for g in range(groups):
        begin = (position == 0) | (position == starts[g])
        fade_step = jnp.where(begin, RESET, step[g])
        drive = step[g] * act[g]
        for j in range(copies):
            to_time_major(sf, fade_step, j * groups + g, length)
            to_time_major(du, drive, j * groups + g, length)
            to_time_major(gy, read_grad[g], j * groups + g, length)
            to_time_major(bc, sel[j, g], j * groups + g, length)
    rates = [rate[s * 8 : s * 8 + 8, :] for s in range(count)]

    def one(k, loop):
        p = length - 1 - k
        row = pl.ds(pl.multiple_of(p * 8, 8), 8)
        step_p, drive_p, grad_p, sel_p = sf[row, :], du[row, :], gy[row, :], bc[row, :]
        carried, state, total = loop
        weight_sum, fade_sum = None, None
        out_c, out_h, out_r = [], [], []
        for s in range(count):
            before = prior[pl.ds(pl.multiple_of((p * count + s) * 8, 8), 8), :]
            e = grad_p * sel_p[:, count + s : count + s + 1] + carried[s]
            cols = slice(s * lanes, (s + 1) * lanes)
            pc[row, cols] = grad_p * state[s]
            pb[row, cols] = e * drive_p
            term = e * sel_p[:, s : s + 1]
            passed = e * jnp.exp2(step_p * rates[s])
            decay = passed * before
            fade_term = decay * rates[s]
            weight_sum = term if weight_sum is None else weight_sum + term
            fade_sum = fade_term if fade_sum is None else fade_sum + fade_term
            out_c.append(passed)
            out_h.append(before)
            out_r.append(total[s] + decay * step_p)
        wt[row, :] = weight_sum
        ft[row, :] = fade_sum
        return tuple(out_c), tuple(out_h), tuple(out_r)

    def parts(ref):
        return tuple(ref[s * 8 : s * 8 + 8, :] for s in range(count))

    c, h, r = lax.fori_loop(
        0, length, one, (parts(carry), parts(held), parts(rate_grad)), unroll=2
    )
    for s in range(count):
        carry[s * 8 : s * 8 + 8, :] = c[s]
        held[s * 8 : s * 8 + 8, :] = h[s]
        rate_grad[s * 8 : s * 8 + 8, :] = r[s]
    res[...] = dot(pb[...].astype(BF), pick_b[...]) + dot(pc[...].astype(BF), pick_c[...])
    for g in range(groups):
        rows = [pl.ds(j * groups + g, length, stride=8) for j in range(copies)]
        weighted[g] = sum(wt[row, :] for row in rows)
        faded[g] = sum(ft[row, :] for row in rows) * (1.0 / LOG2E)
        for j in range(copies):
            sel_grad[j, g] = res[rows[j], :][:, : 2 * count]


def scan_block(length):
    return math.gcd(length, 64)


def scan(starts, step, act, sel, rate):
    groups, total, lanes = step.shape
    length = scan_block(total)
    copies, count = 8 // groups, rate.shape[0] // 8
    whole = pl.BlockSpec((groups, length, lanes), lambda i: (0, i, 0))
    table = pl.BlockSpec((count * 8, lanes), lambda i: (0, 0))
    return pl.pallas_call(
        functools.partial(scan_kernel, groups, length),
        grid=(total // length,),
        in_specs=[
            pl.BlockSpec(memory_space=pltpu.SMEM),
            whole,
            whole,
            pl.BlockSpec((copies, groups, length, 2 * count), lambda i: (0, 0, i, 0)),
            table,
        ],
        out_specs=[whole, pl.BlockSpec((length * count * 8, lanes), lambda i: (i, 0)), table],
        out_shape=[
            jax.ShapeDtypeStruct(step.shape, F32),
            jax.ShapeDtypeStruct((total * count * 8, lanes), F32),
            jax.ShapeDtypeStruct((count * 8, lanes), F32),
        ],
        scratch_shapes=[
            pltpu.VMEM((length * 8, lanes), F32),
            pltpu.VMEM((length * 8, lanes), F32),
            pltpu.VMEM((length * 8, 2 * count), F32),
            pltpu.VMEM((length * 8, lanes), F32),
            pltpu.VMEM((count * 8, lanes), F32),
        ],
        compiler_params=pltpu.CompilerParams(vmem_limit_bytes=VMEM),
        cost_estimate=pl.CostEstimate(
            flops=total * count * 8 * lanes * 8,
            bytes_accessed=total * count * 8 * lanes * 4,
            transcendentals=total * count * 8 * lanes,
        ),
    )(starts, step, act, sel, rate)


def scan_back(starts, step, act, sel, rate, read_grad, prior, end):
    groups, total, lanes = step.shape
    length = scan_block(total)
    blocks = total // length
    copies, count = 8 // groups, rate.shape[0] // 8
    whole = pl.BlockSpec((groups, length, lanes), lambda i: (0, blocks - 1 - i, 0))
    table = pl.BlockSpec((count * 8, lanes), lambda i: (0, 0))
    chosen = pl.BlockSpec((copies, groups, length, 2 * count), lambda i: (0, 0, blocks - 1 - i, 0))
    ones = np.zeros((2, count * lanes, 128), np.float32)
    for s in range(count):
        ones[0, s * lanes : (s + 1) * lanes, s] = 1
        ones[1, s * lanes : (s + 1) * lanes, count + s] = 1
    matrix = pl.BlockSpec((count * lanes, 128), lambda i: (0, 0))
    tall = pltpu.VMEM((length * 8, lanes), F32)
    wide = pltpu.VMEM((length * 8, count * lanes), F32)
    return pl.pallas_call(
        functools.partial(back_kernel, groups, length, blocks),
        grid=(blocks,),
        in_specs=[
            pl.BlockSpec(memory_space=pltpu.SMEM),
            whole,
            whole,
            chosen,
            table,
            whole,
            pl.BlockSpec((length * count * 8, lanes), lambda i: (blocks - 1 - i, 0)),
            table,
            matrix,
            matrix,
        ],
        out_specs=[whole, whole, chosen, table],
        out_shape=[
            jax.ShapeDtypeStruct(step.shape, F32),
            jax.ShapeDtypeStruct(step.shape, F32),
            jax.ShapeDtypeStruct((copies, groups, total, 2 * count), F32),
            jax.ShapeDtypeStruct((count * 8, lanes), F32),
        ],
        scratch_shapes=[
            tall, tall, tall, pltpu.VMEM((length * 8, 2 * count), F32), tall, tall, wide, wide,
            pltpu.VMEM((length * 8, 128), F32),
            pltpu.VMEM((count * 8, lanes), F32),
            pltpu.VMEM((count * 8, lanes), F32),
        ],
        compiler_params=pltpu.CompilerParams(vmem_limit_bytes=VMEM),
        cost_estimate=pl.CostEstimate(
            flops=total * count * 8 * lanes * 16,
            bytes_accessed=total * count * 8 * lanes * 4,
            transcendentals=total * count * 8 * lanes,
        ),
    )(starts, step, act, sel, rate, read_grad, prior, end, jnp.asarray(ones[0], BF), jnp.asarray(ones[1], BF))


def on_device(
    chan, held,
    hidden, modality, starts, norm_gain, in_weight, conv_weight, conv_bias, xproj_weight,
    dtproj_weight, step_bias, decay_log, skip_weight, out_weight, cotangent,
):
    def collect(x):
        return lax.all_gather(x, held, axis=0, tiled=True) if held else x

    def whole(x):
        return lax.all_gather(x, chan, axis=0, tiled=True)

    def scatter(x):
        return lax.psum_scatter(x, chan, scatter_dimension=0, tiled=True)

    def exchange(x):
        return lax.all_to_all(x, chan, 0, 0, tiled=True)

    def settle(x):
        return lax.psum_scatter(x, held, scatter_dimension=0, tiled=True) if held else x

    parts = math.prod(lax.axis_size(a) for a in chan)
    lots = math.prod(lax.axis_size(a) for a in held) if held else 1
    rows, width = hidden.shape[1:]
    own = conv_weight.shape[0]
    lanes = own * lots
    rank = dtproj_weight.shape[0] * parts * lots
    modes = in_weight.shape[1]
    states = decay_log.shape[1]
    mine = hidden[0]
    cot = cotangent[0]

    def shards(w):
        a, k = w.shape[0], w.shape[2] // (lots * parts * own)
        w = w.reshape(a, modes, k, lots, parts, own)
        return jnp.moveaxis(w, 4, 0).reshape(parts, a, modes, k * lots * own)

    def gathered(w):
        moved = exchange(shards(w))
        return collect(moved.reshape(-1, modes, moved.shape[3]))

    def returned(g, out_rows, k):
        g = settle(g)
        g = exchange(g.reshape(parts, out_rows, modes, k, lots, own))
        return jnp.moveaxis(g, 0, 3).reshape(out_rows, modes, k * lots * parts * own)

    gain = lax.all_gather(norm_gain, tuple(held) + tuple(chan), axis=0, tiled=True).astype(F32)
    mode_ids = whole(modality[0])
    begins = lax.all_gather(starts, "grp", axis=0, tiled=True) if "grp" in chan else starts
    groups = begins.shape[0]
    tokens = whole(mine)
    total = tokens.shape[0]
    length = total // groups
    in_cols = gathered(in_weight).reshape(width, modes, 2 * lanes)
    dt_cols = gathered(dtproj_weight).reshape(rank, modes * lanes)
    in_cols = in_cols.reshape(width, modes * 2 * lanes)
    conv_weight, conv_bias, xproj_weight, step_bias, decay_log, skip_weight, out_weight = (
        collect(w)
        for w in (conv_weight, conv_bias, xproj_weight, step_bias, decay_log, skip_weight, out_weight)
    )
    taps = conv_weight.astype(F32)
    conv_base = conv_bias.astype(F32)
    bias = step_bias.astype(F32)
    skip = skip_weight.astype(F32)
    xproj = xproj_weight.reshape(lanes, -1)
    out_rows = jnp.moveaxis(out_weight, 1, 0).reshape(modes * lanes, width)
    masks = (mode_ids[:, None] == jnp.arange(modes, dtype=jnp.int32)[None, :]).astype(F32)
    position = jnp.tile(jnp.arange(length, dtype=jnp.int32), groups)
    second = jnp.repeat(begins, length, total_repeat_length=total)
    begin = jnp.where(position >= second, second, 0)
    copies = 8 // groups
    count = states // copies
    rate = -jnp.exp(decay_log.astype(F32))
    table = jnp.moveaxis(rate.T.reshape(copies, count, lanes), 0, 1)
    table = jnp.repeat(table.reshape(count * copies, 1, lanes), groups, axis=1).reshape(-1, lanes)

    x = tokens.astype(F32)
    normed = (
        x * lax.rsqrt(jnp.mean(x * x, axis=1, keepdims=True) + EPS) * gain
    ).astype(BF)
    proj = pick(dot(normed, in_cols), masks)
    conv_in, gate_in = proj[:, :lanes], proj[:, lanes:]

    def later(v, by):
        v = v.reshape(groups, length, -1)
        return jnp.pad(v, ((0, 0), (by, 0), (0, 0)))[:, :length].reshape(total, -1)

    def earlier(v, by):
        v = v.reshape(groups, length, -1)
        return jnp.pad(v, ((0, 0), (0, by), (0, 0)))[:, by:].reshape(total, -1)

    valid = [(position - 3 + k >= begin).astype(F32)[:, None] for k in range(4)]
    shifted = [later(conv_in, 3 - k) * valid[k] for k in range(4)]
    pre_act = conv_base + sum(taps[:, k] * shifted[k] for k in range(4))
    act = jax.nn.silu(pre_act)
    act_low = act.astype(BF)
    picked = lax.psum(pick(dot(act_low, xproj), masks), chan)
    rank_low = picked[:, :rank].astype(BF)
    sel_in = picked[:, rank : rank + states]
    sel_out = picked[:, rank + states :]
    pre = pick(dot(rank_low, dt_cols), masks) + sum(
        masks[:, m : m + 1] * bias[:, m] for m in range(modes)
    )
    step = jax.nn.softplus(pre)
    sel = jnp.stack(
        [
            jnp.concatenate([v[:, j * count : (j + 1) * count] for v in (sel_in, sel_out)], axis=1)
            for j in range(copies)
        ]
    ).reshape(copies, groups, length, 2 * count)
    grouped = (groups, length, lanes)
    read, prior, end = scan(
        begins, step.reshape(grouped), act.reshape(grouped), sel, table * LOG2E
    )
    read = read.reshape(total, lanes) + skip * act
    gate_act = jax.nn.silu(gate_in)
    gated = spread((read * gate_act).astype(BF), masks)
    branch = scatter(dot(gated, out_rows).astype(BF))
    output = (mine.astype(F32) + branch.astype(F32)).astype(BF)[None]

    cots = whole(cot)
    grad_gated = pick(dot(cots, out_rows, ((1,), (1,))), masks)
    grad_out_weight = jnp.moveaxis(
        dot(gated, cots, ((0,), (0,))).reshape(modes, lanes, width), 0, 1
    )
    read_grad = grad_gated * gate_act
    gate_grad = grad_gated * read * silu_slope(gate_in)
    grad_skip = jnp.sum(read_grad * act, axis=0)
    weighted, faded, sel_grad, rate_grad = scan_back(
        begins, step.reshape(grouped), act.reshape(grouped), sel, table * LOG2E,
        read_grad.reshape(grouped), prior, end,
    )
    weighted = weighted.reshape(total, lanes)
    grad_step = act * weighted + faded.reshape(total, lanes)
    grad_act = skip * read_grad + step * weighted
    rate_grad = rate_grad.reshape(count, copies, groups, lanes).sum(axis=2)
    grad_decay = jnp.moveaxis(rate_grad, 0, 1).reshape(states, lanes).T * rate
    grad_pre = grad_step * jax.nn.sigmoid(pre)
    grad_bias = jnp.stack(
        [jnp.sum(grad_pre * masks[:, m : m + 1], axis=0) for m in range(modes)], axis=1
    )
    pre_low = spread(grad_pre.astype(BF), masks)
    grad_dt = dot(rank_low, pre_low, ((0,), (0,))).reshape(rank, modes, lanes)
    sel_grad = sel_grad.reshape(copies, total, 2, count)
    sel_grad = jnp.moveaxis(sel_grad, 0, 2).reshape(total, 2 * states)
    grad_picked = lax.psum(
        jnp.concatenate([dot(pre_low, dt_cols, ((1,), (1,))), sel_grad], axis=1), chan
    ).astype(BF)
    grad_spread = spread(grad_picked, masks)
    grad_xproj = dot(act_low, grad_spread, ((0,), (0,))).reshape(lanes, modes, -1)
    grad_act = grad_act + dot(grad_spread, xproj, ((1,), (1,)))
    grad_v = grad_act * silu_slope(pre_act)
    grad_conv_bias = jnp.sum(grad_v, axis=0)
    grad_conv = jnp.stack([jnp.sum(grad_v * shifted[k], axis=0) for k in range(4)], axis=1)
    conv_grad = sum(earlier(grad_v * taps[:, k] * valid[k], 3 - k) for k in range(4))
    proj_grad = spread(jnp.concatenate([conv_grad, gate_grad], axis=1).astype(BF), masks)
    grad_in = returned(
        dot(normed, proj_grad, ((0,), (0,))).reshape(width, modes, 2 * lanes).astype(BF),
        in_weight.shape[0], 2,
    ).astype(F32)
    grad_dt = returned(grad_dt, dtproj_weight.shape[0], 1)
    normed_grad = scatter(dot(proj_grad, in_cols, ((1,), (1,))).astype(BF)).astype(F32)
    grad_gain = jnp.sum(grad_in * in_weight.astype(F32), axis=(1, 2)) / norm_gain.astype(F32)
    xm = mine.astype(F32)
    scale = lax.rsqrt(jnp.mean(xm * xm, axis=1, keepdims=True) + EPS)
    unit = xm * scale
    scaled = normed_grad * gain
    grad_hidden = cot.astype(F32) + scale * (
        scaled - unit * jnp.mean(scaled * unit, axis=1, keepdims=True)
    )
    return (
        output,
        grad_hidden[None],
        grad_gain,
        grad_in,
        settle(grad_conv),
        settle(grad_conv_bias),
        settle(grad_xproj),
        grad_dt,
        settle(grad_bias),
        settle(grad_decay),
        settle(grad_skip),
        settle(grad_out_weight),
    )


def solution(mesh):
    both = ("grp", "seq")
    full = mesh.shape["grp"] * mesh.shape["seq"] <= 32
    chan, held = (both, ()) if full else (("seq",), ("grp",))
    row = P(both)
    return jax.shard_map(
        functools.partial(on_device, chan, held),
        mesh=mesh,
        in_specs=(
            P("grp", "seq", None), P("grp", "seq"), P("grp"),
            row, row, row, row, row, row, row, row, row, row,
            P("grp", "seq", None),
        ),
        out_specs=(P("grp", "seq", None), P("grp", "seq", None)) + (row,) * 10,
        check_vma=False,
    )
```

```python
import functools
import math

import jax
import jax.numpy as jnp
import numpy as np
from jax import lax
from jax.experimental import pallas as pl
from jax.experimental.pallas import tpu as pltpu
from jax.sharding import PartitionSpec as P

EPS = 1e-05
BF = jnp.bfloat16
F32 = jnp.float32
LOG2E = math.log2(math.e)
RESET = 1e4
VMEM = 48 * 1024 * 1024


def dot(a, b, dims=((1,), (0,))):
    return lax.dot_general(a, b, (dims, ((), ())), preferred_element_type=F32)


def silu_slope(v):
    s = jax.nn.sigmoid(v)
    return s * (1.0 + v * (1.0 - s))


def after(x, other):
    return x + (other[(0,) * other.ndim] * 0).astype(x.dtype)


def pick(values, masks):
    count = masks.shape[1]
    width = values.shape[1] // count
    return sum(values[:, m * width : (m + 1) * width] * masks[:, m : m + 1] for m in range(count))


def spread(values, masks):
    return jnp.concatenate(
        [values * masks[:, m : m + 1].astype(values.dtype) for m in range(masks.shape[1])], axis=1
    )


def spread_lanes(source, widen, target):

    @pl.loop(0, source.shape[0] // 128)
    def _(n):
        row = pl.ds(pl.multiple_of(n * 128, 128), 128)
        target[row, :] = dot(source[row, :].astype(BF), widen[...])


def widening(columns, lanes):
    ones = np.zeros((2 * columns, columns * lanes), np.float32)
    for s in range(columns):
        ones[s, s * lanes : (s + 1) * lanes] = 1
        ones[columns + s, s * lanes : (s + 1) * lanes] = 1
    return jnp.asarray(ones, BF)


def dot_t(a, b):
    return dot(a, b, ((1,), (1,)))


def t_dot(a, b):
    return dot(a, b, ((0,), (0,)))


def softplus(x):
    return jnp.maximum(x, 0.0) + jnp.log1p(jnp.exp(-jnp.abs(x)))


def packed(values, width):
    count = 128 // width
    span = values.shape[0] // count
    return jnp.concatenate([values[q * span : (q + 1) * span, :] for q in range(count)], axis=1)


def unpacked(values, width):
    values = values.astype(F32)
    return jnp.concatenate(
        [values[:, q * width : (q + 1) * width] for q in range(128 // width)], axis=0
    )


def to_time_major(ref, values, row, count):
    ref[pl.ds(row, count, stride=8), :] = values


def lay_out(groups, length, states, first, starts, step, act, picked, extra, sf, du, bc, also):
    copies = 8 // groups
    position = first + lax.broadcasted_iota(jnp.int32, (length, 1), 0)
    lane = lax.broadcasted_iota(jnp.int32, (1, 4 * states), 1)
    owner = lane % states // (states // copies)
    for g in range(groups):
        begin = (position == 0) | (position == starts[g])
        fade_step = jnp.where(begin, RESET, step[g])
        drive = step[g] * act[g, 0]
        span = length * 2 * states // 128
        chosen = jnp.concatenate(
            [
                unpacked(picked[g, 0, length + n * span : length + (n + 1) * span, :], 2 * states)
                for n in range(2)
            ],
            axis=1,
        )
        for j in range(copies):
            to_time_major(sf, fade_step, j * groups + g, length)
            to_time_major(du, drive, j * groups + g, length)
            to_time_major(bc, jnp.where(owner == j, chosen, 0.0), j * groups + g, length)
            if also is not None:
                to_time_major(also, extra[g, 0], j * groups + g, length)


def pre_step(picked, mask, dt, bias):
    modes, lanes = bias.shape
    product = dot(picked[: mask.shape[0], :], dt[...])
    return sum(
        (product[:, m * lanes : (m + 1) * lanes] + bias[m : m + 1, :]) * mask[:, m : m + 1]
        for m in range(modes)
    )


def scan_kernel(
    groups, length, states, table, starts, places, act, picked, mask, gate, rate, widen, dt, bias, skip,
    y, gated, spread_gated, pre, prior, end, sf, du, bc, ys, state, ex,
):
    copies, count, lanes = 8 // groups, rate.shape[0] // 8, rate.shape[1]
    i = pl.program_id(0)

    @pl.when(i == 0)
    def _():
        state[...] = jnp.zeros_like(state)

    steps = []
    for g in range(groups):
        raw = pre_step(picked[g, 0], mask[g, 0], dt, bias)
        pre[g, 0] = raw
        steps.append(softplus(raw))
    lay_out(groups, length, states, i * length, starts, steps, act, picked, None, sf, du, bc, None)
    spread_lanes(bc, widen, ex)
    rates = [rate[s * 8 : s * 8 + 8, :] for s in range(count)]

    def one(p, h):
        row = pl.ds(pl.multiple_of(p * 8, 8), 8)
        step_p, drive_p = sf[row, :], du[row, :]
        read = None
        out = []
        for s in range(count):
            prior[pl.ds(pl.multiple_of((p * count + s) * 8, 8), 8), :] = h[s]
            now = jnp.exp2(step_p * rates[s]) * h[s] + drive_p * ex[row, s * lanes : (s + 1) * lanes]
            term = now * ex[row, (count + s) * lanes : (count + s + 1) * lanes]
            read = term if read is None else read + term
            out.append(now)
        ys[row, :] = read
        return tuple(out)

    first = tuple(state[s * 8 : s * 8 + 8, :] for s in range(count))
    last = lax.fori_loop(0, length, one, first, unroll=4)
    for s in range(count):
        state[s * 8 : s * 8 + 8, :] = last[s]
    end[...] = state[...]
    for g in range(groups):
        total = sum(ys[pl.ds(j * groups + g, length, stride=8), :] for j in range(copies))
        total = total + skip[...] * act[g, 0]
        y[g, 0] = total
        opened = gate[g, 0]
        low = (total * (opened * jax.nn.sigmoid(opened))).astype(BF)
        gated[g, 0] = low
        for m in range(bias.shape[0]):
            cols = slice(m * lanes, (m + 1) * lanes)
            spread_gated[places[g], 0, :, cols] = low * mask[g, 0, :, m : m + 1].astype(BF)


def back_kernel(
    groups, length, states, top, blocks, table, starts, act, picked, mask, pre, read_grad, prior,
    begun, rate, widen, dt, bias, skip, pick_b, pick_c, *refs,
):
    act_grad, picked_grad, left, rate_grad, dt_grad, bias_grad, skip_grad = refs[-20:-13]
    sf, du, gy, bc, wt, ft, pb, pc, res, carry, held, ex, step = refs[-13:]
    copies, count = 8 // groups, rate.shape[0] // 8
    lanes = rate.shape[1]
    modes = bias.shape[0]
    rank = dt.shape[0]
    i = pl.program_id(0)

    @pl.when(i == 0)
    def _():
        carry[...] = begun[0 : count * 8, :]
        held[...] = begun[count * 8 :, :]
        rate_grad[...] = jnp.zeros_like(rate_grad)
        dt_grad[...] = jnp.zeros_like(dt_grad)
        bias_grad[...] = jnp.zeros_like(bias_grad)
        skip_grad[...] = jnp.zeros_like(skip_grad)

    for g in range(groups):
        step[g] = softplus(pre[g, 0])
    lay_out(
        groups, length, states, (top - i) * length, starts, step, act, picked, read_grad, sf, du, bc, gy
    )
    spread_lanes(bc, widen, ex)
    rates = [rate[s * 8 : s * 8 + 8, :] for s in range(count)]

    def one(k, loop):
        p = length - 1 - k
        row = pl.ds(pl.multiple_of(p * 8, 8), 8)
        step_p, drive_p, grad_p = sf[row, :], du[row, :], gy[row, :]
        carried, state, total = loop
        weight_sum, fade_sum = None, None
        out_c, out_h, out_r = [], [], []
        for s in range(count):
            before = prior[pl.ds(pl.multiple_of((p * count + s) * 8, 8), 8), :]
            cols = slice(s * lanes, (s + 1) * lanes)
            e = grad_p * ex[row, (count + s) * lanes : (count + s + 1) * lanes] + carried[s]
            pc[row, cols] = grad_p * state[s]
            pb[row, cols] = e * drive_p
            term = e * ex[row, cols]
            passed = e * jnp.exp2(step_p * rates[s])
            decay = passed * before
            fade_term = decay * rates[s]
            weight_sum = term if weight_sum is None else weight_sum + term
            fade_sum = fade_term if fade_sum is None else fade_sum + fade_term
            out_c.append(passed)
            out_h.append(before)
            out_r.append(total[s] + decay * step_p)
        wt[row, :] = weight_sum
        ft[row, :] = fade_sum
        return tuple(out_c), tuple(out_h), tuple(out_r)

    def parts(ref):
        return tuple(ref[s * 8 : s * 8 + 8, :] for s in range(count))

    c, h, r = lax.fori_loop(
        0, length, one, (parts(carry), parts(held), parts(rate_grad)), unroll=2
    )
    for s in range(count):
        carry[s * 8 : s * 8 + 8, :] = c[s]
        held[s * 8 : s * 8 + 8, :] = h[s]
        rate_grad[s * 8 : s * 8 + 8, :] = r[s]
    left[0 : count * 8, :] = carry[...]
    left[count * 8 :, :] = held[...]

    @pl.loop(0, res.shape[0] // 128)
    def _(n):
        row = pl.ds(pl.multiple_of(n * 128, 128), 128)
        res[row, :] = dot(pb[row, :].astype(BF), pick_b[...]) + dot(
            pc[row, :].astype(BF), pick_c[...]
        )

    lane = lax.broadcasted_iota(jnp.int32, (1, 128), 1)
    owner = lane % states // count
    for g in range(groups):
        rows = [pl.ds(j * groups + g, length, stride=8) for j in range(copies)]
        weighted = sum(wt[row, :] for row in rows)
        faded = sum(ft[row, :] for row in rows) * (1.0 / LOG2E)
        chosen = sum(jnp.where(owner == j, res[rows[j], :], 0.0) for j in range(copies))
        grad_y, u = read_grad[g, 0], act[g, 0]
        act_grad[g, 0] = skip[...] * grad_y + step[g] * weighted
        pre_grad = (u * weighted + faded) * jax.nn.sigmoid(pre[g, 0])
        skip_grad[...] += jnp.sum(grad_y * u, axis=0, keepdims=True)
        rank_grad = None
        for m in range(modes):
            own = pre_grad * mask[g, 0, :, m : m + 1]
            bias_grad[m : m + 1, :] += jnp.sum(own, axis=0, keepdims=True)
            own = own.astype(BF)
            cols = slice(m * lanes, (m + 1) * lanes)
            term = dot_t(own, dt[:, cols])
            rank_grad = term if rank_grad is None else rank_grad + term
            dt_grad[:, cols] += t_dot(picked[g, 0, 0:length, :], own)
        picked_grad[g, 0, 0:length, :] = rank_grad
        picked_grad[g, 0, length:, :] = packed(chosen[:, 0 : 2 * states], 2 * states)


def spread_lanes(source, widen, target):

    @pl.loop(0, source.shape[0] // 128)
    def _(n):
        row = pl.ds(pl.multiple_of(n * 128, 128), 128)
        target[row, :] = dot(source[row, :].astype(BF), widen[...])


def widening(states, count, lanes):
    ones = np.zeros((2, 2, states, 2 * count * lanes), np.float32)
    for kind in range(2):
        for s in range(states):
            block = kind * count + s % count
            ones[:, kind, s, block * lanes : (block + 1) * lanes] = 1
    return jnp.asarray(ones.reshape(4 * states, -1), BF)


def picking(states, count, lanes):
    ones = np.zeros((2, count * lanes, 128), np.float32)
    for kind in range(2):
        for s in range(states):
            at = s % count
            ones[kind, at * lanes : (at + 1) * lanes, kind * states + s] = 1
    return jnp.asarray(ones[0], BF), jnp.asarray(ones[1], BF)


def conv_kernel(groups, length, table, starts, x, mask, taps, base, xproj, v, act, part, tail, ext):
    i = pl.program_id(0)

    @pl.when(i == 0)
    def _():
        tail[...] = jnp.zeros_like(tail)

    modes = mask.shape[3]
    width = xproj.shape[1] // modes
    position = i * length + lax.broadcasted_iota(jnp.int32, (length, 1), 0)
    for g in range(groups):
        begin = jnp.where(position >= starts[g], starts[g], 0)
        ext[0:8, :] = tail[g]
        ext[8 : 8 + length, :] = x[g, 0]
        tail[g] = x[g, 0, length - 8 : length, :]
        total = base[...]
        for k in range(4):
            valid = (position - 3 + k >= begin).astype(F32)
            total = total + taps[k : k + 1, :] * ext[5 + k : 5 + k + length, :] * valid
        v[g, 0] = total
        active = total * jax.nn.sigmoid(total)
        act[g, 0] = active
        product = dot(active.astype(BF), xproj[...])
        chosen = sum(
            product[:, m * width : (m + 1) * width] * mask[g, 0, :, m : m + 1] for m in range(modes)
        )
        part[g, 0, 0:length, :] = chosen[:, 0:128]
        part[g, 0, length:, :] = packed(chosen[:, 128:], width - 128)


def conv_back_kernel(
    groups, length, blocks, table, starts, grad, sel_grad, v, act, x, mask, taps, xproj, *refs,
):
    x_grad, tap_grad, base_grad, weight_grad, head, ext = refs[-6:]
    i = pl.program_id(0)

    @pl.when(i == 0)
    def _():
        head[...] = jnp.zeros_like(head)
        weight_grad[...] = jnp.zeros_like(weight_grad)
        tap_grad[...] = jnp.zeros_like(tap_grad)
        base_grad[...] = jnp.zeros_like(base_grad)

    modes = mask.shape[3]
    width = xproj.shape[1] // modes
    position = (blocks - 1 - i) * length + lax.broadcasted_iota(jnp.int32, (length, 1), 0)
    for g in range(groups):
        chosen = jnp.concatenate(
            [
                sel_grad[g, 0, 0:length, :].astype(F32),
                unpacked(sel_grad[g, 0, length:, :], width - 128),
            ],
            axis=1,
        ).astype(BF)
        masked = [chosen * mask[g, 0, :, m : m + 1].astype(BF) for m in range(modes)]
        act_grad = grad[g, 0]
        low = act[g, 0].astype(BF)
        for m in range(modes):
            cols = slice(m * width, (m + 1) * width)
            act_grad = act_grad + dot_t(masked[m], xproj[:, cols])
            weight_grad[:, cols] += t_dot(low, masked[m])
        v_grad = act_grad * silu_slope(v[g, 0])
        ext[0:length, :] = v_grad
        ext[length : length + 8, :] = head[g]
        head[g] = v_grad[0:8, :]
        base_grad[...] += jnp.sum(v_grad, axis=0, keepdims=True)
        total = None
        for k in range(4):
            crosses = (position < starts[g]) & (position + 3 - k >= starts[g])
            shifted = jnp.where(crosses, 0.0, ext[3 - k : 3 - k + length, :])
            term = taps[k : k + 1, :] * shifted
            total = term if total is None else total + term
            tap_grad[k : k + 1, :] += jnp.sum(x[g, 0] * shifted, axis=0, keepdims=True)
        total = total.astype(BF)
        lanes = total.shape[1]
        for m in range(modes):
            x_grad[g, 0, :, m * lanes : (m + 1) * lanes] = total * mask[g, 0, :, m : m + 1].astype(BF)


def inproj_kernel(count, *refs):
    pieces, (gain, weight, mask), (normed, proj) = refs[:count], refs[count : count + 3], refs[-2:]
    rows = mask.shape[1] // count
    for n in range(count):
        x = pieces[n][0:rows, :].astype(F32)
        scale = lax.rsqrt(jnp.mean(x * x, axis=1, keepdims=True) + EPS)
        normed[0, n * rows : (n + 1) * rows, :] = (x * scale * gain[...]).astype(BF)
    product = dot(normed[0], weight[...])
    modes = mask.shape[2]
    width = weight.shape[1] // modes
    proj[0] = sum(
        product[:, m * width : (m + 1) * width] * mask[0, :, m : m + 1] for m in range(modes)
    )


def inproj(at, lots, pieces, gain, weight, mask, so_far):
    tall, width = pieces[0].shape
    count = len(pieces)
    rows = mask.shape[1] // count
    modes = mask.shape[2]
    columns = weight.shape[1] // modes
    here = lambda i: (at, 0, 0)
    size = count * rows
    full = lambda shape: pl.BlockSpec(shape, lambda i: (0,) * len(shape))
    aliases = {} if so_far is None else {count + 3: 0, count + 4: 1}
    return pl.pallas_call(
        functools.partial(inproj_kernel, count),
        grid=(1,),
        in_specs=[full((tall, width))] * count
        + [full((1, width)), full(weight.shape), pl.BlockSpec((1, size, modes), here)]
        + [pl.BlockSpec(memory_space=pl.ANY)] * len(aliases),
        out_specs=[pl.BlockSpec((1, size, width), here), pl.BlockSpec((1, size, columns), here)],
        out_shape=[
            jax.ShapeDtypeStruct((lots, size, width), BF),
            jax.ShapeDtypeStruct((lots, size, columns), F32),
        ],
        input_output_aliases=aliases,
        compiler_params=pltpu.CompilerParams(vmem_limit_bytes=VMEM),
        cost_estimate=pl.CostEstimate(
            flops=2 * size * width * weight.shape[1],
            bytes_accessed=4 * size * width,
            transcendentals=0,
        ),
    )(*pieces, gain, weight, mask, *(so_far or ()))


def conv(table, starts, x, mask, taps, base, xproj):
    groups, blocks, length, lanes = x.shape
    modes = mask.shape[3]
    width = xproj.shape[1] // modes
    at = lambda i, t, b: (0, t[i], 0, 0)
    flat = lambda i, t, b: (0, 0)
    block = pl.BlockSpec((groups, 1, length, lanes), at)
    return pl.pallas_call(
        functools.partial(conv_kernel, groups, length),
        grid_spec=pltpu.PrefetchScalarGridSpec(
            num_scalar_prefetch=2,
            grid=(blocks,),
            in_specs=[
                block,
                pl.BlockSpec((groups, 1, length, modes), at),
                pl.BlockSpec(taps.shape, flat),
                pl.BlockSpec(base.shape, flat),
                pl.BlockSpec(xproj.shape, flat),
            ],
            out_specs=[block, block, pl.BlockSpec((groups, 1, length * width // 128, 128), at)],
            scratch_shapes=[
                pltpu.VMEM((groups, 8, lanes), F32),
                pltpu.VMEM((length + 8, lanes), F32),
            ],
        ),
        out_shape=[
            jax.ShapeDtypeStruct(x.shape, F32),
            jax.ShapeDtypeStruct(x.shape, F32),
            jax.ShapeDtypeStruct((groups, blocks, length * width // 128, 128), F32),
        ],
        compiler_params=pltpu.CompilerParams(vmem_limit_bytes=VMEM),
    )(table, starts, x, mask, taps, base, xproj)


def conv_back(table, starts, grad, sel_grad, v, act, x, mask, taps, xproj, before):
    groups, blocks, length, lanes = x.shape
    modes = mask.shape[3]
    width = xproj.shape[1] // modes
    at = lambda i, t, b: (0, t[blocks - 1 - i], 0, 0)
    flat = lambda i, t, b: (0, 0)
    block = pl.BlockSpec((groups, 1, length, lanes), at)
    return pl.pallas_call(
        functools.partial(conv_back_kernel, groups, length, blocks),
        grid_spec=pltpu.PrefetchScalarGridSpec(
            num_scalar_prefetch=2,
            grid=(blocks,),
            in_specs=[
                block,
                pl.BlockSpec((groups, 1, length * width // 128, 128), at),
                block,
                block,
                block,
                pl.BlockSpec((groups, 1, length, modes), at),
                pl.BlockSpec(taps.shape, flat),
                pl.BlockSpec(xproj.shape, flat),
            ]
            + [pl.BlockSpec(memory_space=pl.ANY)] * len(before),
            out_specs=[
                pl.BlockSpec((groups, 1, length, modes * lanes), at),
                pl.BlockSpec((8, lanes), flat),
                pl.BlockSpec((1, lanes), flat),
                pl.BlockSpec(xproj.shape, flat),
            ],
            scratch_shapes=[
                pltpu.VMEM((groups, 8, lanes), F32),
                pltpu.VMEM((length + 8, lanes), F32),
            ],
        ),
        out_shape=[
            jax.ShapeDtypeStruct((groups, blocks, length, modes * lanes), BF),
            jax.ShapeDtypeStruct((8, lanes), F32),
            jax.ShapeDtypeStruct((1, lanes), F32),
            jax.ShapeDtypeStruct(xproj.shape, F32),
        ],
        compiler_params=pltpu.CompilerParams(vmem_limit_bytes=VMEM),
    )(table, starts, grad, sel_grad, v, act, x, mask, taps, xproj, *before)


def flat(array):
    return pl.BlockSpec(array.shape, lambda i, *_: (0,) * array.ndim)


def scan(table, starts, places, act, picked, mask, gate, rate, dt, bias, skip, states):
    groups, blocks, length, lanes = act.shape
    total = blocks * length
    count = rate.shape[0] // 8
    at = lambda i, t, b, p: (0, t[i], 0, 0)
    modes = bias.shape[0]
    block = lambda a: pl.BlockSpec((groups, 1) + a.shape[2:], at)
    widen = widening(states, count, lanes)
    tall = pltpu.VMEM((length * 8, lanes), F32)
    like = jax.ShapeDtypeStruct(act.shape, F32)
    return pl.pallas_call(
        functools.partial(scan_kernel, groups, length, states),
        grid_spec=pltpu.PrefetchScalarGridSpec(
            num_scalar_prefetch=3,
            grid=(blocks,),
            in_specs=[block(a) for a in (act, picked, mask, gate)]
            + [flat(a) for a in (rate, widen, dt, bias, skip)],
            out_specs=[
                block(act),
                block(act),
                pl.BlockSpec((groups, 1, length, modes * lanes), lambda i, t, b, p: (0, i, 0, 0)),
                block(act),
                pl.BlockSpec((length * count * 8, lanes), lambda i, t, b, p: (i, 0)),
                flat(rate),
            ],
            scratch_shapes=[
                tall,
                tall,
                pltpu.VMEM((length * 8, 4 * states), F32),
                tall,
                pltpu.VMEM((count * 8, lanes), F32),
                pltpu.VMEM((length * 8, 2 * count * lanes), F32),
            ],
        ),
        out_shape=[
            like,
            jax.ShapeDtypeStruct(act.shape, BF),
            jax.ShapeDtypeStruct((groups, blocks, length, modes * lanes), BF),
            like,
            jax.ShapeDtypeStruct((total * count * 8, lanes), F32),
            jax.ShapeDtypeStruct((count * 8, lanes), F32),
        ],
        compiler_params=pltpu.CompilerParams(vmem_limit_bytes=VMEM),
        cost_estimate=pl.CostEstimate(flops=10**10, bytes_accessed=10**8, transcendentals=0),
    )(table, starts, places, act, picked, mask, gate, rate, widen, dt, bias, skip)


def scan_back(
    first, last, table, starts, act, picked, mask, pre, read_grad, prior, begun, rate, dt, bias,
    skip, states, so_far, before,
):
    groups, blocks, length, lanes = act.shape
    count = rate.shape[0] // 8
    rank = dt.shape[0]
    modes = bias.shape[0]
    at = lambda i, t, b: (0, t[last - 1 - i], 0, 0)
    block = lambda a: pl.BlockSpec((groups, 1) + a.shape[2:], at)
    widen = widening(states, count, lanes)
    pick_b, pick_c = picking(states, count, lanes)
    tall = pltpu.VMEM((length * 8, lanes), F32)
    wide = pltpu.VMEM((length * 8, count * lanes), F32)
    tables = pltpu.VMEM((count * 8, lanes), F32)
    shapes = [
        jax.ShapeDtypeStruct(act.shape, F32),
        jax.ShapeDtypeStruct((groups, blocks, length + length * 2 * states // 128, 128), F32),
        jax.ShapeDtypeStruct((2 * count * 8, lanes), F32),
        jax.ShapeDtypeStruct((count * 8, lanes), F32),
        jax.ShapeDtypeStruct((rank, modes * lanes), F32),
        jax.ShapeDtypeStruct((8, lanes), F32),
        jax.ShapeDtypeStruct((1, lanes), F32),
    ]
    loaded = (begun, rate, widen, dt, bias, skip, pick_b, pick_c)
    extra = tuple(so_far or ()) + tuple(before)
    at_input = 2 + 6 + len(loaded)
    return pl.pallas_call(
        functools.partial(back_kernel, groups, length, states, last - 1, blocks),
        grid_spec=pltpu.PrefetchScalarGridSpec(
            num_scalar_prefetch=2,
            grid=(last - first,),
            in_specs=[block(a) for a in (act, picked, mask, pre, read_grad)]
            + [pl.BlockSpec((length * count * 8, lanes), lambda i, t, b: (last - 1 - i, 0))]
            + [flat(a) for a in loaded]
            + [pl.BlockSpec(memory_space=pl.ANY)] * len(extra),
            out_specs=[block(shapes[0]), block(shapes[1])] + [flat(a) for a in shapes[2:]],
            scratch_shapes=[
                tall, tall, tall, pltpu.VMEM((length * 8, 4 * states), F32), tall, tall, wide, wide,
                pltpu.VMEM((length * 8, 128), F32),
                tables,
                tables,
                pltpu.VMEM((length * 8, 2 * count * lanes), F32),
                pltpu.VMEM((groups, length, lanes), F32),
            ],
        ),
        out_shape=shapes,
        input_output_aliases={at_input: 0, at_input + 1: 1} if so_far else {},
        compiler_params=pltpu.CompilerParams(vmem_limit_bytes=VMEM),
        cost_estimate=pl.CostEstimate(
            flops=10**10, bytes_accessed=25 * 10**6 * (last - first), transcendentals=0
        ),
    )(table, starts, act, picked, mask, pre, read_grad, prior, *loaded, *extra)


def cot_kernel(
    lots_at, spans_at, cots, out_rows, mask, gated, read, gate, read_grad, gate_grad, weight_grad, whole
):
    count = spans_at.shape[0]
    rows = whole.shape[0] // count

    @pl.when(pl.program_id(0) == 0)
    def _():
        weight_grad[...] = jnp.zeros_like(weight_grad)

    for n in range(count):
        whole[n * rows : (n + 1) * rows, :] = cots[
            0, pl.ds(pl.multiple_of(spans_at[n] * rows, rows), rows), :
        ]
    product = dot_t(whole[...], out_rows[...])
    modes = mask.shape[2]
    lanes = gated.shape[2]
    masks = [mask[0, :, m : m + 1] for m in range(modes)]
    grad = sum(product[:, m * lanes : (m + 1) * lanes] * masks[m] for m in range(modes))
    opened = gate[0]
    read_grad[0] = grad * (opened * jax.nn.sigmoid(opened))
    gate_low = (grad * read[0] * silu_slope(opened)).astype(BF)
    for m in range(modes):
        own = masks[m].astype(BF)
        cols = slice(m * lanes, (m + 1) * lanes)
        gate_grad[0, :, cols] = gate_low * own
        weight_grad[cols, :] += t_dot(gated[0] * own, whole[...])


def cot_part(lots_at, spans_at, cots, out_rows, mask, gated, read, gate):
    lots, size, width = cots.shape
    lanes = gated.shape[2]
    wide = out_rows.shape[0]
    block = lambda w: pl.BlockSpec((1, size, w), lambda i, a, b: (i, 0, 0))
    return pl.pallas_call(
        cot_kernel,
        grid_spec=pltpu.PrefetchScalarGridSpec(
            num_scalar_prefetch=2,
            grid=(lots,),
            in_specs=[pl.BlockSpec((1, size, width), lambda i, a, b: (a[i], 0, 0)), flat(out_rows)]
            + [block(a.shape[2]) for a in (mask, gated, read, gate)],
            out_specs=[block(lanes), block(wide), flat(out_rows)],
            scratch_shapes=[pltpu.VMEM((size, width), BF)],
        ),
        out_shape=[
            jax.ShapeDtypeStruct((lots, size, lanes), F32),
            jax.ShapeDtypeStruct((lots, size, wide), BF),
            jax.ShapeDtypeStruct(out_rows.shape, F32),
        ],
        compiler_params=pltpu.CompilerParams(vmem_limit_bytes=VMEM),
        cost_estimate=pl.CostEstimate(
            flops=4 * lots * size * width * wide, bytes_accessed=3 * lots * size * width, transcendentals=0
        ),
    )(lots_at, spans_at, cots, out_rows, mask, gated, read, gate)


class Dim:

    def __init__(self, axis, stride, size, length):
        self.axis, self.stride, self.size, self.length = axis, stride, size, length

    def here(self):
        return lax.axis_index(self.axis) // self.stride % self.size

    def fetch(self, x, by):
        pairs = []
        for i in range(self.length):
            c = i // self.stride % self.size
            pairs.append((i + ((c + by) % self.size - c) * self.stride, i))
        return lax.ppermute(x, self.axis, pairs)


def dims_of(chan):
    dims = []
    for axis in chan:
        length = lax.axis_size(axis)
        sizes = []
        rest = length
        if axis == "seq":
            rest //= 2
        radix = 4 if axis == "seq" else 2
        while rest > 1:
            sizes.insert(0, min(radix, rest))
            rest //= sizes[0]
        if axis == "seq":
            sizes.append(2)
        stride = length
        for size in sizes:
            stride //= size
            dims.append(Dim(axis, stride, size, length))
    return dims


def gather_pieces(dims, x):
    others, ring, core = dims[:-2], dims[-2], dims[-1]
    got = {}
    first = x
    for k in range(ring.size):
        if k:
            first = ring.fetch(first, 1)
        order = list(range(len(others)))
        if k % 2:
            order.reverse()
        held = {(0,) * len(others): first}
        for d in order:
            for at, block in list(held.items()):
                for r in range(1, others[d].size):
                    block = others[d].fetch(block, 1)
                    held[at[:d] + (r,) + at[d + 1 :]] = block
        for at, block in held.items():
            got[at + (k, 0)] = block
            got[at + (k, 1)] = core.fetch(block, 1)
    return [got[at] for at in sorted(got)]


def pairs_of(dims):
    return [d.size for d in dims[:-2]] == [2, 2]


def gather_stage(dims, x, d):
    got = [x] + [dims[d].fetch(x, r) for r in range(1, dims[d].size)]
    return jnp.concatenate(got, axis=d)


def gather_small(dims, x):
    x = x.reshape((1,) * len(dims) + x.shape)
    x = gather_stage(dims, x, len(dims) - 2)
    if pairs_of(dims):
        halves = jnp.split(x, 2, axis=len(dims))
        halves = [gather_stage(dims, h, n) for n, h in enumerate(halves)]
        halves = [gather_stage(dims, h, 1 - n) for n, h in enumerate(halves)]
        x = jnp.concatenate(halves, axis=len(dims))
    else:
        for d in range(len(dims) - 2):
            x = gather_stage(dims, x, d)
    return gather_stage(dims, x, len(dims) - 1)


def reduce_stage(dims, x, d, kind):
    block = [lax.slice_in_dim(x, r, r + 1, axis=d) for r in range(dims[d].size)]
    return add_up(
        [block[0]] + [dims[d].fetch(block[r].astype(kind), -r) for r in range(1, len(block))]
    )


def reduce_small(dims, x):
    x = reduce_stage(dims, x, len(dims) - 1, F32)
    if pairs_of(dims):
        halves = jnp.split(x, 2, axis=len(dims))
        halves = [reduce_stage(dims, h, n, BF) for n, h in enumerate(halves)]
        halves = [reduce_stage(dims, h, 1 - n, F32) for n, h in enumerate(halves)]
        x = jnp.concatenate(halves, axis=len(dims))
    else:
        for d in range(len(dims) - 2):
            x = reduce_stage(dims, x, d, F32 if d else BF)
    x = reduce_stage(dims, x, len(dims) - 2, F32)
    return x.reshape(x.shape[len(dims) :])


def add_up(parts):
    return sum(p.astype(F32) for p in parts)


def reduce_parts(dims, x, turn, stages):
    order = list(range(len(dims) - 2))
    if turn % 2:
        order.reverse()
    order = [len(dims) - 1] + order + [len(dims) - 2]
    for n, d in enumerate(order):
        size = dims[d].size
        block = [lax.slice_in_dim(x, r, r + 1, axis=d) for r in range(size)]
        if size == 2:
            x = add_up([block[0]] + [dims[d].fetch(block[r], -r) for r in range(1, size)])
        else:
            moving = block[size - 1]
            for r in range(size - 2, -1, -1):
                x = add_up([block[r], dims[d].fetch(moving, -1)])
                moving = x.astype(BF)
        if n < len(order) - 1:
            x = x.astype(BF)
            stages.append((n, x))
    return x.reshape(x.shape[len(dims) :])


def on_device(
    chan, held,
    hidden, modality, starts, norm_gain, in_weight, conv_weight, conv_bias, xproj_weight,
    dtproj_weight, step_bias, decay_log, skip_weight, out_weight, cotangent,
):
    def collect(x):
        return lax.all_gather(x, held, axis=0, tiled=True) if held else x

    def exchange(x):
        return lax.all_to_all(x, chan, 0, 0, tiled=True)

    def settle(x):
        return lax.psum_scatter(x, held, scatter_dimension=0, tiled=True) if held else x

    dims = dims_of(chan)
    sizes = tuple(d.size for d in dims)
    parts = math.prod(sizes)
    lots = math.prod(lax.axis_size(a) for a in held) if held else 1
    groups = parts // lax.axis_size("seq")
    rows, width = hidden.shape[1:]
    own = conv_weight.shape[0]
    lanes = own * lots
    rank_rows = dtproj_weight.shape[0]
    rank = rank_rows * parts * lots
    modes = in_weight.shape[1]
    states = decay_log.shape[1]
    mine = hidden[0]
    cot = cotangent[0]

    def shards(w):
        w = w.reshape(w.shape[0], modes, lots, parts, own)
        return jnp.moveaxis(w, 3, 0).reshape(parts, w.shape[0], modes, lanes)

    def to_owners(g, out_rows):
        return settle(g).reshape(parts, out_rows * modes, lanes)

    def returned(g, out_rows):
        g = g.reshape(parts, out_rows, modes, lots, own)
        return jnp.moveaxis(g, 0, 3).reshape(out_rows, modes, lots * parts * own)

    inner = lanes * parts
    blocks = parts // groups
    note = jnp.concatenate([modality[0], starts // 64, starts % 64]).astype(BF)
    note = jnp.pad(note[None], ((0, 15), (0, width - rows - 2)))
    pieces = gather_pieces(dims, jnp.concatenate([mine, note], axis=0))
    aux = jnp.stack([piece[rows, : rows + 2] for piece in pieces]).astype(jnp.int32)
    aux = aux.reshape(groups, blocks, rows + 2)
    begins = aux[:, 0, rows] * 64 + aux[:, 0, rows + 1]
    mode_ids = aux[:, :, :rows]
    room = -norm_gain.shape[0] % lanes
    notes = jnp.broadcast_to(jnp.pad(norm_gain, (0, room)), (parts, norm_gain.shape[0] + room))
    moved = collect(exchange(jnp.concatenate(
        [
            shards(in_weight[:, :, :inner]).reshape(parts, -1, lanes),
            shards(dtproj_weight).reshape(parts, -1, lanes),
            notes.reshape(parts, -1, lanes),
        ],
        axis=1,
    )))
    cut = in_weight.shape[0] * modes
    further = cut + rank_rows * modes
    x_cols = moved[:, :cut].reshape(width, modes * lanes)
    dt_cols = moved[:, cut:further].reshape(rank, modes * lanes)
    gain = moved[:, further:].reshape(parts * lots, -1)[:, : norm_gain.shape[0]]
    gain = gain.reshape(1, width).astype(F32)
    conv_weight, conv_bias, xproj_weight, step_bias, decay_log, skip_weight, out_weight = (
        collect(w)
        for w in (conv_weight, conv_bias, xproj_weight, step_bias, decay_log, skip_weight, out_weight)
    )
    taps = conv_weight.astype(F32).T
    bias = step_bias.astype(F32).T
    skip = skip_weight.astype(F32)[None]
    xproj = xproj_weight.reshape(lanes, -1)
    out_rows = jnp.moveaxis(out_weight, 1, 0).reshape(modes * lanes, width)
    masks = (mode_ids[..., None] == jnp.arange(modes, dtype=jnp.int32)).astype(F32)
    total = parts * rows
    copies = 8 // groups
    count = states // copies
    rate = -jnp.exp(decay_log.astype(F32))
    rates = jnp.moveaxis(rate.T.reshape(copies, count, lanes), 0, 1)
    rates = jnp.repeat(rates.reshape(count * copies, 1, lanes), groups, axis=1).reshape(-1, lanes)
    rates = rates * LOG2E
    order = jnp.zeros((), jnp.int32)
    spans = jnp.arange(blocks, dtype=jnp.int32)
    stride = blocks
    for d in dims:
        if d.axis == "seq":
            stride //= d.size
            order = order * d.size + (spans // stride % d.size - d.here()) % d.size
    table = order

    def placed(some):
        at = jnp.zeros((), jnp.int32)
        stride = math.prod(d.size for d in some)
        names = jnp.arange(stride, dtype=jnp.int32)
        for d in some:
            stride //= d.size
            at = at * d.size + (names // stride % d.size + d.here()) % d.size
        return at.reshape(-1)

    places = placed([d for d in dims if d.axis == "grp"])

    step_pieces = sizes[-1] * sizes[-2]
    lots_in = parts // step_pieces
    in_masks = masks.reshape(lots_in, step_pieces * rows, modes)
    so_far = None
    for n in range(lots_in):
        so_far = inproj(
            n, lots_in, pieces[n * step_pieces : (n + 1) * step_pieces], gain, x_cols, in_masks, so_far
        )
    normed, conv_in = so_far
    cots = lax.all_gather(after(cot, conv_in), chan, axis=0, tiled=True)
    gate_cols = collect(exchange(shards(after(in_weight[:, :, inner:], conv_in))).reshape(
        -1, modes, lanes
    )).reshape(width, modes * lanes)
    normed = normed.reshape(total, width)
    grouped = (groups, blocks, rows, lanes)
    pre_act, act, partial = conv(
        table, begins, conv_in.reshape(grouped), masks, taps, conv_bias.astype(F32)[None], xproj
    )
    picked = reduce_small(dims, partial.reshape(sizes + (-1, 128)))
    low = picked.astype(BF)
    rest = (picked[rows:] - low[rows:].astype(F32)).astype(BF)
    picked = gather_small(dims, jnp.concatenate([low, rest], axis=0))
    picked = picked.reshape(groups, blocks, -1, 128)
    flat_masks = masks.reshape(total, modes)
    gate_in = pick(dot(normed, gate_cols), flat_masks).reshape(grouped)
    read, gated, spread_gated, pre, prior, end = scan(
        table, begins, places, act, picked, masks, gate_in, rates, dt_cols, bias, skip, states
    )

    def scatter(x, weight, dim, stages):
        got = []
        chunk = width // 4
        for n in range(4):
            w = lax.slice_in_dim(weight, n * chunk, (n + 1) * chunk, axis=1 - dim)
            product = dot(x, w, ((1,), (dim,))).astype(BF).reshape(sizes + (rows, chunk))
            got.append(reduce_parts(dims, product, n, stages))
        return jnp.concatenate(got, axis=1)

    branch = dot(spread_gated.reshape(total, modes * lanes), out_rows).astype(BF)
    branch = lax.psum_scatter(branch, chan, scatter_dimension=0, tiled=True)
    output = (mine.astype(F32) + branch.astype(F32)).astype(BF)[None]

    lot = (lots_in, step_pieces * rows, -1)
    read_grad, gate_grad, grad_out_weight = cot_part(
        placed(dims[:-2]), placed(dims[-2:]), cots.reshape(lots_in, -1, width), out_rows,
        in_masks, gated.reshape(lot), read.reshape(lot), gate_in.reshape(lot),
    )
    grad_out_weight = jnp.moveaxis(grad_out_weight.reshape(modes, lanes, width), 0, 1)
    gate_grad = gate_grad.reshape(total, modes * lanes)
    in_rows = in_weight.shape[0]
    grad_gate_cols = exchange(to_owners(t_dot(normed, gate_grad).astype(BF), in_rows))
    begun = jnp.concatenate([jnp.zeros_like(end), end], axis=0)
    cuts = [blocks, 0]
    so_far = None
    sums = []
    for n in range(len(cuts) - 1):
        act_grad, picked_grad, begun, *more = scan_back(
            cuts[n + 1], cuts[n], table, begins, act, picked, masks, pre,
            read_grad.reshape(grouped), prior, begun, rates, dt_cols, bias, skip, states, so_far,
            [],
        )
        so_far = (act_grad, picked_grad)
        sums.append(more)
    rate_grad, grad_dt, grad_bias, grad_skip = (sum(parts_of) for parts_of in zip(*sums))
    rate_grad = rate_grad.reshape(count, copies, groups, lanes).sum(axis=2)
    grad_decay = jnp.moveaxis(rate_grad, 0, 1).reshape(states, lanes).T * rate
    picked_grad = reduce_small(dims, picked_grad.reshape(sizes + (-1, 128))).astype(BF)
    picked_grad = gather_small(dims, picked_grad).reshape(groups, blocks, -1, 128)
    x_grad, tap_grad, base_grad, grad_xproj = conv_back(
        table, begins, act_grad, picked_grad, pre_act, act, conv_in.reshape(grouped), masks, taps,
        xproj, [grad_gate_cols],
    )
    x_grad = x_grad.reshape(total, modes * lanes)
    grad_x_cols = exchange(jnp.concatenate(
        [
            to_owners(t_dot(normed, x_grad).astype(BF), in_rows),
            to_owners(grad_dt.astype(BF), rank_rows),
        ],
        axis=1,
    ))
    grad_dt = returned(grad_x_cols[:, in_rows * modes :], rank_rows).astype(F32)
    grad_x_cols = returned(grad_x_cols[:, : in_rows * modes], in_rows)
    grad_gate_cols = returned(grad_gate_cols, in_rows)
    normed_grad = scatter(
        jnp.concatenate([x_grad, gate_grad], axis=1),
        jnp.concatenate([x_cols, gate_cols], axis=1), 1, [],
    )
    grad_in = jnp.concatenate([grad_x_cols, grad_gate_cols], axis=2).astype(F32)
    grad_gain = jnp.sum(grad_in * in_weight.astype(F32), axis=(1, 2)) / norm_gain.astype(F32)
    xm = mine.astype(F32)
    scale = lax.rsqrt(jnp.mean(xm * xm, axis=1, keepdims=True) + EPS)
    unit = xm * scale
    scaled = normed_grad * gain
    grad_hidden = cotangent[0].astype(F32) + scale * (
        scaled - unit * jnp.mean(scaled * unit, axis=1, keepdims=True)
    )
    return (
        output,
        grad_hidden[None],
        grad_gain,
        grad_in,
        settle(tap_grad[:4].T),
        settle(base_grad[0]),
        settle(grad_xproj.reshape(lanes, modes, -1)),
        grad_dt,
        settle(grad_bias[:modes].T),
        settle(grad_decay),
        settle(grad_skip[0]),
        settle(grad_out_weight),
    )


def solution(mesh):
    both = ("grp", "seq")
    full = mesh.shape["grp"] * mesh.shape["seq"] <= 32
    chan, held = (both, ()) if full else (("seq",), ("grp",))
    row = P(both)
    return jax.shard_map(
        functools.partial(on_device, chan, held),
        mesh=mesh,
        in_specs=(
            P("grp", "seq", None), P("grp", "seq"), P("grp"),
            row, row, row, row, row, row, row, row, row, row,
            P("grp", "seq", None),
        ),
        out_specs=(P("grp", "seq", None), P("grp", "seq", None)) + (row,) * 10,
        check_vma=False,
    )
```

```python
import functools
import math

import jax
import jax.numpy as jnp
import numpy as np
from jax import lax
from jax.experimental import pallas as pl
from jax.experimental.pallas import tpu as pltpu
from jax.sharding import PartitionSpec as P

EPS = 1e-05
BF = jnp.bfloat16
F32 = jnp.float32
LOG2E = math.log2(math.e)
RESET = 1e4
VMEM = 48 * 1024 * 1024


def dot(a, b, dims=((1,), (0,))):
    return lax.dot_general(a, b, (dims, ((), ())), preferred_element_type=F32)


def silu_slope(v):
    s = jax.nn.sigmoid(v)
    return s * (1.0 + v * (1.0 - s))


def after(x, other):
    return x + (other[(0,) * other.ndim] * 0).astype(x.dtype)


def pick(values, masks):
    count = masks.shape[1]
    width = values.shape[1] // count
    return sum(values[:, m * width : (m + 1) * width] * masks[:, m : m + 1] for m in range(count))


def spread(values, masks):
    return jnp.concatenate(
        [values * masks[:, m : m + 1].astype(values.dtype) for m in range(masks.shape[1])], axis=1
    )


def spread_lanes(source, widen, target):

    low = source[...].astype(BF)
    for c in range(0, target.shape[1], 256):
        target[:, c : c + 256] = dot(low, widen[:, c : c + 256])


def widening(columns, lanes):
    ones = np.zeros((2 * columns, columns * lanes), np.float32)
    for s in range(columns):
        ones[s, s * lanes : (s + 1) * lanes] = 1
        ones[columns + s, s * lanes : (s + 1) * lanes] = 1
    return jnp.asarray(ones, BF)


def dot_t(a, b):
    return dot(a, b, ((1,), (1,)))


def t_dot(a, b):
    return dot(a, b, ((0,), (0,)))


def softplus(x):
    return jnp.maximum(x, 0.0) + jnp.log1p(jnp.exp(-jnp.abs(x)))


def packed(values, width):
    count = 128 // width
    span = values.shape[0] // count
    return jnp.concatenate([values[q * span : (q + 1) * span, :] for q in range(count)], axis=1)


def unpacked(values, width):
    values = values.astype(F32)
    return jnp.concatenate(
        [values[:, q * width : (q + 1) * width] for q in range(128 // width)], axis=0
    )


def to_time_major(ref, values, row, count):
    ref[pl.ds(row, count, stride=8), :] = values


def lay_out(groups, length, states, first, starts, step, act, picked, extra, sf, du, bc, also):
    copies = 8 // groups
    position = first + lax.broadcasted_iota(jnp.int32, (length, 1), 0)
    lane = lax.broadcasted_iota(jnp.int32, (1, 4 * states), 1)
    owner = lane % states // (states // copies)
    for g in range(groups):
        begin = (position == 0) | (position == starts[g])
        fade_step = jnp.where(begin, RESET, step[g])
        drive = step[g] * act[g, 0]
        span = length * 2 * states // 128
        chosen = jnp.concatenate(
            [
                unpacked(picked[g, 0, length + n * span : length + (n + 1) * span, :], 2 * states)
                for n in range(2)
            ],
            axis=1,
        )
        for j in range(copies):
            to_time_major(sf, fade_step, j * groups + g, length)
            to_time_major(du, drive, j * groups + g, length)
            to_time_major(bc, jnp.where(owner == j, chosen, 0.0), j * groups + g, length)
            if also is not None:
                to_time_major(also, extra[g, 0], j * groups + g, length)


def pre_step(picked, mask, dt, bias):
    modes, lanes = bias.shape
    product = dot(picked[: mask.shape[0], :], dt[...])
    return sum(
        (product[:, m * lanes : (m + 1) * lanes] + bias[m : m + 1, :]) * mask[:, m : m + 1]
        for m in range(modes)
    )


def scan_kernel(
    groups, length, states, table, starts, act, picked, mask, rate, widen, dt, bias, skip, y, pre, prior, end, sf, du, bc, ys, state, ex,
):
    copies, count, lanes = 8 // groups, rate.shape[0] // 8, rate.shape[1]
    i = pl.program_id(0)

    @pl.when(i == 0)
    def _():
        state[...] = jnp.zeros_like(state)

    steps = []
    for g in range(groups):
        raw = pre_step(picked[g, 0], mask[g, 0], dt, bias)
        pre[g, 0] = raw
        steps.append(softplus(raw))
    lay_out(groups, length, states, i * length, starts, steps, act, picked, None, sf, du, bc, None)
    spread_lanes(bc, widen, ex)
    rates = [rate[s * 8 : s * 8 + 8, :] for s in range(count)]

    def one(p, h):
        row = pl.ds(pl.multiple_of(p * 8, 8), 8)
        step_p, drive_p = sf[row, :], du[row, :]
        read = None
        out = []
        for s in range(count):
            prior[pl.ds(pl.multiple_of((p * count + s) * 8, 8), 8), :] = h[s]
            now = jnp.exp2(step_p * rates[s]) * h[s] + drive_p * ex[row, s * lanes : (s + 1) * lanes]
            term = now * ex[row, (count + s) * lanes : (count + s + 1) * lanes]
            read = term if read is None else read + term
            out.append(now)
        ys[row, :] = read
        return tuple(out)

    first = tuple(state[s * 8 : s * 8 + 8, :] for s in range(count))
    last = lax.fori_loop(0, length, one, first, unroll=4)
    for s in range(count):
        state[s * 8 : s * 8 + 8, :] = last[s]
    end[...] = state[...]
    for g in range(groups):
        total = sum(ys[pl.ds(j * groups + g, length, stride=8), :] for j in range(copies))
        total = total + skip[...] * act[g, 0]
        y[g, 0] = total


def back_kernel(
    groups, length, states, top, blocks, table, starts, act, picked, mask, pre, read_grad, prior,
    begun, rate, widen, dt, bias, skip, pick_b, pick_c, *refs,
):
    act_grad, picked_grad, left, rate_grad, dt_grad, bias_grad, skip_grad = refs[-20:-13]
    sf, du, gy, bc, wt, ft, pb, pc, res, carry, held, ex, step = refs[-13:]
    copies, count = 8 // groups, rate.shape[0] // 8
    lanes = rate.shape[1]
    modes = bias.shape[0]
    rank = dt.shape[0]
    i = pl.program_id(0)

    @pl.when(i == 0)
    def _():
        carry[...] = begun[0 : count * 8, :]
        held[...] = begun[count * 8 :, :]
        rate_grad[...] = jnp.zeros_like(rate_grad)
        dt_grad[...] = jnp.zeros_like(dt_grad)
        bias_grad[...] = jnp.zeros_like(bias_grad)
        skip_grad[...] = jnp.zeros_like(skip_grad)

    for g in range(groups):
        step[g] = softplus(pre[g, 0])
    lay_out(
        groups, length, states, (top - i) * length, starts, step, act, picked, read_grad, sf, du, bc, gy
    )
    spread_lanes(bc, widen, ex)
    rates = [rate[s * 8 : s * 8 + 8, :] for s in range(count)]

    def one(k, loop):
        p = length - 1 - k
        row = pl.ds(pl.multiple_of(p * 8, 8), 8)
        step_p, drive_p, grad_p = sf[row, :], du[row, :], gy[row, :]
        carried, state, total = loop
        weight_sum, fade_sum = None, None
        out_c, out_h, out_r = [], [], []
        for s in range(count):
            before = prior[pl.ds(pl.multiple_of((p * count + s) * 8, 8), 8), :]
            cols = slice(s * lanes, (s + 1) * lanes)
            e = grad_p * ex[row, (count + s) * lanes : (count + s + 1) * lanes] + carried[s]
            pc[row, cols] = grad_p * state[s]
            pb[row, cols] = e * drive_p
            term = e * ex[row, cols]
            passed = e * jnp.exp2(step_p * rates[s])
            decay = passed * before
            fade_term = decay * rates[s]
            weight_sum = term if weight_sum is None else weight_sum + term
            fade_sum = fade_term if fade_sum is None else fade_sum + fade_term
            out_c.append(passed)
            out_h.append(before)
            out_r.append(total[s] + decay * step_p)
        wt[row, :] = weight_sum
        ft[row, :] = fade_sum
        return tuple(out_c), tuple(out_h), tuple(out_r)

    def parts(ref):
        return tuple(ref[s * 8 : s * 8 + 8, :] for s in range(count))

    c, h, r = lax.fori_loop(
        0, length, one, (parts(carry), parts(held), parts(rate_grad)), unroll=2
    )
    for s in range(count):
        carry[s * 8 : s * 8 + 8, :] = c[s]
        held[s * 8 : s * 8 + 8, :] = h[s]
        rate_grad[s * 8 : s * 8 + 8, :] = r[s]
    left[0 : count * 8, :] = carry[...]
    left[count * 8 :, :] = held[...]
    res[...] = dot(pb[...].astype(BF), pick_b[...]) + dot(pc[...].astype(BF), pick_c[...])
    lane = lax.broadcasted_iota(jnp.int32, (1, 128), 1)
    owner = lane % states // count
    for g in range(groups):
        rows = [pl.ds(j * groups + g, length, stride=8) for j in range(copies)]
        weighted = sum(wt[row, :] for row in rows)
        faded = sum(ft[row, :] for row in rows) * (1.0 / LOG2E)
        chosen = sum(jnp.where(owner == j, res[rows[j], :], 0.0) for j in range(copies))
        grad_y, u = read_grad[g, 0], act[g, 0]
        act_grad[g, 0] = skip[...] * grad_y + step[g] * weighted
        pre_grad = (u * weighted + faded) * jax.nn.sigmoid(pre[g, 0])
        skip_grad[...] += jnp.sum(grad_y * u, axis=0, keepdims=True)
        rank_grad = None
        for m in range(modes):
            own = pre_grad * mask[g, 0, :, m : m + 1]
            bias_grad[m : m + 1, :] += jnp.sum(own, axis=0, keepdims=True)
            own = own.astype(BF)
            cols = slice(m * lanes, (m + 1) * lanes)
            term = dot_t(own, dt[:, cols])
            rank_grad = term if rank_grad is None else rank_grad + term
            dt_grad[:, cols] += t_dot(picked[g, 0, 0:length, :], own)
        picked_grad[g, 0, 0:length, :] = rank_grad
        picked_grad[g, 0, length:, :] = packed(chosen[:, 0 : 2 * states], 2 * states)


def spread_lanes(source, widen, target):

    @pl.loop(0, source.shape[0] // 128)
    def _(n):
        row = pl.ds(pl.multiple_of(n * 128, 128), 128)
        target[row, :] = dot(source[row, :].astype(BF), widen[...])


def widening(states, count, lanes):
    ones = np.zeros((2, 2, states, 2 * count * lanes), np.float32)
    for kind in range(2):
        for s in range(states):
            block = kind * count + s % count
            ones[:, kind, s, block * lanes : (block + 1) * lanes] = 1
    return jnp.asarray(ones.reshape(4 * states, -1), BF)


def picking(states, count, lanes):
    ones = np.zeros((2, count * lanes, 128), np.float32)
    for kind in range(2):
        for s in range(states):
            at = s % count
            ones[kind, at * lanes : (at + 1) * lanes, kind * states + s] = 1
    return jnp.asarray(ones[0], BF), jnp.asarray(ones[1], BF)


def conv_kernel(groups, length, table, starts, x, mask, taps, base, xproj, v, act, part, tail, ext):
    i = pl.program_id(0)

    @pl.when(i == 0)
    def _():
        tail[...] = jnp.zeros_like(tail)

    modes = mask.shape[3]
    width = xproj.shape[1] // modes
    position = i * length + lax.broadcasted_iota(jnp.int32, (length, 1), 0)
    for g in range(groups):
        begin = jnp.where(position >= starts[g], starts[g], 0)
        ext[0:8, :] = tail[g]
        ext[8 : 8 + length, :] = x[g, 0]
        tail[g] = x[g, 0, length - 8 : length, :]
        total = base[...]
        for k in range(4):
            valid = (position - 3 + k >= begin).astype(F32)
            total = total + taps[k : k + 1, :] * ext[5 + k : 5 + k + length, :] * valid
        v[g, 0] = total
        active = total * jax.nn.sigmoid(total)
        act[g, 0] = active
        product = dot(active.astype(BF), xproj[...])
        chosen = sum(
            product[:, m * width : (m + 1) * width] * mask[g, 0, :, m : m + 1] for m in range(modes)
        )
        part[g, 0, 0:length, :] = chosen[:, 0:128]
        part[g, 0, length:, :] = packed(chosen[:, 128:], width - 128)


def conv_back_kernel(
    groups, length, blocks, table, starts, grad, sel_grad, v, act, x, mask, taps, xproj, *refs,
):
    x_grad, tap_grad, base_grad, weight_grad, head, ext = refs[-6:]
    i = pl.program_id(0)

    @pl.when(i == 0)
    def _():
        head[...] = jnp.zeros_like(head)
        weight_grad[...] = jnp.zeros_like(weight_grad)
        tap_grad[...] = jnp.zeros_like(tap_grad)
        base_grad[...] = jnp.zeros_like(base_grad)

    modes = mask.shape[3]
    width = xproj.shape[1] // modes
    position = (blocks - 1 - i) * length + lax.broadcasted_iota(jnp.int32, (length, 1), 0)
    for g in range(groups):
        chosen = jnp.concatenate(
            [
                sel_grad[g, 0, 0:length, :].astype(F32),
                unpacked(sel_grad[g, 0, length:, :], width - 128),
            ],
            axis=1,
        ).astype(BF)
        masked = [chosen * mask[g, 0, :, m : m + 1].astype(BF) for m in range(modes)]
        act_grad = grad[g, 0]
        low = act[g, 0].astype(BF)
        for m in range(modes):
            cols = slice(m * width, (m + 1) * width)
            act_grad = act_grad + dot_t(masked[m], xproj[:, cols])
            weight_grad[:, cols] += t_dot(low, masked[m])
        v_grad = act_grad * silu_slope(v[g, 0])
        ext[0:length, :] = v_grad
        ext[length : length + 8, :] = head[g]
        head[g] = v_grad[0:8, :]
        base_grad[...] += jnp.sum(v_grad, axis=0, keepdims=True)
        total = None
        for k in range(4):
            crosses = (position < starts[g]) & (position + 3 - k >= starts[g])
            shifted = jnp.where(crosses, 0.0, ext[3 - k : 3 - k + length, :])
            term = taps[k : k + 1, :] * shifted
            total = term if total is None else total + term
            tap_grad[k : k + 1, :] += jnp.sum(x[g, 0] * shifted, axis=0, keepdims=True)
        total = total.astype(BF)
        lanes = total.shape[1]
        for m in range(modes):
            x_grad[g, 0, :, m * lanes : (m + 1) * lanes] = total * mask[g, 0, :, m : m + 1].astype(BF)


def inproj_kernel(count, *refs):
    pieces, (gain, weight), (normed, proj, mask, notes) = refs[:count], refs[count : count + 2], refs[-4:]
    modes = mask.shape[2]
    rows = mask.shape[1] // count
    square = (rows, rows)
    same = lax.broadcasted_iota(jnp.int32, square, 0) == lax.broadcasted_iota(jnp.int32, square, 1)
    kind = lax.broadcasted_iota(jnp.int32, (1, modes), 1).astype(F32)
    for n in range(count):
        span = slice(n * rows, (n + 1) * rows)
        x = pieces[n][0:rows, :].astype(F32)
        scale = lax.rsqrt(jnp.mean(x * x, axis=1, keepdims=True) + EPS)
        normed[0, span, :] = (x * scale * gain[...]).astype(BF)
        note = pieces[n][rows : rows + 16, 0:rows].astype(F32)
        column = jnp.sum(jnp.where(same, note[0:1, :], 0.0), axis=1, keepdims=True)
        mask[0, span, :] = (column == kind).astype(F32)
        if n == 0:
            notes[0] = note[0:8, :]
    product = dot(normed[0], weight[...])
    width = weight.shape[1] // modes
    proj[0] = sum(
        product[:, m * width : (m + 1) * width] * mask[0, :, m : m + 1] for m in range(modes)
    )


def inproj(at, lots, rows, modes, pieces, gain, weight, so_far):
    tall, width = pieces[0].shape
    count = len(pieces)
    columns = weight.shape[1] // modes
    here = lambda i: (at, 0, 0)
    size = count * rows
    extra = tuple(so_far or ())
    return pl.pallas_call(
        functools.partial(inproj_kernel, count),
        grid=(1,),
        in_specs=[flat(a) for a in (*pieces, gain, weight)]
        + [pl.BlockSpec(memory_space=pl.ANY)] * len(extra),
        out_specs=[pl.BlockSpec((1,) + shape, here) for shape in (
            (size, width), (size, columns), (size, modes), (8, rows)
        )],
        out_shape=[
            jax.ShapeDtypeStruct((lots, size, width), BF),
            jax.ShapeDtypeStruct((lots, size, columns), F32),
            jax.ShapeDtypeStruct((lots, size, modes), F32),
            jax.ShapeDtypeStruct((lots, 8, rows), F32),
        ],
        input_output_aliases={count + 2 + n: n for n in range(len(extra))},
        compiler_params=pltpu.CompilerParams(vmem_limit_bytes=VMEM),
        cost_estimate=pl.CostEstimate(
            flops=2 * size * width * weight.shape[1],
            bytes_accessed=6 * size * width,
            transcendentals=0,
        ),
    )(*pieces, gain, weight, *extra)


def conv(table, starts, x, mask, taps, base, xproj):
    groups, blocks, length, lanes = x.shape
    modes = mask.shape[3]
    width = xproj.shape[1] // modes
    at = lambda i, t, b: (0, t[i], 0, 0)
    flat = lambda i, t, b: (0, 0)
    block = pl.BlockSpec((groups, 1, length, lanes), at)
    return pl.pallas_call(
        functools.partial(conv_kernel, groups, length),
        grid_spec=pltpu.PrefetchScalarGridSpec(
            num_scalar_prefetch=2,
            grid=(blocks,),
            in_specs=[
                block,
                pl.BlockSpec((groups, 1, length, modes), at),
                pl.BlockSpec(taps.shape, flat),
                pl.BlockSpec(base.shape, flat),
                pl.BlockSpec(xproj.shape, flat),
            ],
            out_specs=[block, block, pl.BlockSpec((groups, 1, length * width // 128, 128), at)],
            scratch_shapes=[
                pltpu.VMEM((groups, 8, lanes), F32),
                pltpu.VMEM((length + 8, lanes), F32),
            ],
        ),
        out_shape=[
            jax.ShapeDtypeStruct(x.shape, F32),
            jax.ShapeDtypeStruct(x.shape, F32),
            jax.ShapeDtypeStruct((groups, blocks, length * width // 128, 128), F32),
        ],
        compiler_params=pltpu.CompilerParams(vmem_limit_bytes=VMEM),
    )(table, starts, x, mask, taps, base, xproj)


def conv_back(table, starts, grad, sel_grad, v, act, x, mask, taps, xproj, before):
    groups, blocks, length, lanes = x.shape
    modes = mask.shape[3]
    width = xproj.shape[1] // modes
    at = lambda i, t, b: (0, t[blocks - 1 - i], 0, 0)
    flat = lambda i, t, b: (0, 0)
    block = pl.BlockSpec((groups, 1, length, lanes), at)
    return pl.pallas_call(
        functools.partial(conv_back_kernel, groups, length, blocks),
        grid_spec=pltpu.PrefetchScalarGridSpec(
            num_scalar_prefetch=2,
            grid=(blocks,),
            in_specs=[
                block,
                pl.BlockSpec((groups, 1, length * width // 128, 128), at),
                block,
                block,
                block,
                pl.BlockSpec((groups, 1, length, modes), at),
                pl.BlockSpec(taps.shape, flat),
                pl.BlockSpec(xproj.shape, flat),
            ]
            + [pl.BlockSpec(memory_space=pl.ANY)] * len(before),
            out_specs=[
                pl.BlockSpec((groups, 1, length, modes * lanes), at),
                pl.BlockSpec((8, lanes), flat),
                pl.BlockSpec((1, lanes), flat),
                pl.BlockSpec(xproj.shape, flat),
            ],
            scratch_shapes=[
                pltpu.VMEM((groups, 8, lanes), F32),
                pltpu.VMEM((length + 8, lanes), F32),
            ],
        ),
        out_shape=[
            jax.ShapeDtypeStruct((groups, blocks, length, modes * lanes), BF),
            jax.ShapeDtypeStruct((8, lanes), F32),
            jax.ShapeDtypeStruct((1, lanes), F32),
            jax.ShapeDtypeStruct(xproj.shape, F32),
        ],
        compiler_params=pltpu.CompilerParams(vmem_limit_bytes=VMEM),
    )(table, starts, grad, sel_grad, v, act, x, mask, taps, xproj, *before)


def flat(array):
    return pl.BlockSpec(array.shape, lambda i, *_: (0,) * array.ndim)


def scan(table, starts, act, picked, mask, rate, dt, bias, skip, states):
    groups, blocks, length, lanes = act.shape
    total = blocks * length
    count = rate.shape[0] // 8
    at = lambda i, t, b: (0, t[i], 0, 0)
    block = lambda a: pl.BlockSpec((groups, 1) + a.shape[2:], at)
    widen = widening(states, count, lanes)
    tall = pltpu.VMEM((length * 8, lanes), F32)
    like = jax.ShapeDtypeStruct(act.shape, F32)
    return pl.pallas_call(
        functools.partial(scan_kernel, groups, length, states),
        grid_spec=pltpu.PrefetchScalarGridSpec(
            num_scalar_prefetch=2,
            grid=(blocks,),
            in_specs=[block(a) for a in (act, picked, mask)]
            + [flat(a) for a in (rate, widen, dt, bias, skip)],
            out_specs=[
                block(act),
                block(act),
                pl.BlockSpec((length * count * 8, lanes), lambda i, t, b: (i, 0)),
                flat(rate),
            ],
            scratch_shapes=[
                tall,
                tall,
                pltpu.VMEM((length * 8, 4 * states), F32),
                tall,
                pltpu.VMEM((count * 8, lanes), F32),
                pltpu.VMEM((length * 8, 2 * count * lanes), F32),
            ],
        ),
        out_shape=[
            like,
            like,
            jax.ShapeDtypeStruct((total * count * 8, lanes), F32),
            jax.ShapeDtypeStruct((count * 8, lanes), F32),
        ],
        compiler_params=pltpu.CompilerParams(vmem_limit_bytes=VMEM),
        cost_estimate=pl.CostEstimate(flops=10**10, bytes_accessed=10**8, transcendentals=0),
    )(table, starts, act, picked, mask, rate, widen, dt, bias, skip)


def gate_kernel(lots_at, spans_at, normed, weight, mask, read, gate, gated, spread_gated):
    modes = mask.shape[2]
    lanes = read.shape[2]
    count = spans_at.shape[0]
    rows = read.shape[1] // count
    product = dot(normed[0], weight[...])
    masks = [mask[0, :, m : m + 1] for m in range(modes)]
    opened = sum(product[:, m * lanes : (m + 1) * lanes] * masks[m] for m in range(modes))
    gate[0] = opened
    low = (read[0] * (opened * jax.nn.sigmoid(opened))).astype(BF)
    gated[0] = low
    for m in range(modes):
        own = low * masks[m].astype(BF)
        for n in range(count):
            place = pl.ds(pl.multiple_of(spans_at[n] * rows, rows), rows)
            spread_gated[0, place, m * lanes : (m + 1) * lanes] = own[n * rows : (n + 1) * rows, :]


def gate_part(lots_at, spans_at, normed, weight, mask, read):
    lots, size, width = normed.shape
    lanes = read.shape[2]
    wide = weight.shape[1]
    block = lambda w: pl.BlockSpec((1, size, w), lambda i, a, b: (i, 0, 0))
    return pl.pallas_call(
        gate_kernel,
        grid_spec=pltpu.PrefetchScalarGridSpec(
            num_scalar_prefetch=2,
            grid=(lots,),
            in_specs=[block(width), flat(weight), block(mask.shape[2]), block(lanes)],
            out_specs=[
                block(lanes), block(lanes), pl.BlockSpec((1, size, wide), lambda i, a, b: (a[i], 0, 0))
            ],
        ),
        out_shape=[
            jax.ShapeDtypeStruct(read.shape, F32),
            jax.ShapeDtypeStruct(read.shape, BF),
            jax.ShapeDtypeStruct((lots, size, wide), BF),
        ],
        compiler_params=pltpu.CompilerParams(vmem_limit_bytes=VMEM),
        cost_estimate=pl.CostEstimate(
            flops=2 * lots * size * width * wide, bytes_accessed=3 * lots * size * width, transcendentals=0
        ),
    )(lots_at, spans_at, normed, weight, mask, read)


def scan_back(
    first, last, table, starts, act, picked, mask, pre, read_grad, prior, begun, rate, dt, bias,
    skip, states, so_far, before,
):
    groups, blocks, length, lanes = act.shape
    count = rate.shape[0] // 8
    rank = dt.shape[0]
    modes = bias.shape[0]
    at = lambda i, t, b: (0, t[last - 1 - i], 0, 0)
    block = lambda a: pl.BlockSpec((groups, 1) + a.shape[2:], at)
    widen = widening(states, count, lanes)
    pick_b, pick_c = picking(states, count, lanes)
    tall = pltpu.VMEM((length * 8, lanes), F32)
    wide = pltpu.VMEM((length * 8, count * lanes), F32)
    tables = pltpu.VMEM((count * 8, lanes), F32)
    shapes = [
        jax.ShapeDtypeStruct(act.shape, F32),
        jax.ShapeDtypeStruct((groups, blocks, length + length * 2 * states // 128, 128), F32),
        jax.ShapeDtypeStruct((2 * count * 8, lanes), F32),
        jax.ShapeDtypeStruct((count * 8, lanes), F32),
        jax.ShapeDtypeStruct((rank, modes * lanes), F32),
        jax.ShapeDtypeStruct((8, lanes), F32),
        jax.ShapeDtypeStruct((1, lanes), F32),
    ]
    loaded = (begun, rate, widen, dt, bias, skip, pick_b, pick_c)
    extra = tuple(so_far or ()) + tuple(before)
    at_input = 2 + 6 + len(loaded)
    return pl.pallas_call(
        functools.partial(back_kernel, groups, length, states, last - 1, blocks),
        grid_spec=pltpu.PrefetchScalarGridSpec(
            num_scalar_prefetch=2,
            grid=(last - first,),
            in_specs=[block(a) for a in (act, picked, mask, pre, read_grad)]
            + [pl.BlockSpec((length * count * 8, lanes), lambda i, t, b: (last - 1 - i, 0))]
            + [flat(a) for a in loaded]
            + [pl.BlockSpec(memory_space=pl.ANY)] * len(extra),
            out_specs=[block(shapes[0]), block(shapes[1])] + [flat(a) for a in shapes[2:]],
            scratch_shapes=[
                tall, tall, tall, pltpu.VMEM((length * 8, 4 * states), F32), tall, tall, wide, wide,
                pltpu.VMEM((length * 8, 128), F32),
                tables,
                tables,
                pltpu.VMEM((length * 8, 2 * count * lanes), F32),
                pltpu.VMEM((groups, length, lanes), F32),
            ],
        ),
        out_shape=shapes,
        input_output_aliases={at_input: 0, at_input + 1: 1} if so_far else {},
        compiler_params=pltpu.CompilerParams(vmem_limit_bytes=VMEM),
        cost_estimate=pl.CostEstimate(
            flops=10**10, bytes_accessed=25 * 10**6 * (last - first), transcendentals=0
        ),
    )(table, starts, act, picked, mask, pre, read_grad, prior, *loaded, *extra)


def cot_kernel(
    lots_at, spans_at, cots, out_rows, mask, gated, read, gate, read_grad, gate_grad, weight_grad, whole
):
    count = spans_at.shape[0]
    rows = whole.shape[0] // count

    @pl.when(pl.program_id(0) == 0)
    def _():
        weight_grad[...] = jnp.zeros_like(weight_grad)

    for n in range(count):
        whole[n * rows : (n + 1) * rows, :] = cots[
            0, pl.ds(pl.multiple_of(spans_at[n] * rows, rows), rows), :
        ]
    product = dot_t(whole[...], out_rows[...])
    modes = mask.shape[2]
    lanes = gated.shape[2]
    masks = [mask[0, :, m : m + 1] for m in range(modes)]
    grad = sum(product[:, m * lanes : (m + 1) * lanes] * masks[m] for m in range(modes))
    opened = gate[0]
    read_grad[0] = grad * (opened * jax.nn.sigmoid(opened))
    gate_low = (grad * read[0] * silu_slope(opened)).astype(BF)
    for m in range(modes):
        own = masks[m].astype(BF)
        cols = slice(m * lanes, (m + 1) * lanes)
        gate_grad[0, :, cols] = gate_low * own
        weight_grad[cols, :] += t_dot(gated[0] * own, whole[...])


def cot_part(lots_at, spans_at, cots, out_rows, mask, gated, read, gate):
    lots, size, width = cots.shape
    lanes = gated.shape[2]
    wide = out_rows.shape[0]
    block = lambda w: pl.BlockSpec((1, size, w), lambda i, a, b: (i, 0, 0))
    return pl.pallas_call(
        cot_kernel,
        grid_spec=pltpu.PrefetchScalarGridSpec(
            num_scalar_prefetch=2,
            grid=(lots,),
            in_specs=[pl.BlockSpec((1, size, width), lambda i, a, b: (a[i], 0, 0)), flat(out_rows)]
            + [block(a.shape[2]) for a in (mask, gated, read, gate)],
            out_specs=[block(lanes), block(wide), flat(out_rows)],
            scratch_shapes=[pltpu.VMEM((size, width), BF)],
        ),
        out_shape=[
            jax.ShapeDtypeStruct((lots, size, lanes), F32),
            jax.ShapeDtypeStruct((lots, size, wide), BF),
            jax.ShapeDtypeStruct(out_rows.shape, F32),
        ],
        compiler_params=pltpu.CompilerParams(vmem_limit_bytes=VMEM),
        cost_estimate=pl.CostEstimate(
            flops=4 * lots * size * width * wide, bytes_accessed=3 * lots * size * width, transcendentals=0
        ),
    )(lots_at, spans_at, cots, out_rows, mask, gated, read, gate)


class Dim:

    def __init__(self, axis, stride, size, length):
        self.axis, self.stride, self.size, self.length = axis, stride, size, length

    def here(self):
        return lax.axis_index(self.axis) // self.stride % self.size

    def fetch(self, x, by):
        pairs = []
        for i in range(self.length):
            c = i // self.stride % self.size
            pairs.append((i + ((c + by) % self.size - c) * self.stride, i))
        return lax.ppermute(x, self.axis, pairs)


def dims_of(chan):
    dims = []
    for axis in chan:
        length = lax.axis_size(axis)
        sizes = []
        rest = length
        if axis == "seq":
            rest //= 2
        radix = 4 if axis == "seq" else 2
        while rest > 1:
            sizes.insert(0, min(radix, rest))
            rest //= sizes[0]
        if axis == "seq":
            sizes.append(2)
        stride = length
        for size in sizes:
            stride //= size
            dims.append(Dim(axis, stride, size, length))
    return dims


def fence(*arrays):
    return list(pl.pallas_call(
        lambda *refs: None,
        in_specs=[pl.BlockSpec(memory_space=pl.ANY)] * len(arrays),
        out_specs=[pl.BlockSpec(memory_space=pl.ANY)] * len(arrays),
        out_shape=[jax.ShapeDtypeStruct(x.shape, x.dtype) for x in arrays],
        input_output_aliases={n: n for n in range(len(arrays))},
    )(*arrays))


def gather_pieces(dims, x):
    others, ring, core = dims[:-2], dims[-2], dims[-1]
    got = {}
    first = x
    for k in range(ring.size):
        if k:
            first = ring.fetch(first, 1)
        order = list(range(len(others)))
        if k % 2:
            order.reverse()
        held = {(0,) * len(others): first}
        for d in order:
            for at, block in list(held.items()):
                for r in range(1, others[d].size):
                    block = others[d].fetch(block, 1)
                    held[at[:d] + (r,) + at[d + 1 :]] = block
        for at, block in held.items():
            got[at + (k, 0)] = block
            got[at + (k, 1)] = core.fetch(block, 1)
    return [got[at] for at in sorted(got)]


def pairs_of(dims):
    return [d.size for d in dims[:-2]] == [2, 2]


def gather_stage(dims, x, d):
    got = [x] + [dims[d].fetch(x, r) for r in range(1, dims[d].size)]
    return jnp.concatenate(got, axis=d)


def gather_small(dims, x):
    x = x.reshape((1,) * len(dims) + x.shape)
    x = gather_stage(dims, x, len(dims) - 2)
    if pairs_of(dims):
        halves = jnp.split(x, 2, axis=len(dims))
        halves = [gather_stage(dims, h, n) for n, h in enumerate(halves)]
        halves = [gather_stage(dims, h, 1 - n) for n, h in enumerate(halves)]
        x = jnp.concatenate(halves, axis=len(dims))
    else:
        for d in range(len(dims) - 2):
            x = gather_stage(dims, x, d)
    return gather_stage(dims, x, len(dims) - 1)


def reduce_stage(dims, x, d, kind):
    block = [lax.slice_in_dim(x, r, r + 1, axis=d) for r in range(dims[d].size)]
    return add_up(
        [block[0]] + [dims[d].fetch(block[r].astype(kind), -r) for r in range(1, len(block))]
    )


def reduce_small(dims, x):
    x = reduce_stage(dims, x, len(dims) - 1, F32)
    if pairs_of(dims):
        halves = jnp.split(x, 2, axis=len(dims))
        halves = [reduce_stage(dims, h, n, BF) for n, h in enumerate(halves)]
        halves = [reduce_stage(dims, h, 1 - n, F32) for n, h in enumerate(halves)]
        x = jnp.concatenate(halves, axis=len(dims))
    else:
        for d in range(len(dims) - 2):
            x = reduce_stage(dims, x, d, F32 if d else BF)
    x = reduce_stage(dims, x, len(dims) - 2, F32)
    return x.reshape(x.shape[len(dims) :])


def add_up(parts):
    return sum(p.astype(F32) for p in parts)


def reduce_parts(dims, x, turn, stages):
    order = list(range(len(dims) - 2))
    if turn % 2:
        order.reverse()
    order = [len(dims) - 1] + order + [len(dims) - 2]
    for n, d in enumerate(order):
        size = dims[d].size
        block = [lax.slice_in_dim(x, r, r + 1, axis=d) for r in range(size)]
        if size == 2:
            x = add_up([block[0]] + [dims[d].fetch(block[r], -r) for r in range(1, size)])
        else:
            moving = block[size - 1]
            for r in range(size - 2, -1, -1):
                x = add_up([block[r], dims[d].fetch(moving, -1)])
                moving = x.astype(BF)
        if n < len(order) - 1:
            x = x.astype(BF)
            stages.append((n, x))
    return x.reshape(x.shape[len(dims) :])


def on_device(
    chan, held,
    hidden, modality, starts, norm_gain, in_weight, conv_weight, conv_bias, xproj_weight,
    dtproj_weight, step_bias, decay_log, skip_weight, out_weight, cotangent,
):
    def collect(x):
        return lax.all_gather(x, held, axis=0, tiled=True) if held else x

    def exchange(x):
        return lax.all_to_all(x, chan, 0, 0, tiled=True)

    def settle(x):
        return lax.psum_scatter(x, held, scatter_dimension=0, tiled=True) if held else x

    dims = dims_of(chan)
    sizes = tuple(d.size for d in dims)
    parts = math.prod(sizes)
    lots = math.prod(lax.axis_size(a) for a in held) if held else 1
    groups = parts // lax.axis_size("seq")
    rows, width = hidden.shape[1:]
    own = conv_weight.shape[0]
    lanes = own * lots
    rank_rows = dtproj_weight.shape[0]
    rank = rank_rows * parts * lots
    modes = in_weight.shape[1]
    states = decay_log.shape[1]
    mine = hidden[0]
    cot = cotangent[0]

    def shards(w):
        w = w.reshape(w.shape[0], modes, lots, parts, own)
        return jnp.moveaxis(w, 3, 0).reshape(parts, w.shape[0], modes, lanes)

    def to_owners(g, out_rows):
        return settle(g).reshape(parts, out_rows * modes, lanes)

    def returned(g, out_rows):
        g = g.reshape(parts, out_rows, modes, lots, own)
        return jnp.moveaxis(g, 0, 3).reshape(out_rows, modes, lots * parts * own)

    inner = lanes * parts
    blocks = parts // groups
    note = jnp.pad(jnp.stack([starts[0] >> 6, starts[0] & 63])[None], ((0, 0), (0, rows - 2)))
    note = jnp.concatenate([modality, note], axis=0).astype(BF)
    note = jnp.pad(note, ((0, 14), (0, width - rows)))
    pieces = gather_pieces(dims, jnp.concatenate([mine, note], axis=0))
    room = -norm_gain.shape[0] % lanes
    notes = jnp.broadcast_to(jnp.pad(norm_gain, (0, room)), (parts, norm_gain.shape[0] + room))
    moved = collect(exchange(jnp.concatenate(
        [
            shards(in_weight[:, :, :inner]).reshape(parts, -1, lanes),
            shards(dtproj_weight).reshape(parts, -1, lanes),
            notes.reshape(parts, -1, lanes),
        ],
        axis=1,
    )))
    cut = in_weight.shape[0] * modes
    further = cut + rank_rows * modes
    x_cols = moved[:, :cut].reshape(width, modes * lanes)
    dt_cols = moved[:, cut:further].reshape(rank, modes * lanes)
    gain = moved[:, further:].reshape(parts * lots, -1)[:, : norm_gain.shape[0]]
    gain = gain.reshape(1, width).astype(F32)
    conv_weight, conv_bias, xproj_weight, step_bias, decay_log, skip_weight, out_weight = (
        collect(w)
        for w in (conv_weight, conv_bias, xproj_weight, step_bias, decay_log, skip_weight, out_weight)
    )
    taps = conv_weight.astype(F32).T
    bias = step_bias.astype(F32).T
    skip = skip_weight.astype(F32)[None]
    xproj = xproj_weight.reshape(lanes, -1)
    out_rows = jnp.moveaxis(out_weight, 1, 0).reshape(modes * lanes, width)
    total = parts * rows
    copies = 8 // groups
    count = states // copies
    rate = -jnp.exp(decay_log.astype(F32))
    rates = jnp.moveaxis(rate.T.reshape(copies, count, lanes), 0, 1)
    rates = jnp.repeat(rates.reshape(count * copies, 1, lanes), groups, axis=1).reshape(-1, lanes)
    rates = rates * LOG2E
    order = jnp.zeros((), jnp.int32)
    spans = jnp.arange(blocks, dtype=jnp.int32)
    stride = blocks
    for d in dims:
        if d.axis == "seq":
            stride //= d.size
            order = order * d.size + (spans // stride % d.size - d.here()) % d.size
    table = order

    def placed(some):
        at = jnp.zeros((), jnp.int32)
        stride = math.prod(d.size for d in some)
        names = jnp.arange(stride, dtype=jnp.int32)
        for d in some:
            stride //= d.size
            at = at * d.size + (names // stride % d.size + d.here()) % d.size
        return at.reshape(-1)


    step_pieces = sizes[-1] * sizes[-2]
    lots_in = parts // step_pieces
    so_far = None
    for n in range(lots_in):
        so_far = inproj(
            n, lots_in, rows, modes, pieces[n * step_pieces : (n + 1) * step_pieces], gain, x_cols, so_far
        )
    normed, conv_in, in_masks, notes = so_far
    masks = in_masks.reshape(groups, blocks, rows, modes)
    notes = notes.reshape(groups, -1, 8, rows)[:, 0, 1].astype(jnp.int32)
    begins = notes[:, 0] * 64 + notes[:, 1]
    cots = lax.all_gather(after(cot, conv_in), chan, axis=0, tiled=True)
    normed = normed.reshape(total, width)
    grouped = (groups, blocks, rows, lanes)
    pre_act, act, partial = conv(
        table, begins, conv_in.reshape(grouped), masks, taps, conv_bias.astype(F32)[None], xproj
    )
    picked = reduce_small(dims, partial.reshape(sizes + (-1, 128)))
    low = picked.astype(BF)
    rest = (picked[rows:] - low[rows:].astype(F32)).astype(BF)
    picked = gather_small(dims, jnp.concatenate([low, rest], axis=0))
    picked = picked.reshape(groups, blocks, -1, 128)
    gate_cols = collect(exchange(shards(after(in_weight[:, :, inner:], picked))).reshape(
        -1, modes, lanes
    )).reshape(width, modes * lanes)
    read, pre, prior, end = scan(
        table, begins, act, picked, masks, rates, dt_cols, bias, skip, states
    )
    lot = (lots_in, step_pieces * rows, -1)
    lots_at, spans_at = placed(dims[:-2]), placed(dims[-2:])
    gate_in, gated, spread_gated = gate_part(
        lots_at, spans_at, normed.reshape(lot), gate_cols, in_masks, read.reshape(lot)
    )

    def scatter(x, weight, dim, stages):
        got = []
        chunk = width // 4
        for n in range(4):
            w = lax.slice_in_dim(weight, n * chunk, (n + 1) * chunk, axis=1 - dim)
            product = dot(x, w, ((1,), (dim,))).astype(BF).reshape(sizes + (rows, chunk))
            got.append(reduce_parts(dims, product, n, stages))
        return jnp.concatenate(got, axis=1)

    branch = dot(spread_gated.reshape(total, modes * lanes), out_rows).astype(BF)
    branch = lax.psum_scatter(branch, chan, scatter_dimension=0, tiled=True)
    output = (mine.astype(F32) + branch.astype(F32)).astype(BF)[None]

    read_grad, gate_grad, grad_out_weight = cot_part(
        lots_at, spans_at, cots.reshape(lots_in, -1, width), out_rows, in_masks, gated,
        read.reshape(lot), gate_in,
    )
    grad_out_weight = jnp.moveaxis(grad_out_weight.reshape(modes, lanes, width), 0, 1)
    gate_grad = gate_grad.reshape(total, modes * lanes)
    in_rows = in_weight.shape[0]
    gate_sent = to_owners(t_dot(normed, gate_grad).astype(BF), in_rows)
    begun = jnp.concatenate([jnp.zeros_like(end), end], axis=0)
    cuts = [blocks, 0]
    so_far = None
    sums = []
    for n in range(len(cuts) - 1):
        act_grad, picked_grad, begun, *more = scan_back(
            cuts[n + 1], cuts[n], table, begins, act, picked, masks, pre,
            read_grad.reshape(grouped), prior, begun, rates, dt_cols, bias, skip, states, so_far,
            [],
        )
        so_far = (act_grad, picked_grad)
        sums.append(more)
    rate_grad, grad_dt, grad_bias, grad_skip = (sum(parts_of) for parts_of in zip(*sums))
    rate_grad = rate_grad.reshape(count, copies, groups, lanes).sum(axis=2)
    grad_decay = jnp.moveaxis(rate_grad, 0, 1).reshape(states, lanes).T * rate
    picked_grad = reduce_small(dims, picked_grad.reshape(sizes + (-1, 128))).astype(BF)
    picked_grad = gather_small(dims, picked_grad).reshape(groups, blocks, -1, 128)
    grad_gate_cols = exchange(after(gate_sent, picked_grad))
    x_grad, tap_grad, base_grad, grad_xproj = conv_back(
        table, begins, act_grad, picked_grad, pre_act, act, conv_in.reshape(grouped), masks, taps,
        xproj, [],
    )
    x_grad = x_grad.reshape(total, modes * lanes)
    grad_x_cols = exchange(jnp.concatenate(
        [
            to_owners(t_dot(normed, x_grad).astype(BF), in_rows),
            to_owners(grad_dt.astype(BF), rank_rows),
        ],
        axis=1,
    ))
    grad_dt = returned(grad_x_cols[:, in_rows * modes :], rank_rows).astype(F32)
    grad_x_cols = returned(grad_x_cols[:, : in_rows * modes], in_rows)
    grad_gate_cols = returned(grad_gate_cols, in_rows)
    normed_grad = scatter(
        jnp.concatenate([x_grad, gate_grad], axis=1),
        jnp.concatenate([x_cols, gate_cols], axis=1), 1, [],
    )
    grad_in = jnp.concatenate([grad_x_cols, grad_gate_cols], axis=2).astype(F32)
    grad_gain = jnp.sum(grad_in * in_weight.astype(F32), axis=(1, 2)) / norm_gain.astype(F32)
    xm = mine.astype(F32)
    scale = lax.rsqrt(jnp.mean(xm * xm, axis=1, keepdims=True) + EPS)
    unit = xm * scale
    scaled = normed_grad * gain
    grad_hidden = cotangent[0].astype(F32) + scale * (
        scaled - unit * jnp.mean(scaled * unit, axis=1, keepdims=True)
    )
    return (
        output,
        grad_hidden[None],
        grad_gain,
        grad_in,
        settle(tap_grad[:4].T),
        settle(base_grad[0]),
        settle(grad_xproj.reshape(lanes, modes, -1)),
        grad_dt,
        settle(grad_bias[:modes].T),
        settle(grad_decay),
        settle(grad_skip[0]),
        settle(grad_out_weight),
    )


def solution(mesh):
    both = ("grp", "seq")
    full = mesh.shape["grp"] * mesh.shape["seq"] <= 32
    chan, held = (both, ()) if full else (("seq",), ("grp",))
    row = P(both)
    return jax.shard_map(
        functools.partial(on_device, chan, held),
        mesh=mesh,
        in_specs=(
            P("grp", "seq", None), P("grp", "seq"), P("grp"),
            row, row, row, row, row, row, row, row, row, row,
            P("grp", "seq", None),
        ),
        out_specs=(P("grp", "seq", None), P("grp", "seq", None)) + (row,) * 10,
        check_vma=False,
    )
```

```python
import functools
import math

import jax
import jax.numpy as jnp
import numpy as np
from jax import lax
from jax.experimental import pallas as pl
from jax.experimental.pallas import tpu as pltpu
from jax.sharding import PartitionSpec as P

EPS = 1e-05
BF = jnp.bfloat16
F32 = jnp.float32
LOG2E = math.log2(math.e)
RESET = 1e4
VMEM = 60 * 1024 * 1024


def dot(a, b, dims=((1,), (0,))):
    return lax.dot_general(a, b, (dims, ((), ())), preferred_element_type=F32)


def silu_slope(v):
    s = jax.nn.sigmoid(v)
    return s * (1.0 + v * (1.0 - s))


def after(x, other):
    return x + (other[(0,) * other.ndim] * 0).astype(x.dtype)


def pick(values, masks):
    count = masks.shape[1]
    width = values.shape[1] // count
    return sum(values[:, m * width : (m + 1) * width] * masks[:, m : m + 1] for m in range(count))


def spread(values, masks):
    return jnp.concatenate(
        [values * masks[:, m : m + 1].astype(values.dtype) for m in range(masks.shape[1])], axis=1
    )


def spread_lanes(source, widen, target):

    low = source[...].astype(BF)
    for c in range(0, target.shape[1], 256):
        target[:, c : c + 256] = dot(low, widen[:, c : c + 256])


def widening(columns, lanes):
    ones = np.zeros((2 * columns, columns * lanes), np.float32)
    for s in range(columns):
        ones[s, s * lanes : (s + 1) * lanes] = 1
        ones[columns + s, s * lanes : (s + 1) * lanes] = 1
    return jnp.asarray(ones, BF)


def dot_t(a, b):
    return dot(a, b, ((1,), (1,)))


def t_dot(a, b):
    return dot(a, b, ((0,), (0,)))


def softplus(x):
    return jnp.maximum(x, 0.0) + jnp.log1p(jnp.exp(-jnp.abs(x)))


def packed(values, width):
    count = 128 // width
    span = values.shape[0] // count
    return jnp.concatenate([values[q * span : (q + 1) * span, :] for q in range(count)], axis=1)


def unpacked(values, width):
    values = values.astype(F32)
    return jnp.concatenate(
        [values[:, q * width : (q + 1) * width] for q in range(128 // width)], axis=0
    )


def to_time_major(ref, values, row, count):
    ref[pl.ds(row, count, stride=8), :] = values


def lay_out(groups, length, states, first, starts, step, act, picked, extra, sf, du, bc, also):
    copies = 8 // groups
    position = first + lax.broadcasted_iota(jnp.int32, (length, 1), 0)
    lane = lax.broadcasted_iota(jnp.int32, (1, 4 * states), 1)
    owner = lane % states // (states // copies)
    for g in range(groups):
        begin = (position == 0) | (position == starts[g])
        fade_step = jnp.where(begin, RESET, step[g])
        drive = step[g] * act[g, 0]
        span = length * 2 * states // 128
        chosen = jnp.concatenate(
            [
                unpacked(picked[g, 0, length + n * span : length + (n + 1) * span, :], 2 * states)
                for n in range(2)
            ],
            axis=1,
        )
        for j in range(copies):
            to_time_major(sf, fade_step, j * groups + g, length)
            to_time_major(du, drive, j * groups + g, length)
            to_time_major(bc, jnp.where(owner == j, chosen, 0.0), j * groups + g, length)
            if also is not None:
                to_time_major(also, extra[g, 0], j * groups + g, length)


def pre_step(picked, mask, dt, bias):
    modes, lanes = bias.shape
    product = dot(picked[: mask.shape[0], :], dt[...])
    return sum(
        (product[:, m * lanes : (m + 1) * lanes] + bias[m : m + 1, :]) * mask[:, m : m + 1]
        for m in range(modes)
    )


def scan_kernel(
    groups, length, states, table, starts, act, picked, mask, rate, widen, dt, bias, skip, y, pre, prior, end, sf, du, bc, ys, state, ex,
):
    copies, count, lanes = 8 // groups, rate.shape[0] // 8, rate.shape[1]
    i = pl.program_id(0)

    @pl.when(i == 0)
    def _():
        state[...] = jnp.zeros_like(state)

    steps = []
    for g in range(groups):
        raw = pre_step(picked[g, 0], mask[g, 0], dt, bias)
        pre[g, 0] = raw
        steps.append(softplus(raw))
    lay_out(groups, length, states, i * length, starts, steps, act, picked, None, sf, du, bc, None)
    spread_lanes(bc, widen, ex)
    rates = [rate[s * 8 : s * 8 + 8, :] for s in range(count)]

    def one(p, h):
        row = pl.ds(pl.multiple_of(p * 8, 8), 8)
        step_p, drive_p = sf[row, :], du[row, :]
        read = None
        out = []
        for s in range(count):
            prior[pl.ds(pl.multiple_of((p * count + s) * 8, 8), 8), :] = h[s]
            now = jnp.exp2(step_p * rates[s]) * h[s] + drive_p * ex[row, s * lanes : (s + 1) * lanes]
            term = now * ex[row, (count + s) * lanes : (count + s + 1) * lanes]
            read = term if read is None else read + term
            out.append(now)
        ys[row, :] = read
        return tuple(out)

    first = tuple(state[s * 8 : s * 8 + 8, :] for s in range(count))
    last = lax.fori_loop(0, length, one, first, unroll=4)
    for s in range(count):
        state[s * 8 : s * 8 + 8, :] = last[s]
    end[...] = state[...]
    for g in range(groups):
        total = sum(ys[pl.ds(j * groups + g, length, stride=8), :] for j in range(copies))
        total = total + skip[...] * act[g, 0]
        y[g, 0] = total


def back_kernel(
    groups, length, states, top, blocks, table, starts, act, picked, mask, pre, read_grad, prior,
    begun, rate, widen, dt, bias, skip, pick_b, pick_c, *refs,
):
    act_grad, picked_grad, left, rate_grad, dt_grad, bias_grad, skip_grad = refs[-20:-13]
    sf, du, gy, bc, wt, ft, pb, pc, res, carry, held, ex, step = refs[-13:]
    copies, count = 8 // groups, rate.shape[0] // 8
    lanes = rate.shape[1]
    modes = bias.shape[0]
    rank = dt.shape[0]
    i = pl.program_id(0)

    @pl.when(i == 0)
    def _():
        carry[...] = begun[0 : count * 8, :]
        held[...] = begun[count * 8 :, :]
        rate_grad[...] = jnp.zeros_like(rate_grad)
        dt_grad[...] = jnp.zeros_like(dt_grad)
        bias_grad[...] = jnp.zeros_like(bias_grad)
        skip_grad[...] = jnp.zeros_like(skip_grad)

    for g in range(groups):
        step[g] = softplus(pre[g, 0])
    lay_out(
        groups, length, states, (top - i) * length, starts, step, act, picked, read_grad, sf, du, bc, gy
    )
    spread_lanes(bc, widen, ex)
    rates = [rate[s * 8 : s * 8 + 8, :] for s in range(count)]

    def one(k, loop):
        p = length - 1 - k
        row = pl.ds(pl.multiple_of(p * 8, 8), 8)
        step_p, drive_p, grad_p = sf[row, :], du[row, :], gy[row, :]
        carried, state, total = loop
        weight_sum, fade_sum = None, None
        out_c, out_h, out_r = [], [], []
        for s in range(count):
            before = prior[pl.ds(pl.multiple_of((p * count + s) * 8, 8), 8), :]
            cols = slice(s * lanes, (s + 1) * lanes)
            e = grad_p * ex[row, (count + s) * lanes : (count + s + 1) * lanes] + carried[s]
            pc[row, cols] = grad_p * state[s]
            pb[row, cols] = e * drive_p
            term = e * ex[row, cols]
            passed = e * jnp.exp2(step_p * rates[s])
            decay = passed * before
            fade_term = decay * rates[s]
            weight_sum = term if weight_sum is None else weight_sum + term
            fade_sum = fade_term if fade_sum is None else fade_sum + fade_term
            out_c.append(passed)
            out_h.append(before)
            out_r.append(total[s] + decay * step_p)
        wt[row, :] = weight_sum
        ft[row, :] = fade_sum
        return tuple(out_c), tuple(out_h), tuple(out_r)

    def parts(ref):
        return tuple(ref[s * 8 : s * 8 + 8, :] for s in range(count))

    c, h, r = lax.fori_loop(
        0, length, one, (parts(carry), parts(held), parts(rate_grad)), unroll=2
    )
    for s in range(count):
        carry[s * 8 : s * 8 + 8, :] = c[s]
        held[s * 8 : s * 8 + 8, :] = h[s]
        rate_grad[s * 8 : s * 8 + 8, :] = r[s]
    left[0 : count * 8, :] = carry[...]
    left[count * 8 :, :] = held[...]
    res[...] = dot(pb[...].astype(BF), pick_b[...]) + dot(pc[...].astype(BF), pick_c[...])
    lane = lax.broadcasted_iota(jnp.int32, (1, 128), 1)
    owner = lane % states // count
    for g in range(groups):
        rows = [pl.ds(j * groups + g, length, stride=8) for j in range(copies)]
        weighted = sum(wt[row, :] for row in rows)
        faded = sum(ft[row, :] for row in rows) * (1.0 / LOG2E)
        chosen = sum(jnp.where(owner == j, res[rows[j], :], 0.0) for j in range(copies))
        grad_y, u = read_grad[g, 0], act[g, 0]
        act_grad[g, 0] = skip[...] * grad_y + step[g] * weighted
        pre_grad = (u * weighted + faded) * jax.nn.sigmoid(pre[g, 0])
        skip_grad[...] += jnp.sum(grad_y * u, axis=0, keepdims=True)
        rank_grad = None
        for m in range(modes):
            own = pre_grad * mask[g, 0, :, m : m + 1]
            bias_grad[m : m + 1, :] += jnp.sum(own, axis=0, keepdims=True)
            own = own.astype(BF)
            cols = slice(m * lanes, (m + 1) * lanes)
            term = dot_t(own, dt[:, cols])
            rank_grad = term if rank_grad is None else rank_grad + term
            dt_grad[:, cols] += t_dot(picked[g, 0, 0:length, :], own)
        picked_grad[g, 0, 0:length, :] = rank_grad
        picked_grad[g, 0, length:, :] = packed(chosen[:, 0 : 2 * states], 2 * states)


def spread_lanes(source, widen, target):

    @pl.loop(0, source.shape[0] // 128)
    def _(n):
        row = pl.ds(pl.multiple_of(n * 128, 128), 128)
        target[row, :] = dot(source[row, :].astype(BF), widen[...])


def widening(states, count, lanes):
    ones = np.zeros((2, 2, states, 2 * count * lanes), np.float32)
    for kind in range(2):
        for s in range(states):
            block = kind * count + s % count
            ones[:, kind, s, block * lanes : (block + 1) * lanes] = 1
    return jnp.asarray(ones.reshape(4 * states, -1), BF)


def picking(states, count, lanes):
    ones = np.zeros((2, count * lanes, 128), np.float32)
    for kind in range(2):
        for s in range(states):
            at = s % count
            ones[kind, at * lanes : (at + 1) * lanes, kind * states + s] = 1
    return jnp.asarray(ones[0], BF), jnp.asarray(ones[1], BF)


def conv_kernel(groups, length, table, starts, x, mask, taps, base, xproj, v, act, part, tail, ext):
    i = pl.program_id(0)

    @pl.when(i == 0)
    def _():
        tail[...] = jnp.zeros_like(tail)

    modes = mask.shape[3]
    width = xproj.shape[1] // modes
    position = i * length + lax.broadcasted_iota(jnp.int32, (length, 1), 0)
    for g in range(groups):
        begin = jnp.where(position >= starts[g], starts[g], 0)
        ext[0:8, :] = tail[g]
        ext[8 : 8 + length, :] = x[g, 0]
        tail[g] = x[g, 0, length - 8 : length, :]
        total = base[...]
        for k in range(4):
            valid = (position - 3 + k >= begin).astype(F32)
            total = total + taps[k : k + 1, :] * ext[5 + k : 5 + k + length, :] * valid
        v[g, 0] = total
        active = total * jax.nn.sigmoid(total)
        act[g, 0] = active
        product = dot(active.astype(BF), xproj[...])
        chosen = sum(
            product[:, m * width : (m + 1) * width] * mask[g, 0, :, m : m + 1] for m in range(modes)
        )
        part[g, 0, 0:length, :] = chosen[:, 0:128]
        part[g, 0, length:, :] = packed(chosen[:, 128:], width - 128)


def conv_back_kernel(
    groups, length, blocks, table, starts, grad, sel_grad, v, act, x, mask, taps, xproj, *refs,
):
    x_grad, tap_grad, base_grad, weight_grad, head, ext = refs[-6:]
    i = pl.program_id(0)

    @pl.when(i == 0)
    def _():
        head[...] = jnp.zeros_like(head)
        weight_grad[...] = jnp.zeros_like(weight_grad)
        tap_grad[...] = jnp.zeros_like(tap_grad)
        base_grad[...] = jnp.zeros_like(base_grad)

    modes = mask.shape[3]
    width = xproj.shape[1] // modes
    position = (blocks - 1 - i) * length + lax.broadcasted_iota(jnp.int32, (length, 1), 0)
    for g in range(groups):
        chosen = jnp.concatenate(
            [
                sel_grad[g, 0, 0:length, :].astype(F32),
                unpacked(sel_grad[g, 0, length:, :], width - 128),
            ],
            axis=1,
        ).astype(BF)
        masked = [chosen * mask[g, 0, :, m : m + 1].astype(BF) for m in range(modes)]
        act_grad = grad[g, 0]
        low = act[g, 0].astype(BF)
        for m in range(modes):
            cols = slice(m * width, (m + 1) * width)
            act_grad = act_grad + dot_t(masked[m], xproj[:, cols])
            weight_grad[:, cols] += t_dot(low, masked[m])
        v_grad = act_grad * silu_slope(v[g, 0])
        ext[0:length, :] = v_grad
        ext[length : length + 8, :] = head[g]
        head[g] = v_grad[0:8, :]
        base_grad[...] += jnp.sum(v_grad, axis=0, keepdims=True)
        total = None
        for k in range(4):
            crosses = (position < starts[g]) & (position + 3 - k >= starts[g])
            shifted = jnp.where(crosses, 0.0, ext[3 - k : 3 - k + length, :])
            term = taps[k : k + 1, :] * shifted
            total = term if total is None else total + term
            tap_grad[k : k + 1, :] += jnp.sum(x[g, 0] * shifted, axis=0, keepdims=True)
        total = total.astype(BF)
        lanes = total.shape[1]
        for m in range(modes):
            x_grad[g, 0, :, m * lanes : (m + 1) * lanes] = total * mask[g, 0, :, m : m + 1].astype(BF)


def inproj_kernel(lots, *refs):
    pieces = refs[:-9]
    gain, weight, normed, proj, mask, notes, cols, whole, arrived = refs[-9:]
    modes = mask.shape[2]
    lanes = weight.shape[2]
    count = len(pieces) // lots
    rows = mask.shape[1] // count
    part = cols.shape[0] // weight.shape[0]
    i = pl.program_id(0)

    def copies(lot):
        return [
            pltpu.make_async_copy(
                pieces[lot * count + n], whole.at[lot % 2, n], arrived.at[lot % 2, n]
            )
            for n in range(count)
        ]

    @pl.when(i == 0)
    def _():
        for copy in copies(0):
            copy.start()
        for n in range(weight.shape[0]):
            for m in range(modes):
                cols[n * part : (n + 1) * part, m * lanes : (m + 1) * lanes] = weight[
                    n, m * part : (m + 1) * part, :
                ]

    for lot in range(lots):

        @pl.when(i == lot)
        def _(lot=lot):
            if lot + 1 < lots:
                for copy in copies(lot + 1):
                    copy.start()
            for copy in copies(lot):
                copy.wait()

    slot = lax.rem(i, 2)
    square = (rows, rows)
    same = lax.broadcasted_iota(jnp.int32, square, 0) == lax.broadcasted_iota(jnp.int32, square, 1)
    kind = lax.broadcasted_iota(jnp.int32, (1, modes), 1).astype(F32)
    for n in range(count):
        span = slice(n * rows, (n + 1) * rows)
        x = whole[slot, n, 0:rows, :].astype(F32)
        scale = lax.rsqrt(jnp.mean(x * x, axis=1, keepdims=True) + EPS)
        normed[0, span, :] = (x * scale * gain[...]).astype(BF)
        note = whole[slot, n, rows : rows + 16, 0:rows].astype(F32)
        column = jnp.sum(jnp.where(same, note[0:1, :], 0.0), axis=1, keepdims=True)
        mask[0, span, :] = (column == kind).astype(F32)
        if n == 0:
            notes[0] = note[0:8, :]
    product = dot(normed[0], cols[...])
    proj[0] = sum(
        product[:, m * lanes : (m + 1) * lanes] * mask[0, :, m : m + 1] for m in range(modes)
    )


def inproj(lots, rows, modes, pieces, gain, weight):
    tall, width = pieces[0].shape
    lanes = weight.shape[2]
    count = len(pieces) // lots
    size = count * rows
    block = lambda *shape: pl.BlockSpec((1,) + shape, lambda i: (i, 0, 0))
    shapes = [
        jax.ShapeDtypeStruct((lots, size, width), BF),
        jax.ShapeDtypeStruct((lots, size, lanes), F32),
        jax.ShapeDtypeStruct((lots, size, modes), F32),
        jax.ShapeDtypeStruct((lots, 8, rows), F32),
        jax.ShapeDtypeStruct((width, modes * lanes), BF),
    ]
    return pl.pallas_call(
        functools.partial(inproj_kernel, lots),
        grid=(lots,),
        in_specs=[pl.BlockSpec(memory_space=pl.ANY)] * len(pieces) + [flat(gain), flat(weight)],
        out_specs=[block(*a.shape[1:]) for a in shapes[:4]] + [flat(shapes[4])],
        out_shape=shapes,
        scratch_shapes=[
            pltpu.VMEM((2, count, tall, width), BF),
            pltpu.SemaphoreType.DMA((2, count)),
        ],
        compiler_params=pltpu.CompilerParams(vmem_limit_bytes=VMEM),
        cost_estimate=pl.CostEstimate(
            flops=2 * lots * size * width * modes * lanes,
            bytes_accessed=6 * lots * size * width,
            transcendentals=0,
        ),
    )(*pieces, gain, weight)


def conv(table, starts, x, mask, taps, base, xproj):
    groups, blocks, length, lanes = x.shape
    modes = mask.shape[3]
    width = xproj.shape[1] // modes
    at = lambda i, t, b: (0, t[i], 0, 0)
    flat = lambda i, t, b: (0, 0)
    block = pl.BlockSpec((groups, 1, length, lanes), at)
    return pl.pallas_call(
        functools.partial(conv_kernel, groups, length),
        grid_spec=pltpu.PrefetchScalarGridSpec(
            num_scalar_prefetch=2,
            grid=(blocks,),
            in_specs=[
                block,
                pl.BlockSpec((groups, 1, length, modes), at),
                pl.BlockSpec(taps.shape, flat),
                pl.BlockSpec(base.shape, flat),
                pl.BlockSpec(xproj.shape, flat),
            ],
            out_specs=[block, block, pl.BlockSpec((groups, 1, length * width // 128, 128), at)],
            scratch_shapes=[
                pltpu.VMEM((groups, 8, lanes), F32),
                pltpu.VMEM((length + 8, lanes), F32),
            ],
        ),
        out_shape=[
            jax.ShapeDtypeStruct(x.shape, F32),
            jax.ShapeDtypeStruct(x.shape, F32),
            jax.ShapeDtypeStruct((groups, blocks, length * width // 128, 128), F32),
        ],
        compiler_params=pltpu.CompilerParams(vmem_limit_bytes=VMEM),
    )(table, starts, x, mask, taps, base, xproj)


def conv_back(table, starts, grad, sel_grad, v, act, x, mask, taps, xproj, before):
    groups, blocks, length, lanes = x.shape
    modes = mask.shape[3]
    width = xproj.shape[1] // modes
    at = lambda i, t, b: (0, t[blocks - 1 - i], 0, 0)
    flat = lambda i, t, b: (0, 0)
    block = pl.BlockSpec((groups, 1, length, lanes), at)
    return pl.pallas_call(
        functools.partial(conv_back_kernel, groups, length, blocks),
        grid_spec=pltpu.PrefetchScalarGridSpec(
            num_scalar_prefetch=2,
            grid=(blocks,),
            in_specs=[
                block,
                pl.BlockSpec((groups, 1, length * width // 128, 128), at),
                block,
                block,
                block,
                pl.BlockSpec((groups, 1, length, modes), at),
                pl.BlockSpec(taps.shape, flat),
                pl.BlockSpec(xproj.shape, flat),
            ]
            + [pl.BlockSpec(memory_space=pl.ANY)] * len(before),
            out_specs=[
                pl.BlockSpec((groups, 1, length, modes * lanes), at),
                pl.BlockSpec((8, lanes), flat),
                pl.BlockSpec((1, lanes), flat),
                pl.BlockSpec(xproj.shape, flat),
            ],
            scratch_shapes=[
                pltpu.VMEM((groups, 8, lanes), F32),
                pltpu.VMEM((length + 8, lanes), F32),
            ],
        ),
        out_shape=[
            jax.ShapeDtypeStruct((groups, blocks, length, modes * lanes), BF),
            jax.ShapeDtypeStruct((8, lanes), F32),
            jax.ShapeDtypeStruct((1, lanes), F32),
            jax.ShapeDtypeStruct(xproj.shape, F32),
        ],
        compiler_params=pltpu.CompilerParams(vmem_limit_bytes=VMEM),
    )(table, starts, grad, sel_grad, v, act, x, mask, taps, xproj, *before)


def flat(array):
    return pl.BlockSpec(array.shape, lambda i, *_: (0,) * array.ndim)


def scan(table, starts, act, picked, mask, rate, dt, bias, skip, states):
    groups, blocks, length, lanes = act.shape
    total = blocks * length
    count = rate.shape[0] // 8
    at = lambda i, t, b: (0, t[i], 0, 0)
    block = lambda a: pl.BlockSpec((groups, 1) + a.shape[2:], at)
    widen = widening(states, count, lanes)
    tall = pltpu.VMEM((length * 8, lanes), F32)
    like = jax.ShapeDtypeStruct(act.shape, F32)
    return pl.pallas_call(
        functools.partial(scan_kernel, groups, length, states),
        grid_spec=pltpu.PrefetchScalarGridSpec(
            num_scalar_prefetch=2,
            grid=(blocks,),
            in_specs=[block(a) for a in (act, picked, mask)]
            + [flat(a) for a in (rate, widen, dt, bias, skip)],
            out_specs=[
                block(act),
                block(act),
                pl.BlockSpec((length * count * 8, lanes), lambda i, t, b: (i, 0)),
                flat(rate),
            ],
            scratch_shapes=[
                tall,
                tall,
                pltpu.VMEM((length * 8, 4 * states), F32),
                tall,
                pltpu.VMEM((count * 8, lanes), F32),
                pltpu.VMEM((length * 8, 2 * count * lanes), F32),
            ],
        ),
        out_shape=[
            like,
            like,
            jax.ShapeDtypeStruct((total * count * 8, lanes), F32),
            jax.ShapeDtypeStruct((count * 8, lanes), F32),
        ],
        compiler_params=pltpu.CompilerParams(vmem_limit_bytes=VMEM),
        cost_estimate=pl.CostEstimate(flops=10**10, bytes_accessed=10**8, transcendentals=0),
    )(table, starts, act, picked, mask, rate, widen, dt, bias, skip)


def gate_kernel(lots_at, spans_at, normed, weight, mask, read, gate, gated, spread_gated):
    modes = mask.shape[2]
    lanes = read.shape[2]
    count = spans_at.shape[0]
    rows = read.shape[1] // count
    product = dot(normed[0], weight[...])
    masks = [mask[0, :, m : m + 1] for m in range(modes)]
    opened = sum(product[:, m * lanes : (m + 1) * lanes] * masks[m] for m in range(modes))
    gate[0] = opened
    low = (read[0] * (opened * jax.nn.sigmoid(opened))).astype(BF)
    gated[0] = low
    for m in range(modes):
        own = low * masks[m].astype(BF)
        for n in range(count):
            place = pl.ds(pl.multiple_of(spans_at[n] * rows, rows), rows)
            spread_gated[0, place, m * lanes : (m + 1) * lanes] = own[n * rows : (n + 1) * rows, :]


def gate_part(lots_at, spans_at, normed, weight, mask, read):
    lots, size, width = normed.shape
    lanes = read.shape[2]
    wide = weight.shape[1]
    block = lambda w: pl.BlockSpec((1, size, w), lambda i, a, b: (i, 0, 0))
    return pl.pallas_call(
        gate_kernel,
        grid_spec=pltpu.PrefetchScalarGridSpec(
            num_scalar_prefetch=2,
            grid=(lots,),
            in_specs=[block(width), flat(weight), block(mask.shape[2]), block(lanes)],
            out_specs=[
                block(lanes), block(lanes), pl.BlockSpec((1, size, wide), lambda i, a, b: (a[i], 0, 0))
            ],
        ),
        out_shape=[
            jax.ShapeDtypeStruct(read.shape, F32),
            jax.ShapeDtypeStruct(read.shape, BF),
            jax.ShapeDtypeStruct((lots, size, wide), BF),
        ],
        compiler_params=pltpu.CompilerParams(vmem_limit_bytes=VMEM),
        cost_estimate=pl.CostEstimate(
            flops=2 * lots * size * width * wide, bytes_accessed=3 * lots * size * width, transcendentals=0
        ),
    )(lots_at, spans_at, normed, weight, mask, read)


def scan_back(
    first, last, table, starts, act, picked, mask, pre, read_grad, prior, begun, rate, dt, bias,
    skip, states, so_far, before,
):
    groups, blocks, length, lanes = act.shape
    count = rate.shape[0] // 8
    rank = dt.shape[0]
    modes = bias.shape[0]
    at = lambda i, t, b: (0, t[last - 1 - i], 0, 0)
    block = lambda a: pl.BlockSpec((groups, 1) + a.shape[2:], at)
    widen = widening(states, count, lanes)
    pick_b, pick_c = picking(states, count, lanes)
    tall = pltpu.VMEM((length * 8, lanes), F32)
    wide = pltpu.VMEM((length * 8, count * lanes), F32)
    tables = pltpu.VMEM((count * 8, lanes), F32)
    shapes = [
        jax.ShapeDtypeStruct(act.shape, F32),
        jax.ShapeDtypeStruct((groups, blocks, length + length * 2 * states // 128, 128), F32),
        jax.ShapeDtypeStruct((2 * count * 8, lanes), F32),
        jax.ShapeDtypeStruct((count * 8, lanes), F32),
        jax.ShapeDtypeStruct((rank, modes * lanes), F32),
        jax.ShapeDtypeStruct((8, lanes), F32),
        jax.ShapeDtypeStruct((1, lanes), F32),
    ]
    loaded = (begun, rate, widen, dt, bias, skip, pick_b, pick_c)
    extra = tuple(so_far or ()) + tuple(before)
    at_input = 2 + 6 + len(loaded)
    return pl.pallas_call(
        functools.partial(back_kernel, groups, length, states, last - 1, blocks),
        grid_spec=pltpu.PrefetchScalarGridSpec(
            num_scalar_prefetch=2,
            grid=(last - first,),
            in_specs=[block(a) for a in (act, picked, mask, pre, read_grad)]
            + [pl.BlockSpec((length * count * 8, lanes), lambda i, t, b: (last - 1 - i, 0))]
            + [flat(a) for a in loaded]
            + [pl.BlockSpec(memory_space=pl.ANY)] * len(extra),
            out_specs=[block(shapes[0]), block(shapes[1])] + [flat(a) for a in shapes[2:]],
            scratch_shapes=[
                tall, tall, tall, pltpu.VMEM((length * 8, 4 * states), F32), tall, tall, wide, wide,
                pltpu.VMEM((length * 8, 128), F32),
                tables,
                tables,
                pltpu.VMEM((length * 8, 2 * count * lanes), F32),
                pltpu.VMEM((groups, length, lanes), F32),
            ],
        ),
        out_shape=shapes,
        input_output_aliases={at_input: 0, at_input + 1: 1} if so_far else {},
        compiler_params=pltpu.CompilerParams(vmem_limit_bytes=VMEM),
        cost_estimate=pl.CostEstimate(
            flops=10**10, bytes_accessed=25 * 10**6 * (last - first), transcendentals=0
        ),
    )(table, starts, act, picked, mask, pre, read_grad, prior, *loaded, *extra)


def cot_kernel(
    lots_at, spans_at, cots, out_rows, mask, gated, read, gate, read_grad, gate_grad, weight_grad, whole
):
    count = spans_at.shape[0]
    rows = whole.shape[0] // count

    @pl.when(pl.program_id(0) == 0)
    def _():
        weight_grad[...] = jnp.zeros_like(weight_grad)

    for n in range(count):
        whole[n * rows : (n + 1) * rows, :] = cots[
            0, pl.ds(pl.multiple_of(spans_at[n] * rows, rows), rows), :
        ]
    product = dot_t(whole[...], out_rows[...])
    modes = mask.shape[2]
    lanes = gated.shape[2]
    masks = [mask[0, :, m : m + 1] for m in range(modes)]
    grad = sum(product[:, m * lanes : (m + 1) * lanes] * masks[m] for m in range(modes))
    opened = gate[0]
    read_grad[0] = grad * (opened * jax.nn.sigmoid(opened))
    gate_low = (grad * read[0] * silu_slope(opened)).astype(BF)
    for m in range(modes):
        own = masks[m].astype(BF)
        cols = slice(m * lanes, (m + 1) * lanes)
        gate_grad[0, :, cols] = gate_low * own
        weight_grad[cols, :] += t_dot(gated[0] * own, whole[...])


def cot_part(lots_at, spans_at, cots, out_rows, mask, gated, read, gate):
    lots, size, width = cots.shape
    lanes = gated.shape[2]
    wide = out_rows.shape[0]
    block = lambda w: pl.BlockSpec((1, size, w), lambda i, a, b: (i, 0, 0))
    return pl.pallas_call(
        cot_kernel,
        grid_spec=pltpu.PrefetchScalarGridSpec(
            num_scalar_prefetch=2,
            grid=(lots,),
            in_specs=[pl.BlockSpec((1, size, width), lambda i, a, b: (a[i], 0, 0)), flat(out_rows)]
            + [block(a.shape[2]) for a in (mask, gated, read, gate)],
            out_specs=[block(lanes), block(wide), flat(out_rows)],
            scratch_shapes=[pltpu.VMEM((size, width), BF)],
        ),
        out_shape=[
            jax.ShapeDtypeStruct((lots, size, lanes), F32),
            jax.ShapeDtypeStruct((lots, size, wide), BF),
            jax.ShapeDtypeStruct(out_rows.shape, F32),
        ],
        compiler_params=pltpu.CompilerParams(vmem_limit_bytes=VMEM),
        cost_estimate=pl.CostEstimate(
            flops=4 * lots * size * width * wide, bytes_accessed=3 * lots * size * width, transcendentals=0
        ),
    )(lots_at, spans_at, cots, out_rows, mask, gated, read, gate)


class Dim:

    def __init__(self, axis, stride, size, length):
        self.axis, self.stride, self.size, self.length = axis, stride, size, length

    def here(self):
        return lax.axis_index(self.axis) // self.stride % self.size

    def fetch(self, x, by):
        pairs = []
        for i in range(self.length):
            c = i // self.stride % self.size
            pairs.append((i + ((c + by) % self.size - c) * self.stride, i))
        return lax.ppermute(x, self.axis, pairs)


def dims_of(chan):
    dims = []
    for axis in chan:
        length = lax.axis_size(axis)
        sizes = []
        rest = length
        if axis == "seq":
            rest //= 2
        radix = 4 if axis == "seq" else 2
        while rest > 1:
            sizes.insert(0, min(radix, rest))
            rest //= sizes[0]
        if axis == "seq":
            sizes.append(2)
        stride = length
        for size in sizes:
            stride //= size
            dims.append(Dim(axis, stride, size, length))
    return dims


def fence(*arrays):
    return list(pl.pallas_call(
        lambda *refs: None,
        in_specs=[pl.BlockSpec(memory_space=pl.ANY)] * len(arrays),
        out_specs=[pl.BlockSpec(memory_space=pl.ANY)] * len(arrays),
        out_shape=[jax.ShapeDtypeStruct(x.shape, x.dtype) for x in arrays],
        input_output_aliases={n: n for n in range(len(arrays))},
    )(*arrays))


def gather_pieces(dims, x):
    others, ring, core = dims[:-2], dims[-2], dims[-1]
    got = {}
    first = x
    for k in range(ring.size):
        if k:
            first = ring.fetch(first, 1)
        order = list(range(len(others)))
        if k % 2:
            order.reverse()
        held = {(0,) * len(others): first}
        for d in order:
            for at, block in list(held.items()):
                for r in range(1, others[d].size):
                    block = others[d].fetch(block, 1)
                    held[at[:d] + (r,) + at[d + 1 :]] = block
        for at, block in held.items():
            got[at + (k, 0)] = block
            got[at + (k, 1)] = core.fetch(block, 1)
    return [got[at] for at in sorted(got)]


def pairs_of(dims):
    return [d.size for d in dims[:-2]] == [2, 2]


def gather_stage(dims, x, d):
    got = [x] + [dims[d].fetch(x, r) for r in range(1, dims[d].size)]
    return jnp.concatenate(got, axis=d)


def gather_small(dims, x):
    x = x.reshape((1,) * len(dims) + x.shape)
    x = gather_stage(dims, x, len(dims) - 2)
    if pairs_of(dims):
        halves = jnp.split(x, 2, axis=len(dims))
        halves = [gather_stage(dims, h, n) for n, h in enumerate(halves)]
        halves = [gather_stage(dims, h, 1 - n) for n, h in enumerate(halves)]
        x = jnp.concatenate(halves, axis=len(dims))
    else:
        for d in range(len(dims) - 2):
            x = gather_stage(dims, x, d)
    return gather_stage(dims, x, len(dims) - 1)


def reduce_stage(dims, x, d, kind):
    block = [lax.slice_in_dim(x, r, r + 1, axis=d) for r in range(dims[d].size)]
    return add_up(
        [block[0]] + [dims[d].fetch(block[r].astype(kind), -r) for r in range(1, len(block))]
    )


def reduce_small(dims, x):
    x = reduce_stage(dims, x, len(dims) - 1, F32)
    if pairs_of(dims):
        halves = jnp.split(x, 2, axis=len(dims))
        halves = [reduce_stage(dims, h, n, BF) for n, h in enumerate(halves)]
        halves = [reduce_stage(dims, h, 1 - n, F32) for n, h in enumerate(halves)]
        x = jnp.concatenate(halves, axis=len(dims))
    else:
        for d in range(len(dims) - 2):
            x = reduce_stage(dims, x, d, F32 if d else BF)
    x = reduce_stage(dims, x, len(dims) - 2, F32)
    return x.reshape(x.shape[len(dims) :])


def add_up(parts):
    return sum(p.astype(F32) for p in parts)


def reduce_parts(dims, x, turn, stages):
    order = list(range(len(dims) - 2))
    if turn % 2:
        order.reverse()
    order = [len(dims) - 1] + order + [len(dims) - 2]
    for n, d in enumerate(order):
        size = dims[d].size
        block = [lax.slice_in_dim(x, r, r + 1, axis=d) for r in range(size)]
        if size == 2:
            x = add_up([block[0]] + [dims[d].fetch(block[r], -r) for r in range(1, size)])
        else:
            moving = block[size - 1]
            for r in range(size - 2, -1, -1):
                x = add_up([block[r], dims[d].fetch(moving, -1)])
                moving = x.astype(BF)
        if n < len(order) - 1:
            x = x.astype(BF)
            stages.append((n, x))
    return x.reshape(x.shape[len(dims) :])


def on_device(
    chan, held,
    hidden, modality, starts, norm_gain, in_weight, conv_weight, conv_bias, xproj_weight,
    dtproj_weight, step_bias, decay_log, skip_weight, out_weight, cotangent,
):
    def collect(x):
        return lax.all_gather(x, held, axis=0, tiled=True) if held else x

    def exchange(x):
        return lax.all_to_all(x, chan, 0, 0, tiled=True)

    def settle(x):
        return lax.psum_scatter(x, held, scatter_dimension=0, tiled=True) if held else x

    dims = dims_of(chan)
    sizes = tuple(d.size for d in dims)
    parts = math.prod(sizes)
    lots = math.prod(lax.axis_size(a) for a in held) if held else 1
    groups = parts // lax.axis_size("seq")
    rows, width = hidden.shape[1:]
    own = conv_weight.shape[0]
    lanes = own * lots
    rank_rows = dtproj_weight.shape[0]
    rank = rank_rows * parts * lots
    modes = in_weight.shape[1]
    states = decay_log.shape[1]
    mine = hidden[0]
    cot = cotangent[0]

    def shards(w):
        w = w.reshape(w.shape[0], modes, lots, parts, own)
        return jnp.moveaxis(w, 3, 0).reshape(parts, w.shape[0], modes, lanes)

    def to_owners(g, out_rows):
        return settle(g).reshape(parts, out_rows * modes, lanes)

    def returned(g, out_rows):
        g = g.reshape(parts, out_rows, modes, lots, own)
        return jnp.moveaxis(g, 0, 3).reshape(out_rows, modes, lots * parts * own)

    inner = lanes * parts
    blocks = parts // groups
    note = jnp.pad(jnp.stack([starts[0] >> 6, starts[0] & 63])[None], ((0, 0), (0, rows - 2)))
    note = jnp.concatenate([modality, note], axis=0).astype(BF)
    note = jnp.pad(note, ((0, 14), (0, width - rows)))
    pieces = gather_pieces(dims, jnp.concatenate([mine, note], axis=0))
    room = -norm_gain.shape[0] % lanes
    notes = jnp.broadcast_to(jnp.pad(norm_gain, (0, room)), (parts, norm_gain.shape[0] + room))
    moved = collect(exchange(jnp.concatenate(
        [
            jnp.swapaxes(shards(in_weight[:, :, :inner]), 1, 2).reshape(parts, -1, lanes),
            shards(dtproj_weight).reshape(parts, -1, lanes),
            notes.reshape(parts, -1, lanes),
        ],
        axis=1,
    )))
    cut = in_weight.shape[0] * modes
    further = cut + rank_rows * modes
    dt_cols = moved[:, cut:further].reshape(rank, modes * lanes)
    gain = moved[:, further:].reshape(parts * lots, -1)[:, : norm_gain.shape[0]]
    gain = gain.reshape(1, width).astype(F32)
    conv_weight, conv_bias, xproj_weight, step_bias, decay_log, skip_weight, out_weight = (
        collect(w)
        for w in (conv_weight, conv_bias, xproj_weight, step_bias, decay_log, skip_weight, out_weight)
    )
    taps = conv_weight.astype(F32).T
    bias = step_bias.astype(F32).T
    skip = skip_weight.astype(F32)[None]
    xproj = xproj_weight.reshape(lanes, -1)
    out_rows = jnp.moveaxis(out_weight, 1, 0).reshape(modes * lanes, width)
    total = parts * rows
    copies = 8 // groups
    count = states // copies
    rate = -jnp.exp(decay_log.astype(F32))
    rates = jnp.moveaxis(rate.T.reshape(copies, count, lanes), 0, 1)
    rates = jnp.repeat(rates.reshape(count * copies, 1, lanes), groups, axis=1).reshape(-1, lanes)
    rates = rates * LOG2E
    order = jnp.zeros((), jnp.int32)
    spans = jnp.arange(blocks, dtype=jnp.int32)
    stride = blocks
    for d in dims:
        if d.axis == "seq":
            stride //= d.size
            order = order * d.size + (spans // stride % d.size - d.here()) % d.size
    table = order

    def placed(some):
        at = jnp.zeros((), jnp.int32)
        stride = math.prod(d.size for d in some)
        names = jnp.arange(stride, dtype=jnp.int32)
        for d in some:
            stride //= d.size
            at = at * d.size + (names // stride % d.size + d.here()) % d.size
        return at.reshape(-1)


    step_pieces = sizes[-1] * sizes[-2]
    lots_in = parts // step_pieces
    normed, conv_in, in_masks, notes, x_cols = inproj(lots_in, rows, modes, pieces, gain, moved)
    masks = in_masks.reshape(groups, blocks, rows, modes)
    notes = notes.reshape(groups, -1, 8, rows)[:, 0, 1].astype(jnp.int32)
    begins = notes[:, 0] * 64 + notes[:, 1]
    cots = lax.all_gather(after(cot, conv_in), chan, axis=0, tiled=True)
    normed = normed.reshape(total, width)
    grouped = (groups, blocks, rows, lanes)
    pre_act, act, partial = conv(
        table, begins, conv_in.reshape(grouped), masks, taps, conv_bias.astype(F32)[None], xproj
    )
    picked = reduce_small(dims, partial.reshape(sizes + (-1, 128)))
    low = picked.astype(BF)
    rest = (picked[rows:] - low[rows:].astype(F32)).astype(BF)
    picked = gather_small(dims, jnp.concatenate([low, rest], axis=0))
    picked = picked.reshape(groups, blocks, -1, 128)
    gate_cols = collect(exchange(shards(after(in_weight[:, :, inner:], picked))).reshape(
        -1, modes, lanes
    )).reshape(width, modes * lanes)
    read, pre, prior, end = scan(
        table, begins, act, picked, masks, rates, dt_cols, bias, skip, states
    )
    lot = (lots_in, step_pieces * rows, -1)
    lots_at, spans_at = placed(dims[:-2]), placed(dims[-2:])
    gate_in, gated, spread_gated = gate_part(
        lots_at, spans_at, normed.reshape(lot), gate_cols, in_masks, read.reshape(lot)
    )

    def scatter(x, weight, dim, stages):
        got = []
        chunk = width // 2
        for n in range(2):
            w = lax.slice_in_dim(weight, n * chunk, (n + 1) * chunk, axis=1 - dim)
            product = dot(x, w, ((1,), (dim,))).astype(BF).reshape(sizes + (rows, chunk))
            got.append(reduce_parts(dims, product, n, stages))
        return jnp.concatenate(got, axis=1)

    branch = dot(spread_gated.reshape(total, modes * lanes), out_rows).astype(BF)
    branch = lax.psum_scatter(branch, chan, scatter_dimension=0, tiled=True)
    output = (mine.astype(F32) + branch.astype(F32)).astype(BF)[None]

    read_grad, gate_grad, grad_out_weight = cot_part(
        lots_at, spans_at, cots.reshape(lots_in, -1, width), out_rows, in_masks, gated,
        read.reshape(lot), gate_in,
    )
    grad_out_weight = jnp.moveaxis(grad_out_weight.reshape(modes, lanes, width), 0, 1)
    gate_grad = gate_grad.reshape(total, modes * lanes)
    in_rows = in_weight.shape[0]
    gate_sent = to_owners(t_dot(normed, gate_grad).astype(BF), in_rows)
    begun = jnp.concatenate([jnp.zeros_like(end), end], axis=0)
    cuts = [blocks, 0]
    so_far = None
    sums = []
    for n in range(len(cuts) - 1):
        act_grad, picked_grad, begun, *more = scan_back(
            cuts[n + 1], cuts[n], table, begins, act, picked, masks, pre,
            read_grad.reshape(grouped), prior, begun, rates, dt_cols, bias, skip, states, so_far,
            [],
        )
        so_far = (act_grad, picked_grad)
        sums.append(more)
    rate_grad, grad_dt, grad_bias, grad_skip = (sum(parts_of) for parts_of in zip(*sums))
    rate_grad = rate_grad.reshape(count, copies, groups, lanes).sum(axis=2)
    grad_decay = jnp.moveaxis(rate_grad, 0, 1).reshape(states, lanes).T * rate
    picked_grad = reduce_small(dims, picked_grad.reshape(sizes + (-1, 128))).astype(BF)
    picked_grad = gather_small(dims, picked_grad).reshape(groups, blocks, -1, 128)
    grad_gate_cols = exchange(after(gate_sent, picked_grad))
    x_grad, tap_grad, base_grad, grad_xproj = conv_back(
        table, begins, act_grad, picked_grad, pre_act, act, conv_in.reshape(grouped), masks, taps,
        xproj, [],
    )
    x_grad = x_grad.reshape(total, modes * lanes)
    grad_x_cols = exchange(jnp.concatenate(
        [
            to_owners(t_dot(normed, x_grad).astype(BF), in_rows),
            to_owners(grad_dt.astype(BF), rank_rows),
        ],
        axis=1,
    ))
    grad_dt = returned(grad_x_cols[:, in_rows * modes :], rank_rows).astype(F32)
    grad_x_cols = returned(grad_x_cols[:, : in_rows * modes], in_rows)
    grad_gate_cols = returned(grad_gate_cols, in_rows)
    normed_grad = scatter(
        jnp.concatenate([x_grad, gate_grad], axis=1),
        jnp.concatenate([x_cols, gate_cols], axis=1), 1, [],
    )
    grad_in = jnp.concatenate([grad_x_cols, grad_gate_cols], axis=2).astype(F32)
    grad_gain = jnp.sum(grad_in * in_weight.astype(F32), axis=(1, 2)) / norm_gain.astype(F32)
    xm = mine.astype(F32)
    scale = lax.rsqrt(jnp.mean(xm * xm, axis=1, keepdims=True) + EPS)
    unit = xm * scale
    scaled = normed_grad * gain
    grad_hidden = cotangent[0].astype(F32) + scale * (
        scaled - unit * jnp.mean(scaled * unit, axis=1, keepdims=True)
    )
    return (
        output,
        grad_hidden[None],
        grad_gain,
        grad_in,
        settle(tap_grad[:4].T),
        settle(base_grad[0]),
        settle(grad_xproj.reshape(lanes, modes, -1)),
        grad_dt,
        settle(grad_bias[:modes].T),
        settle(grad_decay),
        settle(grad_skip[0]),
        settle(grad_out_weight),
    )


def solution(mesh):
    both = ("grp", "seq")
    full = mesh.shape["grp"] * mesh.shape["seq"] <= 32
    chan, held = (both, ()) if full else (("seq",), ("grp",))
    row = P(both)
    return jax.shard_map(
        functools.partial(on_device, chan, held),
        mesh=mesh,
        in_specs=(
            P("grp", "seq", None), P("grp", "seq"), P("grp"),
            row, row, row, row, row, row, row, row, row, row,
            P("grp", "seq", None),
        ),
        out_specs=(P("grp", "seq", None), P("grp", "seq", None)) + (row,) * 10,
        check_vma=False,
    )
```

```python
import functools
import math

import jax
import jax.numpy as jnp
import numpy as np
from jax import lax
from jax.experimental import pallas as pl
from jax.experimental.pallas import tpu as pltpu
from jax.sharding import PartitionSpec as P

EPS = 1e-05
BF = jnp.bfloat16
F32 = jnp.float32
LOG2E = math.log2(math.e)
RESET = 1e4
VMEM = 60 * 1024 * 1024


def dot(a, b, dims=((1,), (0,))):
    return lax.dot_general(a, b, (dims, ((), ())), preferred_element_type=F32)


def silu_slope(v):
    s = jax.nn.sigmoid(v)
    return s * (1.0 + v * (1.0 - s))


def after(x, other):
    return x + (other[(0,) * other.ndim] * 0).astype(x.dtype)


def pick(values, masks):
    count = masks.shape[1]
    width = values.shape[1] // count
    return sum(values[:, m * width : (m + 1) * width] * masks[:, m : m + 1] for m in range(count))


def spread(values, masks):
    return jnp.concatenate(
        [values * masks[:, m : m + 1].astype(values.dtype) for m in range(masks.shape[1])], axis=1
    )


def spread_lanes(source, widen, target):

    low = source[...].astype(BF)
    for c in range(0, target.shape[1], 256):
        target[:, c : c + 256] = dot(low, widen[:, c : c + 256])


def widening(columns, lanes):
    ones = np.zeros((2 * columns, columns * lanes), np.float32)
    for s in range(columns):
        ones[s, s * lanes : (s + 1) * lanes] = 1
        ones[columns + s, s * lanes : (s + 1) * lanes] = 1
    return jnp.asarray(ones, BF)


def dot_t(a, b):
    return dot(a, b, ((1,), (1,)))


def t_dot(a, b):
    return dot(a, b, ((0,), (0,)))


def softplus(x):
    return jnp.maximum(x, 0.0) + jnp.log1p(jnp.exp(-jnp.abs(x)))


def packed(values, width):
    count = 128 // width
    span = values.shape[0] // count
    return jnp.concatenate([values[q * span : (q + 1) * span, :] for q in range(count)], axis=1)


def unpacked(values, width):
    values = values.astype(F32)
    return jnp.concatenate(
        [values[:, q * width : (q + 1) * width] for q in range(128 // width)], axis=0
    )


def to_time_major(ref, values, row, count):
    ref[pl.ds(row, count, stride=8), :] = values


def lay_out(groups, length, states, first, starts, step, act, picked, extra, sf, du, bc, also):
    copies = 8 // groups
    position = first + lax.broadcasted_iota(jnp.int32, (length, 1), 0)
    lane = lax.broadcasted_iota(jnp.int32, (1, 4 * states), 1)
    owner = lane % states // (states // copies)
    for g in range(groups):
        begin = (position == 0) | (position == starts[g])
        fade_step = jnp.where(begin, RESET, step[g])
        drive = step[g] * act[g, 0]
        span = length * 2 * states // 128
        chosen = jnp.concatenate(
            [
                unpacked(picked[g, 0, length + n * span : length + (n + 1) * span, :], 2 * states)
                for n in range(2)
            ],
            axis=1,
        )
        for j in range(copies):
            to_time_major(sf, fade_step, j * groups + g, length)
            to_time_major(du, drive, j * groups + g, length)
            to_time_major(bc, jnp.where(owner == j, chosen, 0.0), j * groups + g, length)
            if also is not None:
                to_time_major(also, extra[g, 0], j * groups + g, length)


def pre_step(picked, mask, dt, bias):
    modes, lanes = bias.shape
    product = dot(picked[: mask.shape[0], :], dt[...])
    return sum(
        (product[:, m * lanes : (m + 1) * lanes] + bias[m : m + 1, :]) * mask[:, m : m + 1]
        for m in range(modes)
    )


def scan_kernel(
    groups, length, states, table, starts, act, picked, mask, rate, widen, dt, bias, skip, y, pre, prior, end, sf, du, bc, ys, state, ex,
):
    copies, count, lanes = 8 // groups, rate.shape[0] // 8, rate.shape[1]
    i = pl.program_id(0)

    @pl.when(i == 0)
    def _():
        state[...] = jnp.zeros_like(state)

    steps = []
    for g in range(groups):
        raw = pre_step(picked[g, 0], mask[g, 0], dt, bias)
        pre[g, 0] = raw
        steps.append(softplus(raw))
    lay_out(groups, length, states, i * length, starts, steps, act, picked, None, sf, du, bc, None)
    spread_lanes(bc, widen, ex)
    rates = [rate[s * 8 : s * 8 + 8, :] for s in range(count)]

    def one(p, h):
        row = pl.ds(pl.multiple_of(p * 8, 8), 8)
        step_p, drive_p = sf[row, :], du[row, :]
        read = None
        out = []
        for s in range(count):
            prior[pl.ds(pl.multiple_of((p * count + s) * 8, 8), 8), :] = h[s]
            now = jnp.exp2(step_p * rates[s]) * h[s] + drive_p * ex[row, s * lanes : (s + 1) * lanes]
            term = now * ex[row, (count + s) * lanes : (count + s + 1) * lanes]
            read = term if read is None else read + term
            out.append(now)
        ys[row, :] = read
        return tuple(out)

    first = tuple(state[s * 8 : s * 8 + 8, :] for s in range(count))
    last = lax.fori_loop(0, length, one, first, unroll=8)
    for s in range(count):
        state[s * 8 : s * 8 + 8, :] = last[s]
    end[...] = state[...]
    for g in range(groups):
        total = sum(ys[pl.ds(j * groups + g, length, stride=8), :] for j in range(copies))
        total = total + skip[...] * act[g, 0]
        y[g, 0] = total


def back_kernel(
    groups, length, states, top, blocks, table, starts, act, picked, mask, pre, read_grad, prior,
    begun, rate, widen, dt, bias, skip, pick_b, pick_c, *refs,
):
    act_grad, picked_grad, left, rate_grad, dt_grad, bias_grad, skip_grad = refs[-20:-13]
    sf, du, gy, bc, wt, ft, pb, pc, res, carry, held, ex, step = refs[-13:]
    copies, count = 8 // groups, rate.shape[0] // 8
    lanes = rate.shape[1]
    modes = bias.shape[0]
    rank = dt.shape[0]
    i = pl.program_id(0)

    @pl.when(i == 0)
    def _():
        carry[...] = begun[0 : count * 8, :]
        held[...] = begun[count * 8 :, :]
        rate_grad[...] = jnp.zeros_like(rate_grad)
        dt_grad[...] = jnp.zeros_like(dt_grad)
        bias_grad[...] = jnp.zeros_like(bias_grad)
        skip_grad[...] = jnp.zeros_like(skip_grad)

    for g in range(groups):
        step[g] = softplus(pre[g, 0])
    lay_out(
        groups, length, states, (top - i) * length, starts, step, act, picked, read_grad, sf, du, bc, gy
    )
    spread_lanes(bc, widen, ex)
    rates = [rate[s * 8 : s * 8 + 8, :] for s in range(count)]

    def one(k, loop):
        p = length - 1 - k
        row = pl.ds(pl.multiple_of(p * 8, 8), 8)
        step_p, drive_p, grad_p = sf[row, :], du[row, :], gy[row, :]
        carried, state, total = loop
        weight_sum, fade_sum = None, None
        out_c, out_h, out_r = [], [], []
        for s in range(count):
            before = prior[pl.ds(pl.multiple_of((p * count + s) * 8, 8), 8), :]
            cols = slice(s * lanes, (s + 1) * lanes)
            e = grad_p * ex[row, (count + s) * lanes : (count + s + 1) * lanes] + carried[s]
            pc[row, cols] = grad_p * state[s]
            pb[row, cols] = e * drive_p
            term = e * ex[row, cols]
            passed = e * jnp.exp2(step_p * rates[s])
            decay = passed * before
            fade_term = decay * rates[s]
            weight_sum = term if weight_sum is None else weight_sum + term
            fade_sum = fade_term if fade_sum is None else fade_sum + fade_term
            out_c.append(passed)
            out_h.append(before)
            out_r.append(total[s] + decay * step_p)
        wt[row, :] = weight_sum
        ft[row, :] = fade_sum
        return tuple(out_c), tuple(out_h), tuple(out_r)

    def parts(ref):
        return tuple(ref[s * 8 : s * 8 + 8, :] for s in range(count))

    c, h, r = lax.fori_loop(
        0, length, one, (parts(carry), parts(held), parts(rate_grad)), unroll=4
    )
    for s in range(count):
        carry[s * 8 : s * 8 + 8, :] = c[s]
        held[s * 8 : s * 8 + 8, :] = h[s]
        rate_grad[s * 8 : s * 8 + 8, :] = r[s]
    left[0 : count * 8, :] = carry[...]
    left[count * 8 :, :] = held[...]
    res[...] = dot(pb[...].astype(BF), pick_b[...]) + dot(pc[...].astype(BF), pick_c[...])
    lane = lax.broadcasted_iota(jnp.int32, (1, 128), 1)
    owner = lane % states // count
    for g in range(groups):
        rows = [pl.ds(j * groups + g, length, stride=8) for j in range(copies)]
        weighted = sum(wt[row, :] for row in rows)
        faded = sum(ft[row, :] for row in rows) * (1.0 / LOG2E)
        chosen = sum(jnp.where(owner == j, res[rows[j], :], 0.0) for j in range(copies))
        grad_y, u = read_grad[g, 0], act[g, 0]
        act_grad[g, 0] = skip[...] * grad_y + step[g] * weighted
        pre_grad = (u * weighted + faded) * jax.nn.sigmoid(pre[g, 0])
        skip_grad[...] += jnp.sum(grad_y * u, axis=0, keepdims=True)
        rank_grad = None
        for m in range(modes):
            own = pre_grad * mask[g, 0, :, m : m + 1]
            bias_grad[m : m + 1, :] += jnp.sum(own, axis=0, keepdims=True)
            own = own.astype(BF)
            cols = slice(m * lanes, (m + 1) * lanes)
            term = dot_t(own, dt[:, cols])
            rank_grad = term if rank_grad is None else rank_grad + term
            dt_grad[:, cols] += t_dot(picked[g, 0, 0:length, :], own)
        picked_grad[g, 0, 0:length, :] = rank_grad
        picked_grad[g, 0, length:, :] = packed(chosen[:, 0 : 2 * states], 2 * states)


def spread_lanes(source, widen, target):

    @pl.loop(0, source.shape[0] // 128)
    def _(n):
        row = pl.ds(pl.multiple_of(n * 128, 128), 128)
        target[row, :] = dot(source[row, :].astype(BF), widen[...])


def widening(states, count, lanes):
    ones = np.zeros((2, 2, states, 2 * count * lanes), np.float32)
    for kind in range(2):
        for s in range(states):
            block = kind * count + s % count
            ones[:, kind, s, block * lanes : (block + 1) * lanes] = 1
    return jnp.asarray(ones.reshape(4 * states, -1), BF)


def picking(states, count, lanes):
    ones = np.zeros((2, count * lanes, 128), np.float32)
    for kind in range(2):
        for s in range(states):
            at = s % count
            ones[kind, at * lanes : (at + 1) * lanes, kind * states + s] = 1
    return jnp.asarray(ones[0], BF), jnp.asarray(ones[1], BF)


def conv_kernel(groups, length, table, starts, x, mask, taps, base, xproj, v, act, part, tail, ext):
    i = pl.program_id(0)

    @pl.when(i == 0)
    def _():
        tail[...] = jnp.zeros_like(tail)

    modes = mask.shape[3]
    width = xproj.shape[1] // modes
    position = i * length + lax.broadcasted_iota(jnp.int32, (length, 1), 0)
    for g in range(groups):
        begin = jnp.where(position >= starts[g], starts[g], 0)
        ext[0:8, :] = tail[g]
        ext[8 : 8 + length, :] = x[g, 0]
        tail[g] = x[g, 0, length - 8 : length, :]
        total = base[...]
        for k in range(4):
            valid = (position - 3 + k >= begin).astype(F32)
            total = total + taps[k : k + 1, :] * ext[5 + k : 5 + k + length, :] * valid
        v[g, 0] = total
        active = total * jax.nn.sigmoid(total)
        act[g, 0] = active
        product = dot(active.astype(BF), xproj[...])
        chosen = sum(
            product[:, m * width : (m + 1) * width] * mask[g, 0, :, m : m + 1] for m in range(modes)
        )
        part[g, 0, 0:length, :] = chosen[:, 0:128]
        part[g, 0, length:, :] = packed(chosen[:, 128:], width - 128)


def conv_back_kernel(
    groups, length, blocks, table, starts, grad, sel_grad, v, act, x, mask, taps, xproj, *refs,
):
    x_grad, tap_grad, base_grad, weight_grad, head, ext = refs[-6:]
    i = pl.program_id(0)

    @pl.when(i == 0)
    def _():
        head[...] = jnp.zeros_like(head)
        weight_grad[...] = jnp.zeros_like(weight_grad)
        tap_grad[...] = jnp.zeros_like(tap_grad)
        base_grad[...] = jnp.zeros_like(base_grad)

    modes = mask.shape[3]
    width = xproj.shape[1] // modes
    position = (blocks - 1 - i) * length + lax.broadcasted_iota(jnp.int32, (length, 1), 0)
    for g in range(groups):
        chosen = jnp.concatenate(
            [
                sel_grad[g, 0, 0:length, :].astype(F32),
                unpacked(sel_grad[g, 0, length:, :], width - 128),
            ],
            axis=1,
        ).astype(BF)
        masked = [chosen * mask[g, 0, :, m : m + 1].astype(BF) for m in range(modes)]
        act_grad = grad[g, 0]
        low = act[g, 0].astype(BF)
        for m in range(modes):
            cols = slice(m * width, (m + 1) * width)
            act_grad = act_grad + dot_t(masked[m], xproj[:, cols])
            weight_grad[:, cols] += t_dot(low, masked[m])
        v_grad = act_grad * silu_slope(v[g, 0])
        ext[0:length, :] = v_grad
        ext[length : length + 8, :] = head[g]
        head[g] = v_grad[0:8, :]
        base_grad[...] += jnp.sum(v_grad, axis=0, keepdims=True)
        total = None
        for k in range(4):
            crosses = (position < starts[g]) & (position + 3 - k >= starts[g])
            shifted = jnp.where(crosses, 0.0, ext[3 - k : 3 - k + length, :])
            term = taps[k : k + 1, :] * shifted
            total = term if total is None else total + term
            tap_grad[k : k + 1, :] += jnp.sum(x[g, 0] * shifted, axis=0, keepdims=True)
        total = total.astype(BF)
        lanes = total.shape[1]
        for m in range(modes):
            x_grad[g, 0, :, m * lanes : (m + 1) * lanes] = total * mask[g, 0, :, m : m + 1].astype(BF)


def inproj_kernel(lots, *refs):
    pieces = refs[:-9]
    gain, weight, normed, proj, mask, notes, cols, whole, arrived = refs[-9:]
    modes = mask.shape[2]
    lanes = weight.shape[2]
    count = len(pieces) // lots
    rows = mask.shape[1] // count
    part = cols.shape[0] // weight.shape[0]
    i = pl.program_id(0)

    def copies(lot):
        return [
            pltpu.make_async_copy(
                pieces[lot * count + n], whole.at[lot % 2, n], arrived.at[lot % 2, n]
            )
            for n in range(count)
        ]

    @pl.when(i == 0)
    def _():
        for copy in copies(0):
            copy.start()
        for n in range(weight.shape[0]):
            for m in range(modes):
                cols[n * part : (n + 1) * part, m * lanes : (m + 1) * lanes] = weight[
                    n, m * part : (m + 1) * part, :
                ]

    for lot in range(lots):

        @pl.when(i == lot)
        def _(lot=lot):
            if lot + 1 < lots:
                for copy in copies(lot + 1):
                    copy.start()
            for copy in copies(lot):
                copy.wait()

    slot = lax.rem(i, 2)
    square = (rows, rows)
    same = lax.broadcasted_iota(jnp.int32, square, 0) == lax.broadcasted_iota(jnp.int32, square, 1)
    kind = lax.broadcasted_iota(jnp.int32, (1, modes), 1).astype(F32)
    for n in range(count):
        span = slice(n * rows, (n + 1) * rows)
        x = whole[slot, n, 0:rows, :].astype(F32)
        scale = lax.rsqrt(jnp.mean(x * x, axis=1, keepdims=True) + EPS)
        normed[0, span, :] = (x * scale * gain[...]).astype(BF)
        note = whole[slot, n, rows : rows + 16, 0:rows].astype(F32)
        column = jnp.sum(jnp.where(same, note[0:1, :], 0.0), axis=1, keepdims=True)
        mask[0, span, :] = (column == kind).astype(F32)
        if n == 0:
            notes[0] = note[0:8, :]
    product = dot(normed[0], cols[...])
    proj[0] = sum(
        product[:, m * lanes : (m + 1) * lanes] * mask[0, :, m : m + 1] for m in range(modes)
    )


def inproj(lots, rows, modes, pieces, gain, weight):
    tall, width = pieces[0].shape
    lanes = weight.shape[2]
    count = len(pieces) // lots
    size = count * rows
    block = lambda *shape: pl.BlockSpec((1,) + shape, lambda i: (i, 0, 0))
    shapes = [
        jax.ShapeDtypeStruct((lots, size, width), BF),
        jax.ShapeDtypeStruct((lots, size, lanes), F32),
        jax.ShapeDtypeStruct((lots, size, modes), F32),
        jax.ShapeDtypeStruct((lots, 8, rows), F32),
        jax.ShapeDtypeStruct((width, modes * lanes), BF),
    ]
    return pl.pallas_call(
        functools.partial(inproj_kernel, lots),
        grid=(lots,),
        in_specs=[pl.BlockSpec(memory_space=pl.ANY)] * len(pieces) + [flat(gain), flat(weight)],
        out_specs=[block(*a.shape[1:]) for a in shapes[:4]] + [flat(shapes[4])],
        out_shape=shapes,
        scratch_shapes=[
            pltpu.VMEM((2, count, tall, width), BF),
            pltpu.SemaphoreType.DMA((2, count)),
        ],
        compiler_params=pltpu.CompilerParams(vmem_limit_bytes=VMEM),
        cost_estimate=pl.CostEstimate(
            flops=2 * lots * size * width * modes * lanes,
            bytes_accessed=6 * lots * size * width,
            transcendentals=0,
        ),
    )(*pieces, gain, weight)


def conv(table, starts, x, mask, taps, base, xproj):
    groups, blocks, length, lanes = x.shape
    modes = mask.shape[3]
    width = xproj.shape[1] // modes
    at = lambda i, t, b: (0, t[i], 0, 0)
    flat = lambda i, t, b: (0, 0)
    block = pl.BlockSpec((groups, 1, length, lanes), at)
    return pl.pallas_call(
        functools.partial(conv_kernel, groups, length),
        grid_spec=pltpu.PrefetchScalarGridSpec(
            num_scalar_prefetch=2,
            grid=(blocks,),
            in_specs=[
                block,
                pl.BlockSpec((groups, 1, length, modes), at),
                pl.BlockSpec(taps.shape, flat),
                pl.BlockSpec(base.shape, flat),
                pl.BlockSpec(xproj.shape, flat),
            ],
            out_specs=[block, block, pl.BlockSpec((groups, 1, length * width // 128, 128), at)],
            scratch_shapes=[
                pltpu.VMEM((groups, 8, lanes), F32),
                pltpu.VMEM((length + 8, lanes), F32),
            ],
        ),
        out_shape=[
            jax.ShapeDtypeStruct(x.shape, F32),
            jax.ShapeDtypeStruct(x.shape, F32),
            jax.ShapeDtypeStruct((groups, blocks, length * width // 128, 128), F32),
        ],
        compiler_params=pltpu.CompilerParams(vmem_limit_bytes=VMEM),
    )(table, starts, x, mask, taps, base, xproj)


def conv_back(table, starts, grad, sel_grad, v, act, x, mask, taps, xproj, before):
    groups, blocks, length, lanes = x.shape
    modes = mask.shape[3]
    width = xproj.shape[1] // modes
    at = lambda i, t, b: (0, t[blocks - 1 - i], 0, 0)
    flat = lambda i, t, b: (0, 0)
    block = pl.BlockSpec((groups, 1, length, lanes), at)
    return pl.pallas_call(
        functools.partial(conv_back_kernel, groups, length, blocks),
        grid_spec=pltpu.PrefetchScalarGridSpec(
            num_scalar_prefetch=2,
            grid=(blocks,),
            in_specs=[
                block,
                pl.BlockSpec((groups, 1, length * width // 128, 128), at),
                block,
                block,
                block,
                pl.BlockSpec((groups, 1, length, modes), at),
                pl.BlockSpec(taps.shape, flat),
                pl.BlockSpec(xproj.shape, flat),
            ]
            + [pl.BlockSpec(memory_space=pl.ANY)] * len(before),
            out_specs=[
                pl.BlockSpec((groups, 1, length, modes * lanes), at),
                pl.BlockSpec((8, lanes), flat),
                pl.BlockSpec((1, lanes), flat),
                pl.BlockSpec(xproj.shape, flat),
            ],
            scratch_shapes=[
                pltpu.VMEM((groups, 8, lanes), F32),
                pltpu.VMEM((length + 8, lanes), F32),
            ],
        ),
        out_shape=[
            jax.ShapeDtypeStruct((groups, blocks, length, modes * lanes), BF),
            jax.ShapeDtypeStruct((8, lanes), F32),
            jax.ShapeDtypeStruct((1, lanes), F32),
            jax.ShapeDtypeStruct(xproj.shape, F32),
        ],
        compiler_params=pltpu.CompilerParams(vmem_limit_bytes=VMEM),
    )(table, starts, grad, sel_grad, v, act, x, mask, taps, xproj, *before)


def flat(array):
    return pl.BlockSpec(array.shape, lambda i, *_: (0,) * array.ndim)


def scan(table, starts, act, picked, mask, rate, dt, bias, skip, states):
    groups, blocks, length, lanes = act.shape
    total = blocks * length
    count = rate.shape[0] // 8
    at = lambda i, t, b: (0, t[i], 0, 0)
    block = lambda a: pl.BlockSpec((groups, 1) + a.shape[2:], at)
    widen = widening(states, count, lanes)
    tall = pltpu.VMEM((length * 8, lanes), F32)
    like = jax.ShapeDtypeStruct(act.shape, F32)
    return pl.pallas_call(
        functools.partial(scan_kernel, groups, length, states),
        grid_spec=pltpu.PrefetchScalarGridSpec(
            num_scalar_prefetch=2,
            grid=(blocks,),
            in_specs=[block(a) for a in (act, picked, mask)]
            + [flat(a) for a in (rate, widen, dt, bias, skip)],
            out_specs=[
                block(act),
                block(act),
                pl.BlockSpec((length * count * 8, lanes), lambda i, t, b: (i, 0)),
                flat(rate),
            ],
            scratch_shapes=[
                tall,
                tall,
                pltpu.VMEM((length * 8, 4 * states), F32),
                tall,
                pltpu.VMEM((count * 8, lanes), F32),
                pltpu.VMEM((length * 8, 2 * count * lanes), F32),
            ],
        ),
        out_shape=[
            like,
            like,
            jax.ShapeDtypeStruct((total * count * 8, lanes), F32),
            jax.ShapeDtypeStruct((count * 8, lanes), F32),
        ],
        compiler_params=pltpu.CompilerParams(vmem_limit_bytes=VMEM),
        cost_estimate=pl.CostEstimate(flops=10**10, bytes_accessed=10**8, transcendentals=0),
    )(table, starts, act, picked, mask, rate, widen, dt, bias, skip)


def gate_kernel(lots_at, spans_at, normed, weight, mask, read, gate, gated, spread_gated):
    modes = mask.shape[2]
    lanes = read.shape[2]
    count = spans_at.shape[0]
    rows = read.shape[1] // count
    product = dot(normed[0], weight[...])
    masks = [mask[0, :, m : m + 1] for m in range(modes)]
    opened = sum(product[:, m * lanes : (m + 1) * lanes] * masks[m] for m in range(modes))
    gate[0] = opened
    low = (read[0] * (opened * jax.nn.sigmoid(opened))).astype(BF)
    gated[0] = low
    for m in range(modes):
        own = low * masks[m].astype(BF)
        for n in range(count):
            place = pl.ds(pl.multiple_of(spans_at[n] * rows, rows), rows)
            spread_gated[0, place, m * lanes : (m + 1) * lanes] = own[n * rows : (n + 1) * rows, :]


def gate_part(lots_at, spans_at, normed, weight, mask, read):
    lots, size, width = normed.shape
    lanes = read.shape[2]
    wide = weight.shape[1]
    block = lambda w: pl.BlockSpec((1, size, w), lambda i, a, b: (i, 0, 0))
    return pl.pallas_call(
        gate_kernel,
        grid_spec=pltpu.PrefetchScalarGridSpec(
            num_scalar_prefetch=2,
            grid=(lots,),
            in_specs=[block(width), flat(weight), block(mask.shape[2]), block(lanes)],
            out_specs=[
                block(lanes), block(lanes), pl.BlockSpec((1, size, wide), lambda i, a, b: (a[i], 0, 0))
            ],
        ),
        out_shape=[
            jax.ShapeDtypeStruct(read.shape, F32),
            jax.ShapeDtypeStruct(read.shape, BF),
            jax.ShapeDtypeStruct((lots, size, wide), BF),
        ],
        compiler_params=pltpu.CompilerParams(vmem_limit_bytes=VMEM),
        cost_estimate=pl.CostEstimate(
            flops=2 * lots * size * width * wide, bytes_accessed=3 * lots * size * width, transcendentals=0
        ),
    )(lots_at, spans_at, normed, weight, mask, read)


def scan_back(
    first, last, table, starts, act, picked, mask, pre, read_grad, prior, begun, rate, dt, bias,
    skip, states, so_far, before,
):
    groups, blocks, length, lanes = act.shape
    count = rate.shape[0] // 8
    rank = dt.shape[0]
    modes = bias.shape[0]
    at = lambda i, t, b: (0, t[last - 1 - i], 0, 0)
    block = lambda a: pl.BlockSpec((groups, 1) + a.shape[2:], at)
    widen = widening(states, count, lanes)
    pick_b, pick_c = picking(states, count, lanes)
    tall = pltpu.VMEM((length * 8, lanes), F32)
    wide = pltpu.VMEM((length * 8, count * lanes), F32)
    tables = pltpu.VMEM((count * 8, lanes), F32)
    shapes = [
        jax.ShapeDtypeStruct(act.shape, F32),
        jax.ShapeDtypeStruct((groups, blocks, length + length * 2 * states // 128, 128), F32),
        jax.ShapeDtypeStruct((2 * count * 8, lanes), F32),
        jax.ShapeDtypeStruct((count * 8, lanes), F32),
        jax.ShapeDtypeStruct((rank, modes * lanes), F32),
        jax.ShapeDtypeStruct((8, lanes), F32),
        jax.ShapeDtypeStruct((1, lanes), F32),
    ]
    loaded = (begun, rate, widen, dt, bias, skip, pick_b, pick_c)
    extra = tuple(so_far or ()) + tuple(before)
    at_input = 2 + 6 + len(loaded)
    return pl.pallas_call(
        functools.partial(back_kernel, groups, length, states, last - 1, blocks),
        grid_spec=pltpu.PrefetchScalarGridSpec(
            num_scalar_prefetch=2,
            grid=(last - first,),
            in_specs=[block(a) for a in (act, picked, mask, pre, read_grad)]
            + [pl.BlockSpec((length * count * 8, lanes), lambda i, t, b: (last - 1 - i, 0))]
            + [flat(a) for a in loaded]
            + [pl.BlockSpec(memory_space=pl.ANY)] * len(extra),
            out_specs=[block(shapes[0]), block(shapes[1])] + [flat(a) for a in shapes[2:]],
            scratch_shapes=[
                tall, tall, tall, pltpu.VMEM((length * 8, 4 * states), F32), tall, tall, wide, wide,
                pltpu.VMEM((length * 8, 128), F32),
                tables,
                tables,
                pltpu.VMEM((length * 8, 2 * count * lanes), F32),
                pltpu.VMEM((groups, length, lanes), F32),
            ],
        ),
        out_shape=shapes,
        input_output_aliases={at_input: 0, at_input + 1: 1} if so_far else {},
        compiler_params=pltpu.CompilerParams(vmem_limit_bytes=VMEM),
        cost_estimate=pl.CostEstimate(
            flops=10**10, bytes_accessed=25 * 10**6 * (last - first), transcendentals=0
        ),
    )(table, starts, act, picked, mask, pre, read_grad, prior, *loaded, *extra)


def cot_kernel(
    lots_at, spans_at, cots, out_rows, mask, gated, read, gate, read_grad, gate_grad, weight_grad, whole
):
    count = spans_at.shape[0]
    rows = whole.shape[0] // count

    @pl.when(pl.program_id(0) == 0)
    def _():
        weight_grad[...] = jnp.zeros_like(weight_grad)

    for n in range(count):
        whole[n * rows : (n + 1) * rows, :] = cots[
            0, pl.ds(pl.multiple_of(spans_at[n] * rows, rows), rows), :
        ]
    product = dot_t(whole[...], out_rows[...])
    modes = mask.shape[2]
    lanes = gated.shape[2]
    masks = [mask[0, :, m : m + 1] for m in range(modes)]
    grad = sum(product[:, m * lanes : (m + 1) * lanes] * masks[m] for m in range(modes))
    opened = gate[0]
    read_grad[0] = grad * (opened * jax.nn.sigmoid(opened))
    gate_low = (grad * read[0] * silu_slope(opened)).astype(BF)
    for m in range(modes):
        own = masks[m].astype(BF)
        cols = slice(m * lanes, (m + 1) * lanes)
        gate_grad[0, :, cols] = gate_low * own
        weight_grad[cols, :] += t_dot(gated[0] * own, whole[...])


def cot_part(lots_at, spans_at, cots, out_rows, mask, gated, read, gate):
    lots, size, width = cots.shape
    lanes = gated.shape[2]
    wide = out_rows.shape[0]
    block = lambda w: pl.BlockSpec((1, size, w), lambda i, a, b: (i, 0, 0))
    return pl.pallas_call(
        cot_kernel,
        grid_spec=pltpu.PrefetchScalarGridSpec(
            num_scalar_prefetch=2,
            grid=(lots,),
            in_specs=[pl.BlockSpec((1, size, width), lambda i, a, b: (a[i], 0, 0)), flat(out_rows)]
            + [block(a.shape[2]) for a in (mask, gated, read, gate)],
            out_specs=[block(lanes), block(wide), flat(out_rows)],
            scratch_shapes=[pltpu.VMEM((size, width), BF)],
        ),
        out_shape=[
            jax.ShapeDtypeStruct((lots, size, lanes), F32),
            jax.ShapeDtypeStruct((lots, size, wide), BF),
            jax.ShapeDtypeStruct(out_rows.shape, F32),
        ],
        compiler_params=pltpu.CompilerParams(vmem_limit_bytes=VMEM),
        cost_estimate=pl.CostEstimate(
            flops=4 * lots * size * width * wide, bytes_accessed=3 * lots * size * width, transcendentals=0
        ),
    )(lots_at, spans_at, cots, out_rows, mask, gated, read, gate)


class Dim:

    def __init__(self, axis, stride, size, length):
        self.axis, self.stride, self.size, self.length = axis, stride, size, length

    def here(self):
        return lax.axis_index(self.axis) // self.stride % self.size

    def fetch(self, x, by):
        pairs = []
        for i in range(self.length):
            c = i // self.stride % self.size
            pairs.append((i + ((c + by) % self.size - c) * self.stride, i))
        return lax.ppermute(x, self.axis, pairs)


def dims_of(chan):
    dims = []
    for axis in chan:
        length = lax.axis_size(axis)
        sizes = []
        rest = length
        if axis == "seq":
            rest //= 2
        radix = 4 if axis == "seq" else 2
        while rest > 1:
            sizes.insert(0, min(radix, rest))
            rest //= sizes[0]
        if axis == "seq":
            sizes.append(2)
        stride = length
        for size in sizes:
            stride //= size
            dims.append(Dim(axis, stride, size, length))
    return dims


def fence(*arrays):
    return list(pl.pallas_call(
        lambda *refs: None,
        in_specs=[pl.BlockSpec(memory_space=pl.ANY)] * len(arrays),
        out_specs=[pl.BlockSpec(memory_space=pl.ANY)] * len(arrays),
        out_shape=[jax.ShapeDtypeStruct(x.shape, x.dtype) for x in arrays],
        input_output_aliases={n: n for n in range(len(arrays))},
    )(*arrays))


def gather_pieces(dims, x):
    others, ring, core = dims[:-2], dims[-2], dims[-1]
    got = {}
    first = x
    for k in range(ring.size):
        if k:
            first = ring.fetch(first, 1)
        order = list(range(len(others)))
        if k % 2:
            order.reverse()
        held = {(0,) * len(others): first}
        for d in order:
            for at, block in list(held.items()):
                for r in range(1, others[d].size):
                    block = others[d].fetch(block, 1)
                    held[at[:d] + (r,) + at[d + 1 :]] = block
        for at, block in held.items():
            got[at + (k, 0)] = block
            got[at + (k, 1)] = core.fetch(block, 1)
    return [got[at] for at in sorted(got)]


def pairs_of(dims):
    return [d.size for d in dims[:-2]] == [2, 2]


def gather_stage(dims, x, d):
    got = [x] + [dims[d].fetch(x, r) for r in range(1, dims[d].size)]
    return jnp.concatenate(got, axis=d)


def gather_small(dims, x):
    x = x.reshape((1,) * len(dims) + x.shape)
    x = gather_stage(dims, x, len(dims) - 2)
    if pairs_of(dims):
        halves = jnp.split(x, 2, axis=len(dims))
        halves = [gather_stage(dims, h, n) for n, h in enumerate(halves)]
        halves = [gather_stage(dims, h, 1 - n) for n, h in enumerate(halves)]
        x = jnp.concatenate(halves, axis=len(dims))
    else:
        for d in range(len(dims) - 2):
            x = gather_stage(dims, x, d)
    return gather_stage(dims, x, len(dims) - 1)


def reduce_stage(dims, x, d, kind):
    block = [lax.slice_in_dim(x, r, r + 1, axis=d) for r in range(dims[d].size)]
    return add_up(
        [block[0]] + [dims[d].fetch(block[r].astype(kind), -r) for r in range(1, len(block))]
    )


def reduce_small(dims, x):
    x = reduce_stage(dims, x, len(dims) - 1, F32)
    if pairs_of(dims):
        halves = jnp.split(x, 2, axis=len(dims))
        halves = [reduce_stage(dims, h, n, BF) for n, h in enumerate(halves)]
        halves = [reduce_stage(dims, h, 1 - n, F32) for n, h in enumerate(halves)]
        x = jnp.concatenate(halves, axis=len(dims))
    else:
        for d in range(len(dims) - 2):
            x = reduce_stage(dims, x, d, F32 if d else BF)
    x = reduce_stage(dims, x, len(dims) - 2, F32)
    return x.reshape(x.shape[len(dims) :])


def add_up(parts):
    return sum(p.astype(F32) for p in parts)


def reduce_parts(dims, x, turn, stages):
    order = list(range(len(dims) - 2))
    if turn % 2:
        order.reverse()
    order = [len(dims) - 1] + order + [len(dims) - 2]
    for n, d in enumerate(order):
        size = dims[d].size
        block = [lax.slice_in_dim(x, r, r + 1, axis=d) for r in range(size)]
        if size == 2:
            x = add_up([block[0]] + [dims[d].fetch(block[r], -r) for r in range(1, size)])
        else:
            moving = block[size - 1]
            for r in range(size - 2, -1, -1):
                x = add_up([block[r], dims[d].fetch(moving, -1)])
                moving = x.astype(BF)
        if n < len(order) - 1:
            x = x.astype(BF)
            stages.append((n, x))
    return x.reshape(x.shape[len(dims) :])


def on_device(
    chan, held,
    hidden, modality, starts, norm_gain, in_weight, conv_weight, conv_bias, xproj_weight,
    dtproj_weight, step_bias, decay_log, skip_weight, out_weight, cotangent,
):
    def collect(x):
        return lax.all_gather(x, held, axis=0, tiled=True) if held else x

    def exchange(x):
        return lax.all_to_all(x, chan, 0, 0, tiled=True)

    def settle(x):
        return lax.psum_scatter(x, held, scatter_dimension=0, tiled=True) if held else x

    dims = dims_of(chan)
    sizes = tuple(d.size for d in dims)
    parts = math.prod(sizes)
    lots = math.prod(lax.axis_size(a) for a in held) if held else 1
    groups = parts // lax.axis_size("seq")
    rows, width = hidden.shape[1:]
    own = conv_weight.shape[0]
    lanes = own * lots
    rank_rows = dtproj_weight.shape[0]
    rank = rank_rows * parts * lots
    modes = in_weight.shape[1]
    states = decay_log.shape[1]
    mine = hidden[0]
    cot = cotangent[0]

    def shards(w):
        w = w.reshape(w.shape[0], modes, lots, parts, own)
        return jnp.moveaxis(w, 3, 0).reshape(parts, w.shape[0], modes, lanes)

    def to_owners(g, out_rows):
        return settle(g).reshape(parts, out_rows * modes, lanes)

    def returned(g, out_rows):
        g = g.reshape(parts, out_rows, modes, lots, own)
        return jnp.moveaxis(g, 0, 3).reshape(out_rows, modes, lots * parts * own)

    inner = lanes * parts
    blocks = parts // groups
    note = jnp.pad(jnp.stack([starts[0] >> 6, starts[0] & 63])[None], ((0, 0), (0, rows - 2)))
    note = jnp.concatenate([modality, note], axis=0).astype(BF)
    note = jnp.pad(note, ((0, 14), (0, width - rows)))
    pieces = gather_pieces(dims, jnp.concatenate([mine, note], axis=0))
    room = -norm_gain.shape[0] % lanes
    notes = jnp.broadcast_to(jnp.pad(norm_gain, (0, room)), (parts, norm_gain.shape[0] + room))
    moved = collect(exchange(jnp.concatenate(
        [
            jnp.swapaxes(shards(in_weight[:, :, :inner]), 1, 2).reshape(parts, -1, lanes),
            shards(dtproj_weight).reshape(parts, -1, lanes),
            notes.reshape(parts, -1, lanes),
        ],
        axis=1,
    )))
    cut = in_weight.shape[0] * modes
    further = cut + rank_rows * modes
    dt_cols = moved[:, cut:further].reshape(rank, modes * lanes)
    gain = moved[:, further:].reshape(parts * lots, -1)[:, : norm_gain.shape[0]]
    gain = gain.reshape(1, width).astype(F32)
    conv_weight, conv_bias, xproj_weight, step_bias, decay_log, skip_weight, out_weight = (
        collect(w)
        for w in (conv_weight, conv_bias, xproj_weight, step_bias, decay_log, skip_weight, out_weight)
    )
    taps = conv_weight.astype(F32).T
    bias = step_bias.astype(F32).T
    skip = skip_weight.astype(F32)[None]
    xproj = xproj_weight.reshape(lanes, -1)
    out_rows = jnp.moveaxis(out_weight, 1, 0).reshape(modes * lanes, width)
    total = parts * rows
    copies = 8 // groups
    count = states // copies
    rate = -jnp.exp(decay_log.astype(F32))
    rates = jnp.moveaxis(rate.T.reshape(copies, count, lanes), 0, 1)
    rates = jnp.repeat(rates.reshape(count * copies, 1, lanes), groups, axis=1).reshape(-1, lanes)
    rates = rates * LOG2E
    order = jnp.zeros((), jnp.int32)
    spans = jnp.arange(blocks, dtype=jnp.int32)
    stride = blocks
    for d in dims:
        if d.axis == "seq":
            stride //= d.size
            order = order * d.size + (spans // stride % d.size - d.here()) % d.size
    table = order

    def placed(some):
        at = jnp.zeros((), jnp.int32)
        stride = math.prod(d.size for d in some)
        names = jnp.arange(stride, dtype=jnp.int32)
        for d in some:
            stride //= d.size
            at = at * d.size + (names // stride % d.size + d.here()) % d.size
        return at.reshape(-1)


    step_pieces = sizes[-1] * sizes[-2]
    lots_in = parts // step_pieces
    normed, conv_in, in_masks, notes, x_cols = inproj(lots_in, rows, modes, pieces, gain, moved)
    masks = in_masks.reshape(groups, blocks, rows, modes)
    notes = notes.reshape(groups, -1, 8, rows)[:, 0, 1].astype(jnp.int32)
    begins = notes[:, 0] * 64 + notes[:, 1]
    cots = lax.all_gather(after(cot, conv_in), chan, axis=0, tiled=True)
    normed = normed.reshape(total, width)
    grouped = (groups, blocks, rows, lanes)
    pre_act, act, partial = conv(
        table, begins, conv_in.reshape(grouped), masks, taps, conv_bias.astype(F32)[None], xproj
    )
    picked = reduce_small(dims, partial.reshape(sizes + (-1, 128)))
    low = picked.astype(BF)
    rest = (picked[rows:] - low[rows:].astype(F32)).astype(BF)
    picked = gather_small(dims, jnp.concatenate([low, rest], axis=0))
    picked = picked.reshape(groups, blocks, -1, 128)
    gate_cols = collect(exchange(shards(after(in_weight[:, :, inner:], picked))).reshape(
        -1, modes, lanes
    )).reshape(width, modes * lanes)
    read, pre, prior, end = scan(
        table, begins, act, picked, masks, rates, dt_cols, bias, skip, states
    )
    lot = (lots_in, step_pieces * rows, -1)
    lots_at, spans_at = placed(dims[:-2]), placed(dims[-2:])
    gate_in, gated, spread_gated = gate_part(
        lots_at, spans_at, normed.reshape(lot), gate_cols, in_masks, read.reshape(lot)
    )

    def scatter(x, weight, dim, stages):
        got = []
        chunk = width // 2
        for n in range(2):
            w = lax.slice_in_dim(weight, n * chunk, (n + 1) * chunk, axis=1 - dim)
            product = dot(x, w, ((1,), (dim,))).astype(BF).reshape(sizes + (rows, chunk))
            got.append(reduce_parts(dims, product, n, stages))
        return jnp.concatenate(got, axis=1)

    branch = dot(spread_gated.reshape(total, modes * lanes), out_rows).astype(BF)
    branch = lax.psum_scatter(branch, chan, scatter_dimension=0, tiled=True)
    output = (mine.astype(F32) + branch.astype(F32)).astype(BF)[None]

    read_grad, gate_grad, grad_out_weight = cot_part(
        lots_at, spans_at, cots.reshape(lots_in, -1, width), out_rows, in_masks, gated,
        read.reshape(lot), gate_in,
    )
    grad_out_weight = jnp.moveaxis(grad_out_weight.reshape(modes, lanes, width), 0, 1)
    gate_grad = gate_grad.reshape(total, modes * lanes)
    in_rows = in_weight.shape[0]
    gate_sent = to_owners(t_dot(normed, gate_grad).astype(BF), in_rows)
    begun = jnp.concatenate([jnp.zeros_like(end), end], axis=0)
    cuts = [blocks, 0]
    so_far = None
    sums = []
    for n in range(len(cuts) - 1):
        act_grad, picked_grad, begun, *more = scan_back(
            cuts[n + 1], cuts[n], table, begins, act, picked, masks, pre,
            read_grad.reshape(grouped), prior, begun, rates, dt_cols, bias, skip, states, so_far,
            [],
        )
        so_far = (act_grad, picked_grad)
        sums.append(more)
    rate_grad, grad_dt, grad_bias, grad_skip = (sum(parts_of) for parts_of in zip(*sums))
    rate_grad = rate_grad.reshape(count, copies, groups, lanes).sum(axis=2)
    grad_decay = jnp.moveaxis(rate_grad, 0, 1).reshape(states, lanes).T * rate
    picked_grad = reduce_small(dims, picked_grad.reshape(sizes + (-1, 128))).astype(BF)
    picked_grad = gather_small(dims, picked_grad).reshape(groups, blocks, -1, 128)
    grad_gate_cols = exchange(after(gate_sent, picked_grad))
    x_grad, tap_grad, base_grad, grad_xproj = conv_back(
        table, begins, act_grad, picked_grad, pre_act, act, conv_in.reshape(grouped), masks, taps,
        xproj, [],
    )
    x_grad = x_grad.reshape(total, modes * lanes)
    grad_x_cols = exchange(jnp.concatenate(
        [
            to_owners(t_dot(normed, x_grad).astype(BF), in_rows),
            to_owners(grad_dt.astype(BF), rank_rows),
        ],
        axis=1,
    ))
    grad_dt = returned(grad_x_cols[:, in_rows * modes :], rank_rows).astype(F32)
    grad_x_cols = returned(grad_x_cols[:, : in_rows * modes], in_rows)
    grad_gate_cols = returned(grad_gate_cols, in_rows)
    normed_grad = scatter(
        jnp.concatenate([x_grad, gate_grad], axis=1),
        jnp.concatenate([x_cols, gate_cols], axis=1), 1, [],
    )
    grad_in = jnp.concatenate([grad_x_cols, grad_gate_cols], axis=2).astype(F32)
    grad_gain = jnp.sum(grad_in * in_weight.astype(F32), axis=(1, 2)) / norm_gain.astype(F32)
    xm = mine.astype(F32)
    scale = lax.rsqrt(jnp.mean(xm * xm, axis=1, keepdims=True) + EPS)
    unit = xm * scale
    scaled = normed_grad * gain
    grad_hidden = cotangent[0].astype(F32) + scale * (
        scaled - unit * jnp.mean(scaled * unit, axis=1, keepdims=True)
    )
    return (
        output,
        grad_hidden[None],
        grad_gain,
        grad_in,
        settle(tap_grad[:4].T),
        settle(base_grad[0]),
        settle(grad_xproj.reshape(lanes, modes, -1)),
        grad_dt,
        settle(grad_bias[:modes].T),
        settle(grad_decay),
        settle(grad_skip[0]),
        settle(grad_out_weight),
    )


def solution(mesh):
    both = ("grp", "seq")
    full = mesh.shape["grp"] * mesh.shape["seq"] <= 32
    chan, held = (both, ()) if full else (("seq",), ("grp",))
    row = P(both)
    return jax.shard_map(
        functools.partial(on_device, chan, held),
        mesh=mesh,
        in_specs=(
            P("grp", "seq", None), P("grp", "seq"), P("grp"),
            row, row, row, row, row, row, row, row, row, row,
            P("grp", "seq", None),
        ),
        out_specs=(P("grp", "seq", None), P("grp", "seq", None)) + (row,) * 10,
        check_vma=False,
    )
```

```python
import functools
import math

import jax
import jax.numpy as jnp
import numpy as np
from jax import lax
from jax.experimental import pallas as pl
from jax.experimental.pallas import tpu as pltpu
from jax.sharding import PartitionSpec as P

EPS = 1e-05
BF = jnp.bfloat16
F32 = jnp.float32
LOG2E = math.log2(math.e)
RESET = 1e4
VMEM = 60 * 1024 * 1024


def dot(a, b, dims=((1,), (0,))):
    return lax.dot_general(a, b, (dims, ((), ())), preferred_element_type=F32)


def silu_slope(v):
    s = jax.nn.sigmoid(v)
    return s * (1.0 + v * (1.0 - s))


def after(x, other):
    return x + (other[(0,) * other.ndim] * 0).astype(x.dtype)


def pick(values, masks):
    count = masks.shape[1]
    width = values.shape[1] // count
    return sum(values[:, m * width : (m + 1) * width] * masks[:, m : m + 1] for m in range(count))


def spread(values, masks):
    return jnp.concatenate(
        [values * masks[:, m : m + 1].astype(values.dtype) for m in range(masks.shape[1])], axis=1
    )


def spread_lanes(source, widen, target):

    low = source[...].astype(BF)
    for c in range(0, target.shape[1], 256):
        target[:, c : c + 256] = dot(low, widen[:, c : c + 256])


def widening(columns, lanes):
    ones = np.zeros((2 * columns, columns * lanes), np.float32)
    for s in range(columns):
        ones[s, s * lanes : (s + 1) * lanes] = 1
        ones[columns + s, s * lanes : (s + 1) * lanes] = 1
    return jnp.asarray(ones, BF)


def dot_t(a, b):
    return dot(a, b, ((1,), (1,)))


def t_dot(a, b):
    return dot(a, b, ((0,), (0,)))


def softplus(x):
    return jnp.maximum(x, 0.0) + jnp.log1p(jnp.exp(-jnp.abs(x)))


def packed(values, width):
    count = 128 // width
    span = values.shape[0] // count
    return jnp.concatenate([values[q * span : (q + 1) * span, :] for q in range(count)], axis=1)


def unpacked(values, width):
    values = values.astype(F32)
    return jnp.concatenate(
        [values[:, q * width : (q + 1) * width] for q in range(128 // width)], axis=0
    )


def to_time_major(ref, values, row, count):
    ref[pl.ds(row, count, stride=8), :] = values


def lay_out(groups, length, states, first, starts, step, act, picked, extra, sf, du, bc, also):
    copies = 8 // groups
    position = first + lax.broadcasted_iota(jnp.int32, (length, 1), 0)
    lane = lax.broadcasted_iota(jnp.int32, (1, 4 * states), 1)
    owner = lane % states // (states // copies)
    for g in range(groups):
        begin = (position == 0) | (position == starts[g])
        fade_step = jnp.where(begin, RESET, step[g])
        drive = step[g] * act[g, 0]
        span = length * 2 * states // 128
        chosen = jnp.concatenate(
            [
                unpacked(picked[g, 0, length + n * span : length + (n + 1) * span, :], 2 * states)
                for n in range(2)
            ],
            axis=1,
        )
        for j in range(copies):
            to_time_major(sf, fade_step, j * groups + g, length)
            to_time_major(du, drive, j * groups + g, length)
            to_time_major(bc, jnp.where(owner == j, chosen, 0.0), j * groups + g, length)
            if also is not None:
                to_time_major(also, extra[g, 0], j * groups + g, length)


def pre_step(picked, mask, dt, bias):
    modes, lanes = bias.shape
    product = dot(picked[: mask.shape[0], :], dt[...])
    return sum(
        (product[:, m * lanes : (m + 1) * lanes] + bias[m : m + 1, :]) * mask[:, m : m + 1]
        for m in range(modes)
    )


def scan_kernel(
    groups, length, states, table, starts, act, picked, mask, rate, widen, dt, bias, skip, y, pre, prior, end, sf, du, bc, ys, state, ex,
):
    copies, count, lanes = 8 // groups, rate.shape[0] // 8, rate.shape[1]
    i = pl.program_id(0)

    @pl.when(i == 0)
    def _():
        state[...] = jnp.zeros_like(state)

    steps = []
    for g in range(groups):
        raw = pre_step(picked[g, 0], mask[g, 0], dt, bias)
        pre[g, 0] = raw
        steps.append(softplus(raw))
    lay_out(groups, length, states, i * length, starts, steps, act, picked, None, sf, du, bc, None)
    spread_lanes(bc, widen, ex)
    rates = [rate[s * 8 : s * 8 + 8, :] for s in range(count)]

    def one(p, h):
        row = pl.ds(pl.multiple_of(p * 8, 8), 8)
        step_p, drive_p = sf[row, :], du[row, :]
        read = None
        out = []
        for s in range(count):
            prior[pl.ds(pl.multiple_of((p * count + s) * 8, 8), 8), :] = h[s]
            now = jnp.exp2(step_p * rates[s]) * h[s] + drive_p * ex[row, s * lanes : (s + 1) * lanes]
            term = now * ex[row, (count + s) * lanes : (count + s + 1) * lanes]
            read = term if read is None else read + term
            out.append(now)
        ys[row, :] = read
        return tuple(out)

    first = tuple(state[s * 8 : s * 8 + 8, :] for s in range(count))
    last = lax.fori_loop(0, length, one, first, unroll=8)
    for s in range(count):
        state[s * 8 : s * 8 + 8, :] = last[s]
    end[...] = state[...]
    for g in range(groups):
        total = sum(ys[pl.ds(j * groups + g, length, stride=8), :] for j in range(copies))
        total = total + skip[...] * act[g, 0]
        y[g, 0] = total


def back_kernel(
    groups, length, states, top, blocks, table, starts, act, picked, mask, pre, read_grad, prior,
    begun, rate, widen, dt, bias, skip, pick_b, pick_c, *refs,
):
    act_grad, picked_grad, left, rate_grad, dt_grad, bias_grad, skip_grad = refs[-20:-13]
    sf, du, gy, bc, wt, ft, pb, pc, res, carry, held, ex, step = refs[-13:]
    copies, count = 8 // groups, rate.shape[0] // 8
    lanes = rate.shape[1]
    modes = bias.shape[0]
    rank = dt.shape[0]
    i = pl.program_id(0)

    @pl.when(i == 0)
    def _():
        carry[...] = begun[0 : count * 8, :]
        held[...] = begun[count * 8 :, :]
        rate_grad[...] = jnp.zeros_like(rate_grad)
        dt_grad[...] = jnp.zeros_like(dt_grad)
        bias_grad[...] = jnp.zeros_like(bias_grad)
        skip_grad[...] = jnp.zeros_like(skip_grad)

    for g in range(groups):
        step[g] = softplus(pre[g, 0])
    lay_out(
        groups, length, states, (top - i) * length, starts, step, act, picked, read_grad, sf, du, bc, gy
    )
    spread_lanes(bc, widen, ex)
    rates = [rate[s * 8 : s * 8 + 8, :] for s in range(count)]

    def one(k, loop):
        p = length - 1 - k
        row = pl.ds(pl.multiple_of(p * 8, 8), 8)
        step_p, drive_p, grad_p = sf[row, :], du[row, :], gy[row, :]
        carried, state, total = loop
        weight_sum, fade_sum = None, None
        out_c, out_h, out_r = [], [], []
        for s in range(count):
            before = prior[pl.ds(pl.multiple_of((p * count + s) * 8, 8), 8), :]
            cols = slice(s * lanes, (s + 1) * lanes)
            e = grad_p * ex[row, (count + s) * lanes : (count + s + 1) * lanes] + carried[s]
            pc[row, cols] = grad_p * state[s]
            pb[row, cols] = e * drive_p
            term = e * ex[row, cols]
            passed = e * jnp.exp2(step_p * rates[s])
            decay = passed * before
            fade_term = decay * rates[s]
            weight_sum = term if weight_sum is None else weight_sum + term
            fade_sum = fade_term if fade_sum is None else fade_sum + fade_term
            out_c.append(passed)
            out_h.append(before)
            out_r.append(total[s] + decay * step_p)
        wt[row, :] = weight_sum
        ft[row, :] = fade_sum
        return tuple(out_c), tuple(out_h), tuple(out_r)

    def parts(ref):
        return tuple(ref[s * 8 : s * 8 + 8, :] for s in range(count))

    c, h, r = lax.fori_loop(
        0, length, one, (parts(carry), parts(held), parts(rate_grad)), unroll=4
    )
    for s in range(count):
        carry[s * 8 : s * 8 + 8, :] = c[s]
        held[s * 8 : s * 8 + 8, :] = h[s]
        rate_grad[s * 8 : s * 8 + 8, :] = r[s]
    left[0 : count * 8, :] = carry[...]
    left[count * 8 :, :] = held[...]
    res[...] = dot(pb[...].astype(BF), pick_b[...]) + dot(pc[...].astype(BF), pick_c[...])
    lane = lax.broadcasted_iota(jnp.int32, (1, 128), 1)
    owner = lane % states // count
    for g in range(groups):
        rows = [pl.ds(j * groups + g, length, stride=8) for j in range(copies)]
        weighted = sum(wt[row, :] for row in rows)
        faded = sum(ft[row, :] for row in rows) * (1.0 / LOG2E)
        chosen = sum(jnp.where(owner == j, res[rows[j], :], 0.0) for j in range(copies))
        grad_y, u = read_grad[g, 0], act[g, 0]
        act_grad[g, 0] = skip[...] * grad_y + step[g] * weighted
        pre_grad = (u * weighted + faded) * jax.nn.sigmoid(pre[g, 0])
        skip_grad[...] += jnp.sum(grad_y * u, axis=0, keepdims=True)
        rank_grad = None
        for m in range(modes):
            own = pre_grad * mask[g, 0, :, m : m + 1]
            bias_grad[m : m + 1, :] += jnp.sum(own, axis=0, keepdims=True)
            own = own.astype(BF)
            cols = slice(m * lanes, (m + 1) * lanes)
            term = dot_t(own, dt[:, cols])
            rank_grad = term if rank_grad is None else rank_grad + term
            dt_grad[:, cols] += t_dot(picked[g, 0, 0:length, :], own)
        picked_grad[g, 0, 0:length, :] = rank_grad
        picked_grad[g, 0, length:, :] = packed(chosen[:, 0 : 2 * states], 2 * states)


def spread_lanes(source, widen, target):

    @pl.loop(0, source.shape[0] // 128)
    def _(n):
        row = pl.ds(pl.multiple_of(n * 128, 128), 128)
        target[row, :] = dot(source[row, :].astype(BF), widen[...])


def widening(states, count, lanes):
    ones = np.zeros((2, 2, states, 2 * count * lanes), np.float32)
    for kind in range(2):
        for s in range(states):
            block = kind * count + s % count
            ones[:, kind, s, block * lanes : (block + 1) * lanes] = 1
    return jnp.asarray(ones.reshape(4 * states, -1), BF)


def picking(states, count, lanes):
    ones = np.zeros((2, count * lanes, 128), np.float32)
    for kind in range(2):
        for s in range(states):
            at = s % count
            ones[kind, at * lanes : (at + 1) * lanes, kind * states + s] = 1
    return jnp.asarray(ones[0], BF), jnp.asarray(ones[1], BF)


def conv_kernel(groups, length, table, starts, x, mask, taps, base, xproj, v, act, part, tail, ext):
    i = pl.program_id(0)

    @pl.when(i == 0)
    def _():
        tail[...] = jnp.zeros_like(tail)

    modes = mask.shape[3]
    width = xproj.shape[1] // modes
    position = i * length + lax.broadcasted_iota(jnp.int32, (length, 1), 0)
    for g in range(groups):
        begin = jnp.where(position >= starts[g], starts[g], 0)
        ext[0:8, :] = tail[g]
        ext[8 : 8 + length, :] = x[g, 0]
        tail[g] = x[g, 0, length - 8 : length, :]
        total = base[...]
        for k in range(4):
            valid = (position - 3 + k >= begin).astype(F32)
            total = total + taps[k : k + 1, :] * ext[5 + k : 5 + k + length, :] * valid
        v[g, 0] = total
        active = total * jax.nn.sigmoid(total)
        act[g, 0] = active
        product = dot(active.astype(BF), xproj[...])
        chosen = sum(
            product[:, m * width : (m + 1) * width] * mask[g, 0, :, m : m + 1] for m in range(modes)
        )
        part[g, 0, 0:length, :] = chosen[:, 0:128]
        part[g, 0, length:, :] = packed(chosen[:, 128:], width - 128)


def conv_back_kernel(
    groups, length, blocks, table, starts, grad, sel_grad, v, act, x, mask, taps, xproj, *refs,
):
    x_grad, tap_grad, base_grad, weight_grad, head, ext = refs[-6:]
    i = pl.program_id(0)

    @pl.when(i == 0)
    def _():
        head[...] = jnp.zeros_like(head)
        weight_grad[...] = jnp.zeros_like(weight_grad)
        tap_grad[...] = jnp.zeros_like(tap_grad)
        base_grad[...] = jnp.zeros_like(base_grad)

    modes = mask.shape[3]
    width = xproj.shape[1] // modes
    position = (blocks - 1 - i) * length + lax.broadcasted_iota(jnp.int32, (length, 1), 0)
    for g in range(groups):
        chosen = jnp.concatenate(
            [
                sel_grad[g, 0, 0:length, :].astype(F32),
                unpacked(sel_grad[g, 0, length:, :], width - 128),
            ],
            axis=1,
        ).astype(BF)
        masked = [chosen * mask[g, 0, :, m : m + 1].astype(BF) for m in range(modes)]
        act_grad = grad[g, 0]
        low = act[g, 0].astype(BF)
        for m in range(modes):
            cols = slice(m * width, (m + 1) * width)
            act_grad = act_grad + dot_t(masked[m], xproj[:, cols])
            weight_grad[:, cols] += t_dot(low, masked[m])
        v_grad = act_grad * silu_slope(v[g, 0])
        ext[0:length, :] = v_grad
        ext[length : length + 8, :] = head[g]
        head[g] = v_grad[0:8, :]
        base_grad[...] += jnp.sum(v_grad, axis=0, keepdims=True)
        total = None
        for k in range(4):
            crosses = (position < starts[g]) & (position + 3 - k >= starts[g])
            shifted = jnp.where(crosses, 0.0, ext[3 - k : 3 - k + length, :])
            term = taps[k : k + 1, :] * shifted
            total = term if total is None else total + term
            tap_grad[k : k + 1, :] += jnp.sum(x[g, 0] * shifted, axis=0, keepdims=True)
        total = total.astype(BF)
        lanes = total.shape[1]
        for m in range(modes):
            x_grad[g, 0, :, m * lanes : (m + 1) * lanes] = total * mask[g, 0, :, m : m + 1].astype(BF)


def inproj_kernel(lots, *refs):
    pieces = refs[:-9]
    gain, weight, normed, proj, mask, notes, cols, whole, arrived = refs[-9:]
    modes = mask.shape[2]
    lanes = weight.shape[2]
    count = len(pieces) // lots
    rows = mask.shape[1] // count
    part = cols.shape[0] // weight.shape[0]
    i = pl.program_id(0)

    def copies(lot):
        return [
            pltpu.make_async_copy(
                pieces[lot * count + n], whole.at[lot % 2, n], arrived.at[lot % 2, n]
            )
            for n in range(count)
        ]

    @pl.when(i == 0)
    def _():
        for copy in copies(0):
            copy.start()
        for n in range(weight.shape[0]):
            for m in range(modes):
                cols[n * part : (n + 1) * part, m * lanes : (m + 1) * lanes] = weight[
                    n, m * part : (m + 1) * part, :
                ]

    for lot in range(lots):

        @pl.when(i == lot)
        def _(lot=lot):
            if lot + 1 < lots:
                for copy in copies(lot + 1):
                    copy.start()
            for copy in copies(lot):
                copy.wait()

    slot = lax.rem(i, 2)
    square = (rows, rows)
    same = lax.broadcasted_iota(jnp.int32, square, 0) == lax.broadcasted_iota(jnp.int32, square, 1)
    kind = lax.broadcasted_iota(jnp.int32, (1, modes), 1).astype(F32)
    for n in range(count):
        span = slice(n * rows, (n + 1) * rows)
        x = whole[slot, n, 0:rows, :].astype(F32)
        scale = lax.rsqrt(jnp.mean(x * x, axis=1, keepdims=True) + EPS)
        normed[0, span, :] = (x * scale * gain[...]).astype(BF)
        note = whole[slot, n, rows : rows + 16, 0:rows].astype(F32)
        column = jnp.sum(jnp.where(same, note[0:1, :], 0.0), axis=1, keepdims=True)
        mask[0, span, :] = (column == kind).astype(F32)
        if n == 0:
            notes[0] = note[0:8, :]
    product = dot(normed[0], cols[...])
    proj[0] = sum(
        product[:, m * lanes : (m + 1) * lanes] * mask[0, :, m : m + 1] for m in range(modes)
    )


def inproj(lots, rows, modes, pieces, gain, weight):
    tall, width = pieces[0].shape
    lanes = weight.shape[2]
    count = len(pieces) // lots
    size = count * rows
    block = lambda *shape: pl.BlockSpec((1,) + shape, lambda i: (i, 0, 0))
    shapes = [
        jax.ShapeDtypeStruct((lots, size, width), BF),
        jax.ShapeDtypeStruct((lots, size, lanes), F32),
        jax.ShapeDtypeStruct((lots, size, modes), F32),
        jax.ShapeDtypeStruct((lots, 8, rows), F32),
        jax.ShapeDtypeStruct((width, modes * lanes), BF),
    ]
    return pl.pallas_call(
        functools.partial(inproj_kernel, lots),
        grid=(lots,),
        in_specs=[pl.BlockSpec(memory_space=pl.ANY)] * len(pieces) + [flat(gain), flat(weight)],
        out_specs=[block(*a.shape[1:]) for a in shapes[:4]] + [flat(shapes[4])],
        out_shape=shapes,
        scratch_shapes=[
            pltpu.VMEM((2, count, tall, width), BF),
            pltpu.SemaphoreType.DMA((2, count)),
        ],
        compiler_params=pltpu.CompilerParams(vmem_limit_bytes=VMEM),
        cost_estimate=pl.CostEstimate(
            flops=2 * lots * size * width * modes * lanes,
            bytes_accessed=6 * lots * size * width,
            transcendentals=0,
        ),
    )(*pieces, gain, weight)


def conv(table, starts, x, mask, taps, base, xproj):
    groups, blocks, length, lanes = x.shape
    modes = mask.shape[3]
    width = xproj.shape[1] // modes
    at = lambda i, t, b: (0, t[i], 0, 0)
    flat = lambda i, t, b: (0, 0)
    block = pl.BlockSpec((groups, 1, length, lanes), at)
    return pl.pallas_call(
        functools.partial(conv_kernel, groups, length),
        grid_spec=pltpu.PrefetchScalarGridSpec(
            num_scalar_prefetch=2,
            grid=(blocks,),
            in_specs=[
                block,
                pl.BlockSpec((groups, 1, length, modes), at),
                pl.BlockSpec(taps.shape, flat),
                pl.BlockSpec(base.shape, flat),
                pl.BlockSpec(xproj.shape, flat),
            ],
            out_specs=[block, block, pl.BlockSpec((groups, 1, length * width // 128, 128), at)],
            scratch_shapes=[
                pltpu.VMEM((groups, 8, lanes), F32),
                pltpu.VMEM((length + 8, lanes), F32),
            ],
        ),
        out_shape=[
            jax.ShapeDtypeStruct(x.shape, F32),
            jax.ShapeDtypeStruct(x.shape, F32),
            jax.ShapeDtypeStruct((groups, blocks, length * width // 128, 128), F32),
        ],
        compiler_params=pltpu.CompilerParams(vmem_limit_bytes=VMEM),
    )(table, starts, x, mask, taps, base, xproj)


def conv_back(table, starts, grad, sel_grad, v, act, x, mask, taps, xproj, before):
    groups, blocks, length, lanes = x.shape
    modes = mask.shape[3]
    width = xproj.shape[1] // modes
    at = lambda i, t, b: (0, t[blocks - 1 - i], 0, 0)
    flat = lambda i, t, b: (0, 0)
    block = pl.BlockSpec((groups, 1, length, lanes), at)
    return pl.pallas_call(
        functools.partial(conv_back_kernel, groups, length, blocks),
        grid_spec=pltpu.PrefetchScalarGridSpec(
            num_scalar_prefetch=2,
            grid=(blocks,),
            in_specs=[
                block,
                pl.BlockSpec((groups, 1, length * width // 128, 128), at),
                block,
                block,
                block,
                pl.BlockSpec((groups, 1, length, modes), at),
                pl.BlockSpec(taps.shape, flat),
                pl.BlockSpec(xproj.shape, flat),
            ]
            + [pl.BlockSpec(memory_space=pl.ANY)] * len(before),
            out_specs=[
                pl.BlockSpec((groups, 1, length, modes * lanes), at),
                pl.BlockSpec((8, lanes), flat),
                pl.BlockSpec((1, lanes), flat),
                pl.BlockSpec(xproj.shape, flat),
            ],
            scratch_shapes=[
                pltpu.VMEM((groups, 8, lanes), F32),
                pltpu.VMEM((length + 8, lanes), F32),
            ],
        ),
        out_shape=[
            jax.ShapeDtypeStruct((groups, blocks, length, modes * lanes), BF),
            jax.ShapeDtypeStruct((8, lanes), F32),
            jax.ShapeDtypeStruct((1, lanes), F32),
            jax.ShapeDtypeStruct(xproj.shape, F32),
        ],
        compiler_params=pltpu.CompilerParams(vmem_limit_bytes=VMEM),
    )(table, starts, grad, sel_grad, v, act, x, mask, taps, xproj, *before)


def flat(array):
    return pl.BlockSpec(array.shape, lambda i, *_: (0,) * array.ndim)


def scan(table, starts, act, picked, mask, rate, dt, bias, skip, states):
    groups, blocks, length, lanes = act.shape
    total = blocks * length
    count = rate.shape[0] // 8
    at = lambda i, t, b: (0, t[i], 0, 0)
    block = lambda a: pl.BlockSpec((groups, 1) + a.shape[2:], at)
    widen = widening(states, count, lanes)
    tall = pltpu.VMEM((length * 8, lanes), F32)
    like = jax.ShapeDtypeStruct(act.shape, F32)
    return pl.pallas_call(
        functools.partial(scan_kernel, groups, length, states),
        grid_spec=pltpu.PrefetchScalarGridSpec(
            num_scalar_prefetch=2,
            grid=(blocks,),
            in_specs=[block(a) for a in (act, picked, mask)]
            + [flat(a) for a in (rate, widen, dt, bias, skip)],
            out_specs=[
                block(act),
                block(act),
                pl.BlockSpec((length * count * 8, lanes), lambda i, t, b: (i, 0)),
                flat(rate),
            ],
            scratch_shapes=[
                tall,
                tall,
                pltpu.VMEM((length * 8, 4 * states), F32),
                tall,
                pltpu.VMEM((count * 8, lanes), F32),
                pltpu.VMEM((length * 8, 2 * count * lanes), F32),
            ],
        ),
        out_shape=[
            like,
            like,
            jax.ShapeDtypeStruct((total * count * 8, lanes), F32),
            jax.ShapeDtypeStruct((count * 8, lanes), F32),
        ],
        compiler_params=pltpu.CompilerParams(vmem_limit_bytes=VMEM),
        cost_estimate=pl.CostEstimate(flops=10**10, bytes_accessed=10**8, transcendentals=0),
    )(table, starts, act, picked, mask, rate, widen, dt, bias, skip)


def gate_kernel(lots_at, spans_at, normed, weight, mask, read, gate, gated, spread_gated):
    modes = mask.shape[2]
    lanes = read.shape[2]
    count = spans_at.shape[0]
    rows = read.shape[1] // count
    product = dot(normed[0], weight[...])
    masks = [mask[0, :, m : m + 1] for m in range(modes)]
    opened = sum(product[:, m * lanes : (m + 1) * lanes] * masks[m] for m in range(modes))
    gate[0] = opened
    low = (read[0] * (opened * jax.nn.sigmoid(opened))).astype(BF)
    gated[0] = low
    for m in range(modes):
        own = low * masks[m].astype(BF)
        for n in range(count):
            place = pl.ds(pl.multiple_of(spans_at[n] * rows, rows), rows)
            spread_gated[0, place, m * lanes : (m + 1) * lanes] = own[n * rows : (n + 1) * rows, :]


def gate_part(lots_at, spans_at, normed, weight, mask, read):
    lots, size, width = normed.shape
    lanes = read.shape[2]
    wide = weight.shape[1]
    block = lambda w: pl.BlockSpec((1, size, w), lambda i, a, b: (i, 0, 0))
    return pl.pallas_call(
        gate_kernel,
        grid_spec=pltpu.PrefetchScalarGridSpec(
            num_scalar_prefetch=2,
            grid=(lots,),
            in_specs=[block(width), flat(weight), block(mask.shape[2]), block(lanes)],
            out_specs=[
                block(lanes), block(lanes), pl.BlockSpec((1, size, wide), lambda i, a, b: (a[i], 0, 0))
            ],
        ),
        out_shape=[
            jax.ShapeDtypeStruct(read.shape, F32),
            jax.ShapeDtypeStruct(read.shape, BF),
            jax.ShapeDtypeStruct((lots, size, wide), BF),
        ],
        compiler_params=pltpu.CompilerParams(vmem_limit_bytes=VMEM),
        cost_estimate=pl.CostEstimate(
            flops=2 * lots * size * width * wide, bytes_accessed=3 * lots * size * width, transcendentals=0
        ),
    )(lots_at, spans_at, normed, weight, mask, read)


def scan_back(
    first, last, table, starts, act, picked, mask, pre, read_grad, prior, begun, rate, dt, bias,
    skip, states, so_far, before,
):
    groups, blocks, length, lanes = act.shape
    count = rate.shape[0] // 8
    rank = dt.shape[0]
    modes = bias.shape[0]
    at = lambda i, t, b: (0, t[last - 1 - i], 0, 0)
    block = lambda a: pl.BlockSpec((groups, 1) + a.shape[2:], at)
    widen = widening(states, count, lanes)
    pick_b, pick_c = picking(states, count, lanes)
    tall = pltpu.VMEM((length * 8, lanes), F32)
    wide = pltpu.VMEM((length * 8, count * lanes), F32)
    tables = pltpu.VMEM((count * 8, lanes), F32)
    shapes = [
        jax.ShapeDtypeStruct(act.shape, F32),
        jax.ShapeDtypeStruct((groups, blocks, length + length * 2 * states // 128, 128), F32),
        jax.ShapeDtypeStruct((2 * count * 8, lanes), F32),
        jax.ShapeDtypeStruct((count * 8, lanes), F32),
        jax.ShapeDtypeStruct((rank, modes * lanes), F32),
        jax.ShapeDtypeStruct((8, lanes), F32),
        jax.ShapeDtypeStruct((1, lanes), F32),
    ]
    loaded = (begun, rate, widen, dt, bias, skip, pick_b, pick_c)
    extra = tuple(so_far or ()) + tuple(before)
    at_input = 2 + 6 + len(loaded)
    return pl.pallas_call(
        functools.partial(back_kernel, groups, length, states, last - 1, blocks),
        grid_spec=pltpu.PrefetchScalarGridSpec(
            num_scalar_prefetch=2,
            grid=(last - first,),
            in_specs=[block(a) for a in (act, picked, mask, pre, read_grad)]
            + [pl.BlockSpec((length * count * 8, lanes), lambda i, t, b: (last - 1 - i, 0))]
            + [flat(a) for a in loaded]
            + [pl.BlockSpec(memory_space=pl.ANY)] * len(extra),
            out_specs=[block(shapes[0]), block(shapes[1])] + [flat(a) for a in shapes[2:]],
            scratch_shapes=[
                tall, tall, tall, pltpu.VMEM((length * 8, 4 * states), F32), tall, tall, wide, wide,
                pltpu.VMEM((length * 8, 128), F32),
                tables,
                tables,
                pltpu.VMEM((length * 8, 2 * count * lanes), F32),
                pltpu.VMEM((groups, length, lanes), F32),
            ],
        ),
        out_shape=shapes,
        input_output_aliases={at_input: 0, at_input + 1: 1} if so_far else {},
        compiler_params=pltpu.CompilerParams(vmem_limit_bytes=VMEM),
        cost_estimate=pl.CostEstimate(
            flops=10**10, bytes_accessed=25 * 10**6 * (last - first), transcendentals=0
        ),
    )(table, starts, act, picked, mask, pre, read_grad, prior, *loaded, *extra)


def cot_kernel(
    lots_at, spans_at, cots, out_rows, mask, gated, read, gate, read_grad, gate_grad, weight_grad, whole
):
    count = spans_at.shape[0]
    rows = whole.shape[0] // count

    @pl.when(pl.program_id(0) == 0)
    def _():
        weight_grad[...] = jnp.zeros_like(weight_grad)

    for n in range(count):
        whole[n * rows : (n + 1) * rows, :] = cots[
            0, pl.ds(pl.multiple_of(spans_at[n] * rows, rows), rows), :
        ]
    product = dot_t(whole[...], out_rows[...])
    modes = mask.shape[2]
    lanes = gated.shape[2]
    masks = [mask[0, :, m : m + 1] for m in range(modes)]
    grad = sum(product[:, m * lanes : (m + 1) * lanes] * masks[m] for m in range(modes))
    opened = gate[0]
    read_grad[0] = grad * (opened * jax.nn.sigmoid(opened))
    gate_low = (grad * read[0] * silu_slope(opened)).astype(BF)
    for m in range(modes):
        own = masks[m].astype(BF)
        cols = slice(m * lanes, (m + 1) * lanes)
        gate_grad[0, :, cols] = gate_low * own
        weight_grad[cols, :] += t_dot(gated[0] * own, whole[...])


def cot_part(lots_at, spans_at, cots, out_rows, mask, gated, read, gate):
    lots, size, width = cots.shape
    lanes = gated.shape[2]
    wide = out_rows.shape[0]
    block = lambda w: pl.BlockSpec((1, size, w), lambda i, a, b: (i, 0, 0))
    return pl.pallas_call(
        cot_kernel,
        grid_spec=pltpu.PrefetchScalarGridSpec(
            num_scalar_prefetch=2,
            grid=(lots,),
            in_specs=[pl.BlockSpec((1, size, width), lambda i, a, b: (a[i], 0, 0)), flat(out_rows)]
            + [block(a.shape[2]) for a in (mask, gated, read, gate)],
            out_specs=[block(lanes), block(wide), flat(out_rows)],
            scratch_shapes=[pltpu.VMEM((size, width), BF)],
        ),
        out_shape=[
            jax.ShapeDtypeStruct((lots, size, lanes), F32),
            jax.ShapeDtypeStruct((lots, size, wide), BF),
            jax.ShapeDtypeStruct(out_rows.shape, F32),
        ],
        compiler_params=pltpu.CompilerParams(vmem_limit_bytes=VMEM),
        cost_estimate=pl.CostEstimate(
            flops=4 * lots * size * width * wide, bytes_accessed=3 * lots * size * width, transcendentals=0
        ),
    )(lots_at, spans_at, cots, out_rows, mask, gated, read, gate)


class Dim:

    def __init__(self, axis, stride, size, length):
        self.axis, self.stride, self.size, self.length = axis, stride, size, length

    def here(self):
        return lax.axis_index(self.axis) // self.stride % self.size

    def fetch(self, x, by):
        pairs = []
        for i in range(self.length):
            c = i // self.stride % self.size
            pairs.append((i + ((c + by) % self.size - c) * self.stride, i))
        return lax.ppermute(x, self.axis, pairs)


def dims_of(chan):
    dims = []
    for axis in chan:
        length = lax.axis_size(axis)
        sizes = []
        rest = length
        if axis == "seq":
            rest //= 2
        radix = 4 if axis == "seq" else 2
        while rest > 1:
            sizes.insert(0, min(radix, rest))
            rest //= sizes[0]
        if axis == "seq":
            sizes.append(2)
        stride = length
        for size in sizes:
            stride //= size
            dims.append(Dim(axis, stride, size, length))
    return dims


def fence(*arrays):
    return list(pl.pallas_call(
        lambda *refs: None,
        in_specs=[pl.BlockSpec(memory_space=pl.ANY)] * len(arrays),
        out_specs=[pl.BlockSpec(memory_space=pl.ANY)] * len(arrays),
        out_shape=[jax.ShapeDtypeStruct(x.shape, x.dtype) for x in arrays],
        input_output_aliases={n: n for n in range(len(arrays))},
    )(*arrays))


def gather_pieces(dims, x):
    others, ring, core = dims[:-2], dims[-2], dims[-1]
    got = {}
    first = x
    for k in range(ring.size):
        if k:
            first = ring.fetch(first, 1)
        order = list(range(len(others)))
        if k % 2:
            order.reverse()
        held = {(0,) * len(others): first}
        for d in order:
            for at, block in list(held.items()):
                for r in range(1, others[d].size):
                    block = others[d].fetch(block, 1)
                    held[at[:d] + (r,) + at[d + 1 :]] = block
        for at, block in held.items():
            got[at + (k, 0)] = block
            got[at + (k, 1)] = core.fetch(block, 1)
    return [got[at] for at in sorted(got)]


def pairs_of(dims):
    return [d.size for d in dims[:-2]] == [2, 2]


def gather_stage(dims, x, d):
    got = [x] + [dims[d].fetch(x, r) for r in range(1, dims[d].size)]
    return jnp.concatenate(got, axis=d)


def gather_small(dims, x):
    x = x.reshape((1,) * len(dims) + x.shape)
    x = gather_stage(dims, x, len(dims) - 2)
    if pairs_of(dims):
        halves = jnp.split(x, 2, axis=len(dims))
        halves = [gather_stage(dims, h, n) for n, h in enumerate(halves)]
        halves = [gather_stage(dims, h, 1 - n) for n, h in enumerate(halves)]
        x = jnp.concatenate(halves, axis=len(dims))
    else:
        for d in range(len(dims) - 2):
            x = gather_stage(dims, x, d)
    return gather_stage(dims, x, len(dims) - 1)


def reduce_stage(dims, x, d, kind):
    block = [lax.slice_in_dim(x, r, r + 1, axis=d) for r in range(dims[d].size)]
    return add_up(
        [block[0]] + [dims[d].fetch(block[r].astype(kind), -r) for r in range(1, len(block))]
    )


def reduce_small(dims, x):
    x = reduce_stage(dims, x, len(dims) - 1, F32)
    if pairs_of(dims):
        halves = jnp.split(x, 2, axis=len(dims))
        halves = [reduce_stage(dims, h, n, BF) for n, h in enumerate(halves)]
        halves = [reduce_stage(dims, h, 1 - n, F32) for n, h in enumerate(halves)]
        x = jnp.concatenate(halves, axis=len(dims))
    else:
        for d in range(len(dims) - 2):
            x = reduce_stage(dims, x, d, F32 if d else BF)
    x = reduce_stage(dims, x, len(dims) - 2, F32)
    return x.reshape(x.shape[len(dims) :])


def add_up(parts):
    return sum(p.astype(F32) for p in parts)


def reduce_parts(dims, x, turn, stages):
    order = list(range(len(dims) - 2))
    if turn % 2:
        order.reverse()
    order = [len(dims) - 1] + order + [len(dims) - 2]
    for n, d in enumerate(order):
        size = dims[d].size
        block = [lax.slice_in_dim(x, r, r + 1, axis=d) for r in range(size)]
        if size == 2:
            x = add_up([block[0]] + [dims[d].fetch(block[r], -r) for r in range(1, size)])
        else:
            moving = block[size - 1]
            for r in range(size - 2, -1, -1):
                x = add_up([block[r], dims[d].fetch(moving, -1)])
                moving = x.astype(BF)
        if n < len(order) - 1:
            x = x.astype(BF)
            stages.append((n, x))
    return x.reshape(x.shape[len(dims) :])


def on_device(
    chan, held,
    hidden, modality, starts, norm_gain, in_weight, conv_weight, conv_bias, xproj_weight,
    dtproj_weight, step_bias, decay_log, skip_weight, out_weight, cotangent,
):
    def collect(x):
        return lax.all_gather(x, held, axis=0, tiled=True) if held else x

    def exchange(x):
        return lax.all_to_all(x, chan, 0, 0, tiled=True)

    def settle(x):
        return lax.psum_scatter(x, held, scatter_dimension=0, tiled=True) if held else x

    dims = dims_of(chan)
    sizes = tuple(d.size for d in dims)
    parts = math.prod(sizes)
    lots = math.prod(lax.axis_size(a) for a in held) if held else 1
    groups = parts // lax.axis_size("seq")
    rows, width = hidden.shape[1:]
    own = conv_weight.shape[0]
    lanes = own * lots
    rank_rows = dtproj_weight.shape[0]
    rank = rank_rows * parts * lots
    modes = in_weight.shape[1]
    states = decay_log.shape[1]
    mine = hidden[0]
    cot = cotangent[0]

    def shards(w):
        w = w.reshape(w.shape[0], modes, lots, parts, own)
        return jnp.moveaxis(w, 3, 0).reshape(parts, w.shape[0], modes, lanes)

    def to_owners(g, out_rows):
        return settle(g).reshape(parts, out_rows * modes, lanes)

    def returned(g, out_rows):
        g = g.reshape(parts, out_rows, modes, lots, own)
        return jnp.moveaxis(g, 0, 3).reshape(out_rows, modes, lots * parts * own)

    inner = lanes * parts
    blocks = parts // groups
    note = jnp.pad(jnp.stack([starts[0] >> 6, starts[0] & 63])[None], ((0, 0), (0, rows - 2)))
    note = jnp.concatenate([modality, note], axis=0).astype(BF)
    note = jnp.pad(note, ((0, 14), (0, width - rows)))
    pieces = gather_pieces(dims, jnp.concatenate([mine, note], axis=0))
    room = -norm_gain.shape[0] % lanes
    notes = jnp.broadcast_to(jnp.pad(norm_gain, (0, room)), (parts, norm_gain.shape[0] + room))
    moved = collect(exchange(jnp.concatenate(
        [
            jnp.swapaxes(shards(in_weight[:, :, :inner]), 1, 2).reshape(parts, -1, lanes),
            shards(dtproj_weight).reshape(parts, -1, lanes),
            notes.reshape(parts, -1, lanes),
        ],
        axis=1,
    )))
    cut = in_weight.shape[0] * modes
    further = cut + rank_rows * modes
    dt_cols = moved[:, cut:further].reshape(rank, modes * lanes)
    gain = moved[:, further:].reshape(parts * lots, -1)[:, : norm_gain.shape[0]]
    gain = gain.reshape(1, width).astype(F32)
    conv_weight, conv_bias, xproj_weight, step_bias, decay_log, skip_weight, out_weight = (
        collect(w)
        for w in (conv_weight, conv_bias, xproj_weight, step_bias, decay_log, skip_weight, out_weight)
    )
    taps = conv_weight.astype(F32).T
    bias = step_bias.astype(F32).T
    skip = skip_weight.astype(F32)[None]
    xproj = xproj_weight.reshape(lanes, -1)
    out_rows = jnp.moveaxis(out_weight, 1, 0).reshape(modes * lanes, width)
    total = parts * rows
    copies = 8 // groups
    count = states // copies
    rate = -jnp.exp(decay_log.astype(F32))
    rates = jnp.moveaxis(rate.T.reshape(copies, count, lanes), 0, 1)
    rates = jnp.repeat(rates.reshape(count * copies, 1, lanes), groups, axis=1).reshape(-1, lanes)
    rates = rates * LOG2E
    order = jnp.zeros((), jnp.int32)
    spans = jnp.arange(blocks, dtype=jnp.int32)
    stride = blocks
    for d in dims:
        if d.axis == "seq":
            stride //= d.size
            order = order * d.size + (spans // stride % d.size - d.here()) % d.size
    table = order

    def placed(some):
        at = jnp.zeros((), jnp.int32)
        stride = math.prod(d.size for d in some)
        names = jnp.arange(stride, dtype=jnp.int32)
        for d in some:
            stride //= d.size
            at = at * d.size + (names // stride % d.size + d.here()) % d.size
        return at.reshape(-1)


    step_pieces = sizes[-1] * sizes[-2]
    lots_in = parts // step_pieces
    normed, conv_in, in_masks, notes, x_cols = inproj(lots_in, rows, modes, pieces, gain, moved)
    masks = in_masks.reshape(groups, blocks, rows, modes)
    notes = notes.reshape(groups, -1, 8, rows)[:, 0, 1].astype(jnp.int32)
    begins = notes[:, 0] * 64 + notes[:, 1]
    cots = lax.all_gather(after(cot, conv_in), chan, axis=0, tiled=True)
    normed = normed.reshape(total, width)
    grouped = (groups, blocks, rows, lanes)
    pre_act, act, partial = conv(
        table, begins, conv_in.reshape(grouped), masks, taps, conv_bias.astype(F32)[None], xproj
    )
    picked = reduce_small(dims, partial.reshape(sizes + (-1, 128)))
    low = picked.astype(BF)
    rest = (picked[rows:] - low[rows:].astype(F32)).astype(BF)
    picked = gather_small(dims, jnp.concatenate([low, rest], axis=0))
    picked = picked.reshape(groups, blocks, -1, 128)
    gate_cols = collect(exchange(shards(after(in_weight[:, :, inner:], picked))).reshape(
        -1, modes, lanes
    )).reshape(width, modes * lanes)
    read, pre, prior, end = scan(
        table, begins, act, picked, masks, rates, dt_cols, bias, skip, states
    )
    lot = (lots_in, step_pieces * rows, -1)
    lots_at, spans_at = placed(dims[:-2]), placed(dims[-2:])
    gate_in, gated, spread_gated = gate_part(
        lots_at, spans_at, normed.reshape(lot), gate_cols, in_masks, read.reshape(lot)
    )

    def scatter(x, weight, dim, stages):
        got = []
        chunk = width // 2
        for n in range(2):
            w = lax.slice_in_dim(weight, n * chunk, (n + 1) * chunk, axis=1 - dim)
            product = dot(x, w, ((1,), (dim,))).astype(BF).reshape(sizes + (rows, chunk))
            got.append(reduce_parts(dims, product, n, stages))
        return jnp.concatenate(got, axis=1)

    branch = dot(spread_gated.reshape(total, modes * lanes), out_rows).astype(BF)
    branch = lax.psum_scatter(branch, chan, scatter_dimension=0, tiled=True)
    output = (mine.astype(F32) + branch.astype(F32)).astype(BF)[None]

    read_grad, gate_grad, grad_out_weight = cot_part(
        lots_at, spans_at, cots.reshape(lots_in, -1, width), out_rows, in_masks, gated,
        read.reshape(lot), gate_in,
    )
    grad_out_weight = jnp.moveaxis(grad_out_weight.reshape(modes, lanes, width), 0, 1)
    gate_grad = gate_grad.reshape(total, modes * lanes)
    in_rows = in_weight.shape[0]
    gate_sent = to_owners(t_dot(normed, gate_grad).astype(BF), in_rows)
    begun = jnp.concatenate([jnp.zeros_like(end), end], axis=0)
    cuts = [blocks, 0]
    so_far = None
    sums = []
    for n in range(len(cuts) - 1):
        act_grad, picked_grad, begun, *more = scan_back(
            cuts[n + 1], cuts[n], table, begins, act, picked, masks, pre,
            read_grad.reshape(grouped), prior, begun, rates, dt_cols, bias, skip, states, so_far,
            [],
        )
        so_far = (act_grad, picked_grad)
        sums.append(more)
    rate_grad, grad_dt, grad_bias, grad_skip = (sum(parts_of) for parts_of in zip(*sums))
    rate_grad = rate_grad.reshape(count, copies, groups, lanes).sum(axis=2)
    grad_decay = jnp.moveaxis(rate_grad, 0, 1).reshape(states, lanes).T * rate
    picked_grad = reduce_small(dims, picked_grad.reshape(sizes + (-1, 128))).astype(BF)
    picked_grad = gather_small(dims, picked_grad).reshape(groups, blocks, -1, 128)
    gate_sent, picked_grad = fence(gate_sent, picked_grad)
    grad_gate_cols = exchange(gate_sent)
    x_grad, tap_grad, base_grad, grad_xproj = conv_back(
        table, begins, act_grad, picked_grad, pre_act, act, conv_in.reshape(grouped), masks, taps,
        xproj, [],
    )
    x_grad = x_grad.reshape(total, modes * lanes)
    grad_x_cols = exchange(jnp.concatenate(
        [
            to_owners(t_dot(normed, x_grad).astype(BF), in_rows),
            to_owners(grad_dt.astype(BF), rank_rows),
        ],
        axis=1,
    ))
    grad_dt = returned(grad_x_cols[:, in_rows * modes :], rank_rows).astype(F32)
    grad_x_cols = returned(grad_x_cols[:, : in_rows * modes], in_rows)
    grad_gate_cols = returned(grad_gate_cols, in_rows)
    normed_grad = scatter(
        jnp.concatenate([x_grad, gate_grad], axis=1),
        jnp.concatenate([x_cols, gate_cols], axis=1), 1, [],
    )
    grad_in = jnp.concatenate([grad_x_cols, grad_gate_cols], axis=2).astype(F32)
    grad_gain = jnp.sum(grad_in * in_weight.astype(F32), axis=(1, 2)) / norm_gain.astype(F32)
    xm = mine.astype(F32)
    scale = lax.rsqrt(jnp.mean(xm * xm, axis=1, keepdims=True) + EPS)
    unit = xm * scale
    scaled = normed_grad * gain
    grad_hidden = cotangent[0].astype(F32) + scale * (
        scaled - unit * jnp.mean(scaled * unit, axis=1, keepdims=True)
    )
    return (
        output,
        grad_hidden[None],
        grad_gain,
        grad_in,
        settle(tap_grad[:4].T),
        settle(base_grad[0]),
        settle(grad_xproj.reshape(lanes, modes, -1)),
        grad_dt,
        settle(grad_bias[:modes].T),
        settle(grad_decay),
        settle(grad_skip[0]),
        settle(grad_out_weight),
    )


def solution(mesh):
    both = ("grp", "seq")
    full = mesh.shape["grp"] * mesh.shape["seq"] <= 32
    chan, held = (both, ()) if full else (("seq",), ("grp",))
    row = P(both)
    return jax.shard_map(
        functools.partial(on_device, chan, held),
        mesh=mesh,
        in_specs=(
            P("grp", "seq", None), P("grp", "seq"), P("grp"),
            row, row, row, row, row, row, row, row, row, row,
            P("grp", "seq", None),
        ),
        out_specs=(P("grp", "seq", None), P("grp", "seq", None)) + (row,) * 10,
        check_vma=False,
    )
```
